256 devices in a mesh: mod: 2 (over core), tp: 32 (over y, z), seq: 4 (over x).
Axes of the slice: x: 4, y: 4, z: 8, core: 2. Of those that a mesh axis runs over, the one named last changes fastest.
Arguments:
- tokens: bfloat16 [2048, 8192], P('seq', ('mod', 'tp')), may hold values from -6 to 6
- modality: int32 [2048], P('seq'), may hold values from 0 to 1, as said below
- norm_gain: float32 [2, 8192], P('mod'), may hold values from 0.25 to 1.75
- w_qkv: bfloat16 [2, 8192, 3, 4096], P('mod', None, None, 'tp'), may hold values from -0.0625 to 0.0625
- qk_gain: float32 [2, 4096], P(None, 'tp'), may hold values from 0.48 to 9.6
- w_out: bfloat16 [2, 4096, 8192], P('mod', 'tp'), may hold values from -1.5 to 1.5
Outputs:
- attended: bfloat16 [2048, 8192], P('seq', ('mod', 'tp'))
The draws below stay inside these ranges and needn't reach their ends.
Inputs may be any that keep to these rules, and one draw needn't show every extreme that they name: `modality`: 1 marks image tokens and 0 text tokens; exactly 1024 tokens are image tokens, those at the 1024 positions from some start on, continuing from position 0 where they pass the end of the sequence.
All inputs are finite; a program needn't handle non-finite values.
Results may differ from the reference program's by a relative error of at most 0.01.
The reference program's roundings to bfloat16 on the way (of `normed`, `values`, `weights` and `heads_out`) count: a program that leaves them out, or rounds other values in their place, can miss the bound.
Values may be sent and summed in bfloat16 or wider, within the bound.
No kernel may reach another device: no remote copies, remote signals or barrier semaphores. Data moves between devices by JAX's collectives and lax.ppermute only.
A program may use at most 128 MiB of HBM per device.

```python
import math
import jax
import jax.numpy as jnp
from jax import lax

D = 8192
HEADS = 32
HD = 128
TOKENS = 2048
SPAN = 1024


def draw_modality(key, part):
    key = jax.random.fold_in(key, 11)
    begin_at = jax.random.randint(key, (), 0, TOKENS)
    places = jnp.arange(TOKENS, dtype=jnp.int32)
    offset = (places - begin_at + TOKENS) % TOKENS
    return (offset < SPAN).astype(jnp.int32)


def draw_qk_gain(key, part):
    key = jax.random.fold_in(key, 7)
    head_key, fine_key = jax.random.split(key)
    lowest, highest = (0.6, 1.6)
    head_scale = jnp.exp(jax.random.uniform(head_key, (2, HEADS, 1), jnp.float32, jnp.log(lowest), jnp.log(highest)))
    fine_gain = jax.random.uniform(fine_key, (2, HEADS, HD), jnp.float32, 0.8, 1.2)
    return (head_scale * fine_gain).reshape(2, HEADS * HD).astype(jnp.float32)


def raised(array, own_key, source, target, blocks, factor):
    owner, partner = [(jnp.arange(array.shape[position]) // (array.shape[position] // blocks)).reshape([-1 if axis == position else 1 for axis in range(array.ndim)]) for position in (source, target)]
    chosen = jax.random.permutation(own_key, blocks)[partner]
    strong = (owner == chosen) | (owner == (partner + blocks // 2) % blocks)
    return jnp.where(strong, factor * array, array)


def shard_levels(own_key, extent, shards, least, top_value):
    def one(axis_at, blocks):
        heights = jax.random.uniform(jax.random.fold_in(jax.random.fold_in(own_key, 6), axis_at), (blocks,), jnp.float32, least / len(shards), top_value / len(shards))
        return jnp.repeat(jnp.exp(heights), extent[axis_at] // blocks).reshape((-1,) + (1,) * (len(extent) - axis_at - 1))

    loudness = one(*shards[0])
    for cut in shards[1:]:
        loudness = loudness * one(*cut)
    return loudness


def bell_draw(key, dims, spread, most, pieces=(), kind=jnp.bfloat16):
    drawn = spread * jax.random.normal(key, dims, jnp.float32)
    if pieces:
        drawn = drawn * shard_levels(key, dims, pieces, -0.22, 0.18)
    return jnp.clip(drawn, -most, most).astype(kind)


def gaussian_with(key, extent, width, reach, cuts, heavy, kind=jnp.bfloat16):
    values = width * jax.random.normal(key, extent, jnp.float32)
    if cuts:
        values = values * shard_levels(key, extent, cuts, -0.22, 0.18)
    return jnp.clip(raised(values, jax.random.fold_in(key, 3), *heavy), -reach, reach).astype(kind)


def setup_inputs(seed: int = 0) -> dict:
    splits = jax.random.split(jax.random.key(seed), 7)
    return {
        "tokens": bell_draw(splits[0], (TOKENS, D), 1.0, 6.0, ((0, 4), (1, 64))),
        "modality": draw_modality(jax.random.fold_in(splits[6], 71), 0),
        "norm_gain": jnp.clip(1.0 + 0.15 * jax.random.normal(splits[2], (2, D), jnp.float32), 0.25, 1.75),
        "w_qkv": bell_draw(splits[3], (2, D, 3, HEADS * HD), D ** -0.5, 0.0625, ((0, 2), (3, 32))),
        "qk_gain": draw_qk_gain(jax.random.fold_in(splits[6], 71), 0),
        "w_out": gaussian_with(splits[5], (2, HEADS * HD, D), (HD // 2) ** -0.5, 1.5, ((0, 2), (1, 32)), (1, 2, 32, 2.75)),
    }


epsilon = 1e-05
masked_score = -1e+30

def headnorm(projected, gain_row):
    row_count = projected.shape[0]
    by_head = projected.reshape(row_count, -1, HD)
    average = lax.optimization_barrier(jnp.mean(by_head, axis=2, keepdims=True))
    centred = by_head - average
    variance = lax.optimization_barrier(jnp.mean(centred * centred, axis=2, keepdims=True))
    return centred * lax.rsqrt(variance + epsilon) * gain_row.reshape(1, -1, HD)

def rotate(by_head, places):
    half_dim = HD // 2
    inverse = 1.0 / 10000.0 ** (jnp.arange(half_dim, dtype=jnp.float32) * (2.0 / HD))
    angles = places.astype(jnp.float32)[:, None] * inverse[None, :]
    cosines = jnp.cos(angles)[:, None, :]
    sines = jnp.sin(angles)[:, None, :]
    lower_half = by_head[:, :, :half_dim]
    upper_half = by_head[:, :, half_dim:]
    return jnp.concatenate([lower_half * cosines - upper_half * sines, upper_half * cosines + lower_half * sines], axis=2)

def project(tokens, gain_row, w_section, qk_gain, places):
    row_count = tokens.shape[0]
    as_float = tokens.astype(jnp.float32)
    inv_rms = lax.rsqrt(lax.optimization_barrier(jnp.mean(as_float * as_float, axis=1, keepdims=True)) + epsilon)
    normed = (as_float * inv_rms * gain_row[None, :]).astype(jnp.bfloat16)
    col_width = w_section.shape[2]
    projected = jnp.dot(normed, w_section.reshape(w_section.shape[0], 3 * col_width), preferred_element_type=jnp.float32)
    projected = projected.reshape(row_count, 3, col_width)
    queries = rotate(headnorm(projected[:, 0], qk_gain[0]), places).astype(jnp.bfloat16)
    key_rows = rotate(headnorm(projected[:, 1], qk_gain[1]), places).astype(jnp.bfloat16)
    value_rows = projected[:, 2].reshape(row_count, -1, HD).astype(jnp.bfloat16)
    return (queries, key_rows, value_rows)

def reference(tokens, modality, norm_gain, w_qkv, qk_gain, w_out):
    places = jnp.arange(TOKENS, dtype=jnp.int32)
    text_side = project(tokens, norm_gain[0], w_qkv[0], qk_gain, places)
    image_side = project(tokens, norm_gain[1], w_qkv[1], qk_gain, places)
    is_image = (modality == 1)[:, None, None]
    queries = jnp.where(is_image, image_side[0], text_side[0])
    key_rows = jnp.where(is_image, image_side[1], text_side[1])
    value_rows = jnp.where(is_image, image_side[2], text_side[2])
    inv_root = 1.0 / math.sqrt(HD)

    def one_head(operands):
        head_query, head_keys, head_values = operands
        scores = jnp.dot(head_query, head_keys.T, preferred_element_type=jnp.float32) * inv_root
        allowed = places[None, :] <= places[:, None]
        scores = jnp.where(allowed, scores, masked_score)
        largest = lax.optimization_barrier(jnp.max(scores, axis=1, keepdims=True))
        weights = jnp.where(allowed, jnp.exp(scores - largest), 0.0)
        denominator = lax.optimization_barrier(jnp.sum(weights, axis=1, keepdims=True))
        summed = jnp.dot(weights.astype(jnp.bfloat16), head_values, preferred_element_type=jnp.float32)
        return (summed / denominator).astype(jnp.bfloat16)
    per_head = lax.map(one_head, (jnp.transpose(queries, (1, 0, 2)), jnp.transpose(key_rows, (1, 0, 2)), jnp.transpose(value_rows, (1, 0, 2))))
    heads_out = jnp.transpose(per_head, (1, 0, 2)).reshape(TOKENS, HEADS * HD)
    text_out = jnp.dot(heads_out, w_out[0], preferred_element_type=jnp.float32)
    image_out = jnp.dot(heads_out, w_out[1], preferred_element_type=jnp.float32)
    return jnp.where((modality == 1)[:, None], image_out, text_out).astype(jnp.bfloat16)
```

```python
import math

import jax
import jax.numpy as jnp
from jax import lax
from jax.experimental import pallas as pl
from jax.experimental.pallas import tpu as pltpu
from jax.sharding import Mesh
from jax.sharding import PartitionSpec as P

HD = 128
EPS = 1e-05
MASKED = -1e30
NY = 4
NZ = 8
NX = 4
AXES = ("mod", "y", "z", "seq")
ROWS_A = 256


def pairs(dc, dy, dz, dx, wrap_x=True):
    out = []
    for c in range(2):
        for y in range(NY):
            for z in range(NZ):
                for x in range(NX):
                    if not wrap_x and not 0 <= x - dx < NX:
                        continue
                    source = ((c * NY + y) * NZ + z) * NX + x
                    to = (((c - dc) % 2 * NY + (y - dy) % NY) * NZ + (z - dz) % NZ) * NX + (x - dx) % NX
                    out.append((source, to))
    return out


def take(x, dc=0, dy=0, dz=0, dx=0, wrap_x=True):
    return lax.ppermute(x, AXES, pairs(dc, dy, dz, dx, wrap_x))


def gather_a(rows):
    s1, s3, s2 = take(rows, dy=1), take(rows, dy=-1), take(rows, dy=2)
    own = jnp.stack([rows, s1, s2, s3])
    f1, b1 = take(own, dz=1), take(own, dz=-1)
    f2, b2 = take(f1, dz=1), take(b1, dz=-1)
    f3, b3 = take(f2, dz=1), take(b2, dz=-1)
    f4, b4 = take(f3[:2], dz=1), take(b3[2:], dz=-1)
    return [own, f1, f2, f3, jnp.concatenate([f4, b4]), b3, b2, b1]


def gather_b(rows):
    got = [rows] + [take(rows, dz=d if d < 5 else d - 8) for d in range(1, NZ)]
    own = jnp.stack(got)
    f1, b1 = take(own, dy=1), take(own, dy=-1)
    f2, b2 = take(f1[:4], dy=1), take(b1[4:], dy=-1)
    return [own, f1, jnp.concatenate([f2, b2]), b1]


def qkv_kernel(z_first, at_ref, inv_ref, own_row_ref, gain_ref, gain_other_ref, w_ref, w_other_ref, *rest):
    pieces, out_ref, acc = rest[:-2], rest[-2], rest[-1]
    step = pl.program_id(0)
    inverse = inv_ref[...]
    own_row = own_row_ref[...] > 0
    normed, own_w, other_w = [], [], []
    for k, piece in enumerate(pieces):
        if z_first:
            yi, zi = lax.rem(at_ref[1] + k, NY), lax.rem(at_ref[2] + step, NZ)
            where = (0, yi, 0)
        else:
            yi, zi = lax.rem(at_ref[1] + step, NY), lax.rem(at_ref[2] + k, NZ)
            where = (0, 0, zi)
        gain = jnp.where(own_row, gain_ref[yi, pl.ds(zi, 1), :], gain_other_ref[yi, pl.ds(zi, 1), :])
        normed.append((piece[0].astype(jnp.float32) * inverse * gain).astype(jnp.bfloat16))
        own_w.append(jnp.concatenate([w_ref[(p, *where)] for p in range(3)], axis=1))
        other_w.append(jnp.concatenate([w_other_ref[(p, *where)] for p in range(3)], axis=1))
    left = jnp.concatenate(normed, axis=1)
    right = jnp.concatenate(
        [jnp.concatenate(own_w, axis=0), jnp.concatenate(other_w, axis=0)], axis=1
    )
    part = jnp.dot(left, right, preferred_element_type=jnp.float32)

    @pl.when(step == 0)
    def _():
        acc[...] = part

    @pl.when(step > 0)
    def _():
        acc[...] += part

    @pl.when(step == pl.num_programs(0) - 1)
    def _():
        out_ref[...] = jnp.where(own_row, acc[:, : 3 * HD], acc[:, 3 * HD :])


def qkv_part(at, inverse, own_row, gain, gain_other, w, w_other, pieces, z_first):
    rows = pieces[0].shape[1]
    steps = pieces[0].shape[0]
    if z_first:
        block = (3, 1, NY, 1, HD, HD)
        index = lambda g, at: (0, at[0], 0, lax.rem(at[2] + g, NZ), 0, 0)
        index_other = lambda g, at: (0, 0, 0, lax.rem(at[2] + g, NZ), 0, 0)
    else:
        block = (3, 1, 1, NZ, HD, HD)
        index = lambda g, at: (0, at[0], lax.rem(at[1] + g, NY), 0, 0, 0)
        index_other = lambda g, at: (0, 0, lax.rem(at[1] + g, NY), 0, 0, 0)

    def body(*refs):
        qkv_kernel(z_first, *refs)

    whole = lambda shape: pl.BlockSpec(shape, lambda g, at: (0,) * len(shape))
    return pl.pallas_call(
        body,
        grid_spec=pltpu.PrefetchScalarGridSpec(
            num_scalar_prefetch=1,
            grid=(steps,),
            in_specs=[
                whole((rows, 1)),
                whole((rows, 1)),
                whole((NY, NZ, HD)),
                whole((NY, NZ, HD)),
                pl.BlockSpec(block, index),
                pl.BlockSpec(block, index_other),
            ]
            + [pl.BlockSpec((1, rows, HD), lambda g, at: (g, 0, 0)) for _ in pieces],
            out_specs=whole((rows, 3 * HD)),
            scratch_shapes=[pltpu.VMEM((rows, 6 * HD), jnp.float32)],
        ),
        out_shape=jax.ShapeDtypeStruct((rows, 3 * HD), jnp.float32),
        compiler_params=pltpu.CompilerParams(vmem_limit_bytes=40 * 2**20),
        cost_estimate=pl.CostEstimate(
            flops=2 * rows * 4096 * 6 * HD, bytes_accessed=8 * 2**20, transcendentals=0
        ),
    )(at, inverse, own_row, gain, gain_other, w, w_other, *pieces)


def headnorm(x, gain_row):
    average = jnp.mean(x, axis=1, keepdims=True)
    centred = x - average
    variance = jnp.mean(centred * centred, axis=1, keepdims=True)
    return centred * lax.rsqrt(variance + EPS) * gain_row[None, :]


def rotate(x, cosines, sines):
    lower, upper = x[:, : HD // 2], x[:, HD // 2 :]
    return jnp.concatenate([lower * cosines - upper * sines, upper * cosines + lower * sines], axis=1)


def attention_kernel(base_ref, q_ref, *rest):
    key_refs, out_ref = rest[:-1], rest[-1]
    rows = q_ref.shape[0]
    queries = q_ref[...]
    scale = 1.0 / math.sqrt(HD)
    row = base_ref[0] + lax.broadcasted_iota(jnp.int32, (rows, rows), 0)
    column = lax.broadcasted_iota(jnp.int32, (rows, rows), 1)
    blocks = [(ref, i) for ref in key_refs for i in range(ref.shape[0])]
    scores, seen = [], []
    for n, (ref, i) in enumerate(blocks):
        s = lax.dot_general(queries, ref[i, 0], (((1,), (1,)), ((), ())), preferred_element_type=jnp.float32)
        allowed = column + base_ref[n] <= row
        seen.append(allowed)
        scores.append(jnp.where(allowed, s * scale, MASKED))
    best = scores[0].max(axis=1, keepdims=True)
    for s in scores[1:]:
        best = jnp.maximum(best, s.max(axis=1, keepdims=True))
    total = jnp.zeros((rows, 1), jnp.float32)
    out = jnp.zeros((rows, HD), jnp.float32)
    for n, (ref, i) in enumerate(blocks):
        weights = jnp.where(seen[n], jnp.exp(scores[n] - best), 0.0)
        total += weights.sum(axis=1, keepdims=True)
        out += jnp.dot(weights.astype(jnp.bfloat16), ref[i, 1], preferred_element_type=jnp.float32)
    out_ref[...] = (out / total).astype(jnp.bfloat16)


def attention(bases, queries, keys):
    vmem = pl.BlockSpec(memory_space=pltpu.VMEM)
    return pl.pallas_call(
        attention_kernel,
        in_specs=[pl.BlockSpec(memory_space=pltpu.SMEM)] + [vmem] * (1 + len(keys)),
        out_specs=vmem,
        out_shape=jax.ShapeDtypeStruct(queries.shape, jnp.bfloat16),
        compiler_params=pltpu.CompilerParams(vmem_limit_bytes=40 * 2**20),
        cost_estimate=pl.CostEstimate(flops=2**28, bytes_accessed=2**20, transcendentals=2**19),
    )(bases, queries, *keys)


def out_kernel(own_row_ref, w_ref, w_other_ref, h0, h1, h2, h3, out_ref):
    heads = jnp.concatenate([h0[...], h1[...], h2[...], h3[...]], axis=1)
    sums = []
    for ref in (w_ref, w_other_ref):
        w = jnp.concatenate([ref[x, y] for y in range(NY) for x in range(NX)], axis=0)
        sums.append(jnp.dot(heads, w, preferred_element_type=jnp.float32))
    out_ref[0] = jnp.where(own_row_ref[...] > 0, *sums).astype(jnp.bfloat16)


def out_part(own_row, w, w_other, heads):
    rows = heads[0].shape[0]
    width = w.shape[-1] // NZ
    whole = lambda shape: pl.BlockSpec(shape, lambda g: (0,) * len(shape))
    weights = pl.BlockSpec((NX, NY, HD // NX, width), lambda g: (0, 0, 0, g))
    return pl.pallas_call(
        out_kernel,
        grid=(NZ,),
        in_specs=[whole((rows, 1)), weights, weights] + [whole((rows, HD))] * NY,
        out_specs=pl.BlockSpec((1, rows, width), lambda g: (g, 0, 0)),
        out_shape=jax.ShapeDtypeStruct((NZ, rows, width), jnp.bfloat16),
        compiler_params=pltpu.CompilerParams(vmem_limit_bytes=40 * 2**20),
        cost_estimate=pl.CostEstimate(
            flops=4 * rows * NY * HD * NZ * width, bytes_accessed=5 * 2**20, transcendentals=0
        ),
    )(own_row, w, w_other, *heads)


def spread_w_out(w_out, y, seq):
    quarter = lax.dynamic_slice_in_dim(w_out[0], seq * (HD // NX), HD // NX, axis=0)
    by_y = quarter.reshape(HD // NX, 2, NY, NZ, HD).transpose(2, 0, 3, 1, 4).reshape(NY, HD // NX, 2 * NZ * HD)
    pick = lambda d: lax.dynamic_index_in_dim(by_y, lax.rem(y - d + NY, NY), axis=0, keepdims=False)
    s1, s3, s2 = take(pick(1), dy=1), take(pick(3), dy=-1), take(pick(2), dy=2)
    lines = jnp.stack([pick(0), s1, s2, s3])
    return lax.all_gather(lines, "seq", axis=0)


def shards(tokens, modality, norm_gain, w_qkv, qk_gain, w_out):
    row_count = tokens.shape[0]
    half = row_count // 2
    c, y, z, seq = (lax.axis_index(a) for a in AXES)
    own_row = (modality == c).astype(jnp.int32)[:, None]

    squares = jnp.sum(jnp.square(tokens.astype(jnp.float32)), axis=1)
    pieces_a = gather_a(tokens[:ROWS_A])
    pieces_b = gather_b(tokens[ROWS_A:])
    squares = lax.psum(squares, ("mod", "y", "z"))
    inverse = lax.rsqrt(squares / (2 * NY * NZ * HD) + EPS)[:, None]

    w = w_qkv[0].transpose(1, 0, 2).reshape(3, 2, NY, NZ, HD, HD)
    gains = norm_gain.reshape(2, NY, NZ, HD)
    w_other = take(lax.dynamic_slice_in_dim(w, 1 - c, 1, axis=1), dc=1)
    gain_other = take(lax.dynamic_index_in_dim(gains, 1 - c, axis=0, keepdims=False), dc=1)
    gain = lax.dynamic_index_in_dim(gains, c, axis=0, keepdims=False)
    w_cols = spread_w_out(w_out, y, seq)
    w_cols_other = take(w_cols, dc=1)

    at = jnp.stack([c, y, z]).astype(jnp.int32)
    common = lambda rows: (at, inverse[rows], own_row[rows], gain, gain_other, w, w_other)
    part_a = qkv_part(*common(slice(None, ROWS_A)), pieces_a, False)
    part_b = qkv_part(*common(slice(ROWS_A, None)), pieces_b, True)
    parts = jnp.concatenate([part_a, part_b]).reshape(2, half, 3 * HD)
    mine = lax.dynamic_index_in_dim(parts, c, axis=0, keepdims=False)
    theirs = lax.dynamic_index_in_dim(parts, 1 - c, axis=0, keepdims=False)
    projected = mine + take(theirs, dc=1)

    first = seq * row_count + c * half
    places = first + jnp.arange(half, dtype=jnp.int32)
    rates = 1.0 / 10000.0 ** (jnp.arange(HD // 2, dtype=jnp.float32) * (2.0 / HD))
    angles = places.astype(jnp.float32)[:, None] * rates[None, :]
    cosines, sines = jnp.cos(angles), jnp.sin(angles)
    queries = rotate(headnorm(projected[:, :HD], qk_gain[0]), cosines, sines).astype(jnp.bfloat16)
    keys = rotate(headnorm(projected[:, HD : 2 * HD], qk_gain[1]), cosines, sines).astype(jnp.bfloat16)
    values = projected[:, 2 * HD :].astype(jnp.bfloat16)

    own_keys = jnp.stack([keys, values])
    got = jnp.stack([own_keys] + [take(own_keys, dx=-d, wrap_x=False) for d in (1, 2, 3)])
    sibling = take(got, dc=1)
    never = 1 << 20
    begin = [jnp.where(seq >= d, (seq - d) * row_count, never) for d in range(NX)]
    bases = jnp.stack([b + c * half for b in begin] + [b + (1 - c) * half for b in begin]).astype(jnp.int32)
    heads_out = attention(bases, queries, [got, sibling])

    h1, h3, h2 = take(heads_out, dy=1), take(heads_out, dy=-1), take(heads_out, dy=2)
    own_half = lax.dynamic_slice_in_dim(own_row, c * half, half, axis=0)
    partial = out_part(own_half, w_cols, w_cols_other, [heads_out, h1, h2, h3])
    spread = lax.all_to_all(partial, "z", 0, 0)
    summed = jnp.sum(spread.astype(jnp.float32), axis=0).astype(jnp.bfloat16).reshape(half, 2, HD)
    keep = lax.dynamic_index_in_dim(summed, c, axis=1, keepdims=False)
    other = take(lax.dynamic_index_in_dim(summed, 1 - c, axis=1, keepdims=False), dc=1)
    return jnp.where(c == 0, jnp.concatenate([keep, other]), jnp.concatenate([other, keep]))


def solution(mesh):
    mesh = Mesh(mesh.devices.reshape(2, NY, NZ, NX), AXES)
    tp = ("y", "z")
    placed = (
        P("seq", ("mod", *tp)),
        P("seq"),
        P("mod", None),
        P("mod", None, None, tp),
        P(None, tp),
        P("mod", tp, None),
    )
    return jax.shard_map(shards, mesh=mesh, in_specs=placed, out_specs=P("seq", ("mod", *tp)), check_vma=False)
```

```python
import math

import jax
import jax.numpy as jnp
import numpy as np
from jax import lax
from jax.experimental import pallas as pl
from jax.experimental.pallas import tpu as pltpu
from jax.sharding import Mesh
from jax.sharding import PartitionSpec as P

HD = 128
EPS = 1e-05
MASKED = -1e30
NY = 4
NZ = 8
NX = 4
AXES = ("mod", "y", "z", "seq")


def pairs(moves, wrap_x=True):
    out = []
    for c in range(2):
        if moves[c] is None:
            continue
        dc, dy, dz, dx = moves[c]
        for y in range(NY):
            for z in range(NZ):
                for x in range(NX):
                    if not wrap_x and not 0 <= x + dx < NX:
                        continue
                    source = (((c + dc) % 2 * NY + (y + dy) % NY) * NZ + (z + dz) % NZ) * NX + (x + dx) % NX
                    out.append((source, ((c * NY + y) * NZ + z) * NX + x))
    return out


def take(x, dc=0, dy=0, dz=0, dx=0, wrap_x=True):
    return lax.ppermute(x, AXES, pairs([(dc, dy, dz, dx)] * 2, wrap_x))


def take_by_core(x, on_y, on_z):
    return lax.ppermute(x, AXES, pairs([m and (0, *m, 0) for m in (on_y, on_z)]))


FIRST_Y = (0, 1, 3, 2)
FIRST_Z = (0, 1, 7, 2)
LATER_Z = (3, 6, 4, 5)


def gather(c, rows):
    k1 = take_by_core(rows, (1, 0), (0, 1))
    k2 = take_by_core(rows, (-1, 0), (0, -1))
    k3 = take_by_core(rows, (2, 0), (0, 2))
    g0 = jnp.stack([rows, k1, k2, k3])
    x1 = take_by_core(g0, (0, 1), (1, 0))
    x2 = take_by_core(g0, (0, -1), (-1, 0))
    k4 = take_by_core(k3, None, (0, 1))
    k5 = take_by_core(k2, None, (0, -1))
    k6 = take_by_core(k3, None, (0, 2))
    k7 = take_by_core(k2, None, (0, -2))
    g1 = jnp.stack([k4, k5, k6, k7])
    x3 = take_by_core(x1, (0, 1), (1, 0))
    x4 = take_by_core(jnp.where(c == 0, x2, g1), (0, -1), (-1, 0))
    x5 = take_by_core(jnp.where(c == 0, x3, g1), (0, 1), (1, 0))
    x6 = take_by_core(x4, (0, -1), (-1, 0))
    x7 = take_by_core(x5, (0, 1), None)
    return [g0, x1, x2, x3, x4, x5, x6], g1, x7


PLACES = np.array(
    [
        [[(dy, dz) for dy in FIRST_Y] for dz in (0, 1, 7, 2, 6, 3, 5, 4)],
        [
            [(dy, dz) for dz in order]
            for dy, order in (
                (0, FIRST_Z), (1, FIRST_Z), (3, FIRST_Z), (2, FIRST_Z),
                (3, LATER_Z), (1, LATER_Z), (2, LATER_Z), (0, LATER_Z),
            )
        ],
    ],
    np.int32,
)


def qkv_kernel(table_ref, inv_ref, own_row_ref, gain_ref, gain_other_ref, *rest):
    own_ws, other_ws, pieces = rest[:8], rest[8:16], rest[16:24]
    last_ref, out_ref, acc = rest[24:]
    step = pl.program_id(0)
    inverse = inv_ref[...]
    own_row = own_row_ref[...] > 0
    on_y = table_ref[0] == 0
    normed, right = [], []
    for k, piece in enumerate(pieces):
        at = 1 + 2 * (4 * k + step)
        yi, zi = table_ref[at], table_ref[at + 1]
        gain = jnp.where(own_row, gain_ref[yi, pl.ds(zi, 1), :], gain_other_ref[yi, pl.ds(zi, 1), :])
        value = piece[0] if k < 7 else jnp.where(on_y, last_ref[0], piece[0])
        normed.append((value.astype(jnp.float32) * inverse * gain).astype(jnp.bfloat16))
        right.append(jnp.concatenate([w[p, 0, 0, 0] for w in (own_ws[k], other_ws[k]) for p in range(3)], axis=1))
    part = jnp.dot(
        jnp.concatenate(normed, axis=1), jnp.concatenate(right, axis=0), preferred_element_type=jnp.float32
    )

    @pl.when(step == 0)
    def _():
        acc[...] = part

    @pl.when(step > 0)
    def _():
        acc[...] += part

    @pl.when(step == pl.num_programs(0) - 1)
    def _():
        out_ref[...] = jnp.where(own_row, acc[:, : 3 * HD], acc[:, 3 * HD :])


def project(table, inverse, own_row, gain, gain_other, w, w_other, arrays, g1, x7):
    rows = g1.shape[1]
    block = (3, 1, 1, 1, HD, HD)
    whole = lambda shape: pl.BlockSpec(shape, lambda g, t: (0,) * len(shape))
    piece = pl.BlockSpec((1, rows, HD), lambda g, t: (g, 0, 0))
    weights = lambda k, other: pl.BlockSpec(
        block, lambda g, t: (0, 0 if other else t[0], t[1 + 2 * (4 * k + g)], t[2 + 2 * (4 * k + g)], 0, 0)
    )
    return pl.pallas_call(
        qkv_kernel,
        grid_spec=pltpu.PrefetchScalarGridSpec(
            num_scalar_prefetch=1,
            grid=(4,),
            in_specs=[whole((rows, 1)), whole((rows, 1)), whole((NY, NZ, HD)), whole((NY, NZ, HD))]
            + [weights(k, False) for k in range(8)]
            + [weights(k, True) for k in range(8)]
            + [piece] * 9,
            out_specs=whole((rows, 3 * HD)),
            scratch_shapes=[pltpu.VMEM((rows, 6 * HD), jnp.float32)],
        ),
        out_shape=jax.ShapeDtypeStruct((rows, 3 * HD), jnp.float32),
        compiler_params=pltpu.CompilerParams(vmem_limit_bytes=40 * 2**20),
        cost_estimate=pl.CostEstimate(
            flops=2 * rows * 4096 * 6 * HD, bytes_accessed=11 * 2**20, transcendentals=0
        ),
    )(table, inverse, own_row, gain, gain_other, *[w] * 8, *[w_other] * 8, *arrays, g1, x7)


def headnorm(x, gain_row):
    average = jnp.mean(x, axis=1, keepdims=True)
    centred = x - average
    variance = jnp.mean(centred * centred, axis=1, keepdims=True)
    return centred * lax.rsqrt(variance + EPS) * gain_row[None, :]


def rotate(x, cosines, sines):
    lower, upper = x[:, : HD // 2], x[:, HD // 2 :]
    return jnp.concatenate([lower * cosines - upper * sines, upper * cosines + lower * sines], axis=1)


def attention_kernel(base_ref, q_ref, *rest):
    key_refs, out_ref = rest[:-1], rest[-1]
    rows = q_ref.shape[0]
    queries = q_ref[...]
    scale = 1.0 / math.sqrt(HD)
    row = base_ref[0] + lax.broadcasted_iota(jnp.int32, (rows, rows), 0)
    column = lax.broadcasted_iota(jnp.int32, (rows, rows), 1)
    blocks = [(ref, i) for ref in key_refs for i in range(ref.shape[0])]
    scores, seen = [], []
    for n, (ref, i) in enumerate(blocks):
        s = lax.dot_general(queries, ref[i, 0], (((1,), (1,)), ((), ())), preferred_element_type=jnp.float32)
        allowed = column + base_ref[n] <= row
        seen.append(allowed)
        scores.append(jnp.where(allowed, s * scale, MASKED))
    best = scores[0].max(axis=1, keepdims=True)
    for s in scores[1:]:
        best = jnp.maximum(best, s.max(axis=1, keepdims=True))
    total = jnp.zeros((rows, 1), jnp.float32)
    out = jnp.zeros((rows, HD), jnp.float32)
    for n, (ref, i) in enumerate(blocks):
        weights = jnp.where(seen[n], jnp.exp(scores[n] - best), 0.0)
        total += weights.sum(axis=1, keepdims=True)
        out += jnp.dot(weights.astype(jnp.bfloat16), ref[i, 1], preferred_element_type=jnp.float32)
    out_ref[...] = (out / total).astype(jnp.bfloat16)


def attention(bases, queries, keys):
    vmem = pl.BlockSpec(memory_space=pltpu.VMEM)
    return pl.pallas_call(
        attention_kernel,
        in_specs=[pl.BlockSpec(memory_space=pltpu.SMEM)] + [vmem] * (1 + len(keys)),
        out_specs=vmem,
        out_shape=jax.ShapeDtypeStruct(queries.shape, jnp.bfloat16),
        compiler_params=pltpu.CompilerParams(vmem_limit_bytes=40 * 2**20),
        cost_estimate=pl.CostEstimate(flops=2**28, bytes_accessed=2**20, transcendentals=2**19),
    )(bases, queries, *keys)


def out_kernel(own_row_ref, w_ref, w_other_ref, h0, h1, h2, h3, out_ref):
    heads = jnp.concatenate([h0[...], h1[...], h2[...], h3[...]], axis=1)
    sums = []
    for ref in (w_ref, w_other_ref):
        w = jnp.concatenate([ref[x, y] for y in range(NY) for x in range(NX)], axis=0)
        sums.append(jnp.dot(heads, w, preferred_element_type=jnp.float32))
    out_ref[0] = jnp.where(own_row_ref[...] > 0, *sums).astype(jnp.bfloat16)


def out_part(own_row, w, w_other, heads):
    rows = heads[0].shape[0]
    width = w.shape[-1] // NZ
    whole = lambda shape: pl.BlockSpec(shape, lambda g: (0,) * len(shape))
    weights = pl.BlockSpec((NX, NY, HD // NX, width), lambda g: (0, 0, 0, g))
    return pl.pallas_call(
        out_kernel,
        grid=(NZ,),
        in_specs=[whole((rows, 1)), weights, weights] + [whole((rows, HD))] * NY,
        out_specs=pl.BlockSpec((1, rows, width), lambda g: (g, 0, 0)),
        out_shape=jax.ShapeDtypeStruct((NZ, rows, width), jnp.bfloat16),
        compiler_params=pltpu.CompilerParams(vmem_limit_bytes=40 * 2**20),
        cost_estimate=pl.CostEstimate(
            flops=4 * rows * NY * HD * NZ * width, bytes_accessed=5 * 2**20, transcendentals=0
        ),
    )(own_row, w, w_other, *heads)


def spread_w_out(w_out, y, seq):
    quarter = lax.dynamic_slice_in_dim(w_out[0], seq * (HD // NX), HD // NX, axis=0)
    by_y = quarter.reshape(HD // NX, 2, NY, NZ, HD).transpose(2, 0, 3, 1, 4).reshape(NY, HD // NX, 2 * NZ * HD)
    pick = lambda d: lax.dynamic_index_in_dim(by_y, lax.rem(y - d + NY, NY), axis=0, keepdims=False)
    s1, s3, s2 = take(pick(1), dy=1), take(pick(3), dy=-1), take(pick(2), dy=2)
    lines = jnp.stack([pick(0), s1, s2, s3])
    return lax.all_gather(lines, "seq", axis=0)


def shards(tokens, modality, norm_gain, w_qkv, qk_gain, w_out):
    row_count = tokens.shape[0]
    half = row_count // 2
    c, y, z, seq = (lax.axis_index(a) for a in AXES)
    own_row = (modality == c).astype(jnp.int32)[:, None]

    w = w_qkv[0].transpose(1, 0, 2).reshape(3, 2, NY, NZ, HD, HD)
    gains = norm_gain.reshape(2, NY, NZ, HD)
    w_other = take(lax.dynamic_slice_in_dim(w, 1 - c, 1, axis=1), dc=1)
    gain_other = take(lax.dynamic_index_in_dim(gains, 1 - c, axis=0, keepdims=False), dc=1)
    gain = lax.dynamic_index_in_dim(gains, c, axis=0, keepdims=False)

    arrays, g1, x7 = gather(c, tokens)
    w_out, _ = lax.optimization_barrier((w_out, arrays[1]))
    w_cols = spread_w_out(w_out, y, seq)
    w_cols_other = take(w_cols, dc=1)

    squared = lambda a: jnp.sum(jnp.square(a.astype(jnp.float32)), axis=(0, 2))
    squares = sum(squared(a) for a in arrays) + jnp.where(c == 0, squared(x7), squared(g1))
    squares = squares + take(squares, dc=1)
    inverse = lax.rsqrt(squares / (2 * NY * NZ * HD) + EPS)[:, None]

    places = jnp.asarray(PLACES)[c].reshape(32, 2)
    places = lax.rem(places + jnp.stack([y, z]).astype(jnp.int32)[None, :], jnp.array([NY, NZ], jnp.int32)[None, :])
    table = jnp.concatenate([c.astype(jnp.int32)[None], places.reshape(64)])
    parts = project(table, inverse, own_row, gain, gain_other, w, w_other, arrays, g1, x7)
    parts = parts.reshape(2, half, 3 * HD)
    mine = lax.dynamic_index_in_dim(parts, c, axis=0, keepdims=False)
    theirs = lax.dynamic_index_in_dim(parts, 1 - c, axis=0, keepdims=False)
    projected = mine + take(theirs, dc=1)

    first = seq * row_count + c * half
    places = first + jnp.arange(half, dtype=jnp.int32)
    rates = 1.0 / 10000.0 ** (jnp.arange(HD // 2, dtype=jnp.float32) * (2.0 / HD))
    angles = places.astype(jnp.float32)[:, None] * rates[None, :]
    cosines, sines = jnp.cos(angles), jnp.sin(angles)
    queries = rotate(headnorm(projected[:, :HD], qk_gain[0]), cosines, sines).astype(jnp.bfloat16)
    keys = rotate(headnorm(projected[:, HD : 2 * HD], qk_gain[1]), cosines, sines).astype(jnp.bfloat16)
    values = projected[:, 2 * HD :].astype(jnp.bfloat16)

    own_keys = jnp.stack([keys, values])
    got = jnp.stack([own_keys] + [take(own_keys, dx=-d, wrap_x=False) for d in (1, 2, 3)])
    sibling = take(got, dc=1)
    never = 1 << 20
    begin = [jnp.where(seq >= d, (seq - d) * row_count, never) for d in range(NX)]
    bases = jnp.stack([b + c * half for b in begin] + [b + (1 - c) * half for b in begin]).astype(jnp.int32)
    heads_out = attention(bases, queries, [got, sibling])

    h1, h3, h2 = take(heads_out, dy=1), take(heads_out, dy=-1), take(heads_out, dy=2)
    own_half = lax.dynamic_slice_in_dim(own_row, c * half, half, axis=0)
    partial = out_part(own_half, w_cols, w_cols_other, [heads_out, h1, h2, h3])
    spread = lax.all_to_all(partial, "z", 0, 0)
    summed = jnp.sum(spread.astype(jnp.float32), axis=0).astype(jnp.bfloat16).reshape(half, 2, HD)
    keep = lax.dynamic_index_in_dim(summed, c, axis=1, keepdims=False)
    other = take(lax.dynamic_index_in_dim(summed, 1 - c, axis=1, keepdims=False), dc=1)
    return jnp.where(c == 0, jnp.concatenate([keep, other]), jnp.concatenate([other, keep]))


def solution(mesh):
    mesh = Mesh(mesh.devices.reshape(2, NY, NZ, NX), AXES)
    tp = ("y", "z")
    placed = (
        P("seq", ("mod", *tp)),
        P("seq"),
        P("mod", None),
        P("mod", None, None, tp),
        P(None, tp),
        P("mod", tp, None),
    )
    return jax.shard_map(shards, mesh=mesh, in_specs=placed, out_specs=P("seq", ("mod", *tp)), check_vma=False)
```

```python
import math

import jax
import jax.numpy as jnp
from jax import lax
from jax.experimental import pallas as pl
from jax.experimental.pallas import tpu as pltpu
from jax.sharding import Mesh
from jax.sharding import PartitionSpec as P

HD = 128
EPS = 1e-05
MASKED = -1e30
NY = 4
NZ = 8
NX = 4
AXES = ("mod", "y", "z", "seq")


def pairs(moves, wrap_x=True):
    out = []
    for c in range(2):
        if moves[c] is None:
            continue
        dc, dy, dz, dx = moves[c]
        for y in range(NY):
            for z in range(NZ):
                for x in range(NX):
                    if not wrap_x and not 0 <= x + dx < NX:
                        continue
                    source = (((c + dc) % 2 * NY + (y + dy) % NY) * NZ + (z + dz) % NZ) * NX + (x + dx) % NX
                    out.append((source, ((c * NY + y) * NZ + z) * NX + x))
    return out


def take(x, dc=0, dy=0, dz=0, dx=0, wrap_x=True):
    return lax.ppermute(x, AXES, pairs([(dc, dy, dz, dx)] * 2, wrap_x))


def take_by_core(x, on_y, on_z):
    return lax.ppermute(x, AXES, pairs([m and (0, *m, 0) for m in (on_y, on_z)]))


def gather(rows):
    k1 = take_by_core(rows, (1, 0), (0, 2))
    k2 = take_by_core(rows, (-1, 0), (0, -2))
    k3 = take_by_core(rows, (2, 0), (0, 4))
    g0 = jnp.stack([rows, k1, k2, k3])
    g1 = take_by_core(g0, (0, 1), (0, -1))
    x2 = take_by_core(g0, (0, -1), (-1, 0))
    x1 = take_by_core(g1, (0, 1), (1, 0))
    x4 = take_by_core(x2, (0, -1), (-1, 0))
    x3 = take_by_core(x1, (0, 1), (1, 0))
    x6 = take_by_core(x4, (0, -1), (-1, 0))
    x5 = take_by_core(x3, (0, 1), (1, 0))
    return [g0, g1, x1, x2, x3, x4, x5, x6]


OFFSETS = ((0, 0, 0), (1, 0, 7), (2, 1, 7), (7, 3, 0), (3, 2, 7), (6, 2, 0), (4, 3, 7), (5, 1, 0))


def place(at, k, step):
    turn = step ^ (step >> 1)
    dz0, dy1, dz1 = OFFSETS[k]
    dy = jnp.where(at[0] == 0, turn, dy1)
    dz = jnp.where(at[0] == 0, dz0, 2 * turn + dz1)
    return (at[1] + dy) & (NY - 1), (at[2] + dz) & (NZ - 1)


def qkv_kernel(at_ref, inv_ref, own_row_ref, gain_ref, gain_other_ref, *rest):
    own_ws, other_ws, pieces = rest[:8], rest[8:16], rest[16:24]
    out_ref, acc = rest[24:]
    step = pl.program_id(0)
    inverse = inv_ref[...]
    own_row = own_row_ref[...] > 0
    normed, right = [], []
    for k, piece in enumerate(pieces):
        yi, zi = place(at_ref, k, step)
        gain = jnp.where(own_row, gain_ref[yi, pl.ds(zi, 1), :], gain_other_ref[yi, pl.ds(zi, 1), :])
        normed.append((piece[0].astype(jnp.float32) * inverse * gain).astype(jnp.bfloat16))
        right.append(jnp.concatenate([w[p, 0, 0, 0] for w in (own_ws[k], other_ws[k]) for p in range(3)], axis=1))
    part = jnp.dot(
        jnp.concatenate(normed, axis=1), jnp.concatenate(right, axis=0), preferred_element_type=jnp.float32
    )

    @pl.when(step == 0)
    def _():
        acc[...] = part

    @pl.when(step > 0)
    def _():
        acc[...] += part

    @pl.when(step == pl.num_programs(0) - 1)
    def _():
        out_ref[...] = jnp.where(own_row, acc[:, : 3 * HD], acc[:, 3 * HD :])


def project(at, inverse, own_row, gain, gain_other, w, w_other, arrays):
    rows = arrays[0].shape[1]
    block = (3, 1, 1, 1, HD, HD)
    whole = lambda shape: pl.BlockSpec(shape, lambda g, at: (0,) * len(shape))
    piece = pl.BlockSpec((1, rows, HD), lambda g, at: (g, 0, 0))
    weights = lambda k, other: pl.BlockSpec(
        block, lambda g, at: (0, 0 if other else at[0], *place(at, k, g), 0, 0)
    )
    return pl.pallas_call(
        qkv_kernel,
        grid_spec=pltpu.PrefetchScalarGridSpec(
            num_scalar_prefetch=1,
            grid=(4,),
            in_specs=[whole((rows, 1)), whole((rows, 1)), whole((NY, NZ, HD)), whole((NY, NZ, HD))]
            + [weights(k, False) for k in range(8)]
            + [weights(k, True) for k in range(8)]
            + [piece] * 8,
            out_specs=whole((rows, 3 * HD)),
            scratch_shapes=[pltpu.VMEM((rows, 6 * HD), jnp.float32)],
        ),
        out_shape=jax.ShapeDtypeStruct((rows, 3 * HD), jnp.float32),
        compiler_params=pltpu.CompilerParams(vmem_limit_bytes=56 * 2**20),
        cost_estimate=pl.CostEstimate(
            flops=2 * rows * 4096 * 6 * HD, bytes_accessed=11 * 2**20, transcendentals=0
        ),
    )(at, inverse, own_row, gain, gain_other, *[w] * 8, *[w_other] * 8, *arrays)


def headnorm(x, gain_row):
    average = jnp.mean(x, axis=1, keepdims=True)
    centred = x - average
    variance = jnp.mean(centred * centred, axis=1, keepdims=True)
    return centred * lax.rsqrt(variance + EPS) * gain_row[None, :]


def rotate(x, cosines, sines):
    lower, upper = x[:, : HD // 2], x[:, HD // 2 :]
    return jnp.concatenate([lower * cosines - upper * sines, upper * cosines + lower * sines], axis=1)


def attention_kernel(base_ref, q_ref, *rest):
    key_refs, out_ref = rest[:-1], rest[-1]
    rows = q_ref.shape[0]
    queries = q_ref[...]
    scale = 1.0 / math.sqrt(HD)
    row = base_ref[0] + lax.broadcasted_iota(jnp.int32, (rows, rows), 0)
    column = lax.broadcasted_iota(jnp.int32, (rows, rows), 1)
    blocks = [(ref, i) for ref in key_refs for i in range(ref.shape[0])]
    scores, seen = [], []
    for n, (ref, i) in enumerate(blocks):
        s = lax.dot_general(queries, ref[i, 0], (((1,), (1,)), ((), ())), preferred_element_type=jnp.float32)
        allowed = column + base_ref[n] <= row
        seen.append(allowed)
        scores.append(jnp.where(allowed, s * scale, MASKED))
    best = scores[0].max(axis=1, keepdims=True)
    for s in scores[1:]:
        best = jnp.maximum(best, s.max(axis=1, keepdims=True))
    total = jnp.zeros((rows, 1), jnp.float32)
    out = jnp.zeros((rows, HD), jnp.float32)
    for n, (ref, i) in enumerate(blocks):
        weights = jnp.where(seen[n], jnp.exp(scores[n] - best), 0.0)
        total += weights.sum(axis=1, keepdims=True)
        out += jnp.dot(weights.astype(jnp.bfloat16), ref[i, 1], preferred_element_type=jnp.float32)
    out_ref[...] = (out / total).astype(jnp.bfloat16)


def attention(bases, queries, keys):
    vmem = pl.BlockSpec(memory_space=pltpu.VMEM)
    return pl.pallas_call(
        attention_kernel,
        in_specs=[pl.BlockSpec(memory_space=pltpu.SMEM)] + [vmem] * (1 + len(keys)),
        out_specs=vmem,
        out_shape=jax.ShapeDtypeStruct(queries.shape, jnp.bfloat16),
        compiler_params=pltpu.CompilerParams(vmem_limit_bytes=40 * 2**20),
        cost_estimate=pl.CostEstimate(flops=2**28, bytes_accessed=2**20, transcendentals=2**19),
    )(bases, queries, *keys)


def out_kernel(own_row_ref, w0, w1, o0, o1, h0, h1, h2, h3, out_ref):
    heads = jnp.concatenate([h0[...], h1[...], h2[...], h3[...]], axis=1)
    own_row = own_row_ref[...] > 0
    sections = []
    for refs in ((w0, w1), (o0, o1)):
        w = jnp.concatenate(
            [jnp.concatenate([ref[x, y] for y in range(NY) for x in range(NX)], axis=0) for ref in refs], axis=1
        )
        sections.append(jnp.dot(heads, w, preferred_element_type=jnp.float32))
    both = jnp.where(own_row, *sections).astype(jnp.bfloat16)
    for i in range(2):
        out_ref[i, :, :HD] = both[:, i * HD : (i + 1) * HD]
        out_ref[i, :, HD:] = both[:, (2 + i) * HD : (3 + i) * HD]


def out_part(own_row, w, w_other, heads):
    rows = heads[0].shape[0]
    steps = NZ // 2
    whole = lambda shape: pl.BlockSpec(shape, lambda g: (0,) * len(shape))
    left = pl.BlockSpec((NX, NY, HD // NX, 2 * HD), lambda g: (0, 0, 0, g))
    right = pl.BlockSpec((NX, NY, HD // NX, 2 * HD), lambda g: (0, 0, 0, steps + g))
    return pl.pallas_call(
        out_kernel,
        grid=(steps,),
        in_specs=[whole((rows, 1)), left, right, left, right] + [whole((rows, HD))] * NY,
        out_specs=pl.BlockSpec((2, rows, 2 * HD), lambda g: (g, 0, 0)),
        out_shape=jax.ShapeDtypeStruct((NZ, rows, 2 * HD), jnp.bfloat16),
        compiler_params=pltpu.CompilerParams(vmem_limit_bytes=56 * 2**20),
        cost_estimate=pl.CostEstimate(
            flops=8 * rows * NY * HD * NZ * HD, bytes_accessed=5 * 2**20, transcendentals=0
        ),
    )(own_row, w, w, w_other, w_other, *heads)


def spread_w_out(w_out, y, seq):
    rows, width = HD // NX, NZ * HD

    def pick(d):
        column = ((y - d) & (NY - 1)) * width
        cut = lambda first: lax.dynamic_slice(w_out[0], (seq * rows, first + column), (rows, width))
        return jnp.concatenate([cut(0), cut(NY * width)], axis=1)

    s1, s3, s2 = take(pick(1), dy=1), take(pick(3), dy=-1), take(pick(2), dy=2)
    lines = jnp.stack([pick(0), s1, s2, s3])
    return lax.all_gather(lines, "seq", axis=0)


def shards(tokens, modality, norm_gain, w_qkv, qk_gain, w_out):
    row_count = tokens.shape[0]
    half = row_count // 2
    c, y, z, seq = (lax.axis_index(a) for a in AXES)
    own_row = (modality == c).astype(jnp.int32)[:, None]

    arrays = gather(tokens)
    w_cols = spread_w_out(w_out, y, seq)

    w = w_qkv[0].transpose(1, 0, 2).reshape(3, 2, NY, NZ, HD, HD)
    gains = norm_gain.reshape(2, NY, NZ, HD)
    gain_other = take(lax.dynamic_index_in_dim(gains, 1 - c, axis=0, keepdims=False), dc=1)
    gain = lax.dynamic_index_in_dim(gains, c, axis=0, keepdims=False)
    w_send, gain_other = lax.optimization_barrier((lax.dynamic_slice_in_dim(w, 1 - c, 1, axis=1), gain_other))
    w_other = take(w_send, dc=1)

    squared = [jnp.sum(jnp.square(a.astype(jnp.float32)), axis=(0, 2)) for a in arrays]
    early, w_cols = lax.optimization_barrier((sum(squared[:6]), w_cols))
    w_cols_other = take(w_cols, dc=1)
    squares = early + squared[6] + squared[7]
    squares = squares + take(squares, dc=1)
    inverse = lax.rsqrt(squares / (2 * NY * NZ * HD) + EPS)[:, None]
    at = jnp.stack([c, y, z]).astype(jnp.int32)
    parts = project(at, inverse, own_row, gain, gain_other, w, w_other, arrays)
    parts = parts.reshape(2, half, 3 * HD)
    mine = lax.dynamic_index_in_dim(parts, c, axis=0, keepdims=False)
    theirs = lax.dynamic_index_in_dim(parts, 1 - c, axis=0, keepdims=False)
    projected = mine + take(theirs, dc=1)

    first = seq * row_count + c * half
    places = first + jnp.arange(half, dtype=jnp.int32)
    rates = 1.0 / 10000.0 ** (jnp.arange(HD // 2, dtype=jnp.float32) * (2.0 / HD))
    angles = places.astype(jnp.float32)[:, None] * rates[None, :]
    cosines, sines = jnp.cos(angles), jnp.sin(angles)
    queries = rotate(headnorm(projected[:, :HD], qk_gain[0]), cosines, sines).astype(jnp.bfloat16)
    keys = rotate(headnorm(projected[:, HD : 2 * HD], qk_gain[1]), cosines, sines).astype(jnp.bfloat16)
    values = projected[:, 2 * HD :].astype(jnp.bfloat16)

    own_keys = jnp.stack([keys, values])
    got = jnp.stack([own_keys] + [take(own_keys, dx=-d, wrap_x=False) for d in (1, 2, 3)])
    sibling = take(got, dc=1)
    never = 1 << 20
    begin = [jnp.where(seq >= d, (seq - d) * row_count, never) for d in range(NX)]
    bases = jnp.stack([b + c * half for b in begin] + [b + (1 - c) * half for b in begin]).astype(jnp.int32)
    heads_out = attention(bases, queries, [got, sibling])

    h1, h3, h2 = take(heads_out, dy=1), take(heads_out, dy=-1), take(heads_out, dy=2)
    own_half = lax.dynamic_slice_in_dim(own_row, c * half, half, axis=0)
    partial = out_part(own_half, w_cols, w_cols_other, [heads_out, h1, h2, h3])
    spread = lax.all_to_all(partial, "z", 0, 0)
    summed = jnp.sum(spread.astype(jnp.float32), axis=0).astype(jnp.bfloat16).reshape(half, 2, HD)
    keep = lax.dynamic_index_in_dim(summed, c, axis=1, keepdims=False)
    other = take(lax.dynamic_index_in_dim(summed, 1 - c, axis=1, keepdims=False), dc=1)
    return jnp.where(c == 0, jnp.concatenate([keep, other]), jnp.concatenate([other, keep]))


def solution(mesh):
    mesh = Mesh(mesh.devices.reshape(2, NY, NZ, NX), AXES)
    tp = ("y", "z")
    placed = (
        P("seq", ("mod", *tp)),
        P("seq"),
        P("mod", None),
        P("mod", None, None, tp),
        P(None, tp),
        P("mod", tp, None),
    )
    return jax.shard_map(shards, mesh=mesh, in_specs=placed, out_specs=P("seq", ("mod", *tp)), check_vma=False)
```

```python
import math

import jax
import jax.numpy as jnp
from jax import lax
from jax.experimental import pallas as pl
from jax.experimental.pallas import tpu as pltpu
from jax.sharding import Mesh
from jax.sharding import PartitionSpec as P

HD = 128
EPS = 1e-05
MASKED = -1e30
NY = 4
NZ = 8
NX = 4
AXES = ("mod", "y", "zh", "zl", "seq")


def pairs(moves, wrap_x=True):
    out = []
    for c in range(2):
        if moves[c] is None:
            continue
        dc, dy, dz, dx = moves[c]
        for y in range(NY):
            for z in range(NZ):
                for x in range(NX):
                    if not wrap_x and not 0 <= x + dx < NX:
                        continue
                    from_z = z ^ 1 if dz == "pair" else (z + dz) % NZ
                    source = (((c + dc) % 2 * NY + (y + dy) % NY) * NZ + from_z) * NX + (x + dx) % NX
                    out.append((source, ((c * NY + y) * NZ + z) * NX + x))
    return out


def take(x, dc=0, dy=0, dz=0, dx=0, wrap_x=True):
    return lax.ppermute(x, AXES, pairs([(dc, dy, dz, dx)] * 2, wrap_x))


def take_by_core(x, on_y, on_z):
    return lax.ppermute(x, AXES, pairs([m and (0, *m, 0) for m in (on_y, on_z)]))


def gather(rows):
    k1 = take_by_core(rows, (1, 0), (0, 2))
    k2 = take_by_core(rows, (-1, 0), (0, -2))
    k3 = take_by_core(rows, (2, 0), (0, 4))
    g0 = jnp.stack([rows, k1, k2, k3])
    g1 = take_by_core(g0, (0, 1), (0, -1))
    x2 = take_by_core(g0, (0, -1), (-1, 0))
    x1 = take_by_core(g1, (0, 1), (1, 0))
    x4 = take_by_core(x2, (0, -1), (-1, 0))
    x3 = take_by_core(x1, (0, 1), (1, 0))
    x6 = take_by_core(x4, (0, -1), (-1, 0))
    x5 = take_by_core(x3, (0, 1), (1, 0))
    return [g0, g1, x1, x2, x3, x4, x5, x6], [k1, k2, k3]


OFFSETS = ((0, 0, 0), (1, 0, 7), (2, 1, 7), (7, 3, 0), (3, 2, 7), (6, 2, 0), (4, 3, 7), (5, 1, 0))


def place(at, k, step):
    turn = step ^ (step >> 1)
    dz0, dy1, dz1 = OFFSETS[k]
    dy = jnp.where(at[0] == 0, turn, dy1)
    dz = jnp.where(at[0] == 0, dz0, 2 * turn + dz1)
    return (at[1] + dy) & (NY - 1), (at[2] + dz) & (NZ - 1)


def columns(row):
    return jnp.broadcast_to(row, (HD, row.shape[1])).T


def qkv_kernel(at_ref, squares_ref, modality_ref, gain_ref, gain_other_ref, *rest):
    own_ws, other_ws, pieces = rest[:8], rest[8:16], rest[16:24]
    out_ref, acc, inv, own = rest[24:]
    step = pl.program_id(0)

    @pl.when(step == 0)
    def _():
        inv[...] = columns(lax.rsqrt(squares_ref[...] / (2 * NY * NZ * HD) + EPS))
        own[...] = columns((modality_ref[...] == at_ref[0]).astype(jnp.float32))

    inverse = inv[...]
    own_row = own[...] > 0
    normed, right = [], []
    for k, piece in enumerate(pieces):
        yi, zi = place(at_ref, k, step)
        gain = jnp.where(own_row, gain_ref[yi, pl.ds(zi, 1), :], gain_other_ref[yi, pl.ds(zi, 1), :])
        normed.append((piece[0].astype(jnp.float32) * inverse * gain).astype(jnp.bfloat16))
        right.append(jnp.concatenate([w[p, 0, 0, 0] for w in (own_ws[k], other_ws[k]) for p in range(3)], axis=1))
    part = jnp.dot(
        jnp.concatenate(normed, axis=1), jnp.concatenate(right, axis=0), preferred_element_type=jnp.float32
    )

    @pl.when(step == 0)
    def _():
        acc[...] = part

    @pl.when(step > 0)
    def _():
        acc[...] += part

    @pl.when(step == pl.num_programs(0) - 1)
    def _():
        for p in range(3):
            low, high = acc[:, p * HD : (p + 1) * HD], acc[:, (3 + p) * HD : (4 + p) * HD]
            out_ref[:, p * HD : (p + 1) * HD] = jnp.where(own_row, low, high)


def project(at, squares, modality, gain, gain_other, w, w_other, arrays):
    rows = arrays[0].shape[1]
    block = (3, 1, 1, 1, HD, HD)
    whole = lambda shape: pl.BlockSpec(shape, lambda g, at: (0,) * len(shape))
    piece = pl.BlockSpec((1, rows, HD), lambda g, at: (g, 0, 0))
    weights = lambda k, other: pl.BlockSpec(
        block, lambda g, at: (0, 0 if other else at[0], *place(at, k, g), 0, 0)
    )
    return pl.pallas_call(
        qkv_kernel,
        grid_spec=pltpu.PrefetchScalarGridSpec(
            num_scalar_prefetch=1,
            grid=(4,),
            in_specs=[whole((1, rows)), whole((1, rows)), whole((NY, NZ, HD)), whole((NY, NZ, HD))]
            + [weights(k, False) for k in range(8)]
            + [weights(k, True) for k in range(8)]
            + [piece] * 8,
            out_specs=whole((rows, 3 * HD)),
            scratch_shapes=[pltpu.VMEM((rows, w), jnp.float32) for w in (6 * HD, HD, HD)],
        ),
        out_shape=jax.ShapeDtypeStruct((rows, 3 * HD), jnp.float32),
        compiler_params=pltpu.CompilerParams(vmem_limit_bytes=56 * 2**20),
        cost_estimate=pl.CostEstimate(
            flops=2 * rows * 4096 * 6 * HD, bytes_accessed=11 * 2**20, transcendentals=0
        ),
    )(at, squares, modality, gain, gain_other, *[w] * 8, *[w_other] * 8, *arrays)


def headnorm(x, gain_row):
    average = jnp.mean(x, axis=1, keepdims=True)
    centred = x - average
    variance = jnp.mean(centred * centred, axis=1, keepdims=True)
    return centred * lax.rsqrt(variance + EPS) * gain_row[None, :]


def rotate(x, cosines, sines):
    lower, upper = x[:, : HD // 2], x[:, HD // 2 :]
    return jnp.concatenate([lower * cosines - upper * sines, upper * cosines + lower * sines], axis=1)


def attention_kernel(base_ref, q_ref, *rest):
    key_refs, out_ref = rest[:-1], rest[-1]
    rows = q_ref.shape[0]
    queries = q_ref[...]
    scale = 1.0 / math.sqrt(HD)
    row = base_ref[0] + lax.broadcasted_iota(jnp.int32, (rows, rows), 0)
    column = lax.broadcasted_iota(jnp.int32, (rows, rows), 1)
    blocks = [(ref, i) for ref in key_refs for i in range(ref.shape[0])]
    scores, seen = [], []
    for n, (ref, i) in enumerate(blocks):
        s = lax.dot_general(queries, ref[i, 0], (((1,), (1,)), ((), ())), preferred_element_type=jnp.float32)
        allowed = column + base_ref[n] <= row
        seen.append(allowed)
        scores.append(jnp.where(allowed, s * scale, MASKED))
    best = scores[0].max(axis=1, keepdims=True)
    for s in scores[1:]:
        best = jnp.maximum(best, s.max(axis=1, keepdims=True))
    total = jnp.zeros((rows, 1), jnp.float32)
    out = jnp.zeros((rows, HD), jnp.float32)
    for n, (ref, i) in enumerate(blocks):
        weights = jnp.where(seen[n], jnp.exp(scores[n] - best), 0.0)
        total += weights.sum(axis=1, keepdims=True)
        out += jnp.dot(weights.astype(jnp.bfloat16), ref[i, 1], preferred_element_type=jnp.float32)
    out_ref[...] = (out / total).astype(jnp.bfloat16)


def attention(bases, queries, keys):
    vmem = pl.BlockSpec(memory_space=pltpu.VMEM)
    return pl.pallas_call(
        attention_kernel,
        in_specs=[pl.BlockSpec(memory_space=pltpu.SMEM)] + [vmem] * (1 + len(keys)),
        out_specs=vmem,
        out_shape=jax.ShapeDtypeStruct(queries.shape, jnp.bfloat16),
        compiler_params=pltpu.CompilerParams(vmem_limit_bytes=40 * 2**20),
        cost_estimate=pl.CostEstimate(flops=2**28, bytes_accessed=2**20, transcendentals=2**19),
    )(bases, queries, *keys)


def out_kernel(at_ref, modality_ref, w0, w1, o0, o1, h0, h1, h2, h3, out_ref):
    heads = jnp.concatenate([h[e] for h in (h0, h1, h2, h3) for e in range(2)], axis=1)
    own_row = columns((modality_ref[...] == at_ref[0]).astype(jnp.float32)) > 0
    for i, refs in enumerate(((w0, o0), (w1, o1))):
        sections = []
        for ref in refs:
            w = jnp.concatenate(
                [ref[x, y, e] for y in range(NY) for e in range(2) for x in range(NX)], axis=0
            )
            sections.append(jnp.dot(heads, w, preferred_element_type=jnp.float32))
        out_ref[0, :, i * HD : (i + 1) * HD] = jnp.where(own_row, *sections).astype(jnp.bfloat16)


def out_part(at, modality, w, w_other, heads):
    rows = heads[0].shape[1]
    steps = NZ // 2
    whole = lambda shape: pl.BlockSpec(shape, lambda g, at: (0,) * len(shape))
    left = pl.BlockSpec((NX, NY, 2, HD // NX, HD), lambda g, at: (0, 0, 0, 0, g))
    right = pl.BlockSpec((NX, NY, 2, HD // NX, HD), lambda g, at: (0, 0, 0, 0, steps + g))
    return pl.pallas_call(
        out_kernel,
        grid_spec=pltpu.PrefetchScalarGridSpec(
            num_scalar_prefetch=1,
            grid=(steps,),
            in_specs=[whole((1, rows)), left, right, left, right] + [whole((2, rows, HD))] * NY,
            out_specs=pl.BlockSpec((1, rows, 2 * HD), lambda g, at: (g, 0, 0)),
        ),
        out_shape=jax.ShapeDtypeStruct((steps, rows, 2 * HD), jnp.bfloat16),
        compiler_params=pltpu.CompilerParams(vmem_limit_bytes=56 * 2**20),
        cost_estimate=pl.CostEstimate(
            flops=8 * rows * NY * HD * NZ * HD, bytes_accessed=5 * 2**20, transcendentals=0
        ),
    )(at, modality, w, w, w_other, w_other, *heads)


def cut_kernel(at_ref, w_ref, keep_ref, send_ref):
    odd = at_ref[2] & 1
    for d in range(NY):
        to_y = (at_ref[1] - d) & (NY - 1)
        for c in range(2):
            for zh in range(NZ // 2):
                first = (c * NY + to_y) * NZ * HD + 2 * zh * HD
                lanes = pl.ds((c * (NZ // 2) + zh) * HD, HD)
                keep_ref[d, :, lanes] = w_ref[:, pl.ds(pl.multiple_of(first + odd * HD, HD), HD)]
                send_ref[d, :, lanes] = w_ref[:, pl.ds(pl.multiple_of(first + (1 - odd) * HD, HD), HD)]


def after(x, *others):
    return lax.optimization_barrier((x, *others))[0]


def spread_w_out(at, w_out, first, second, third):
    rows, width = HD // NX, NZ * HD
    piece = jax.ShapeDtypeStruct((NY, rows, width), jnp.bfloat16)
    whole = pl.BlockSpec((NY, rows, width), lambda g, at: (0, 0, 0))
    keep, send = pl.pallas_call(
        cut_kernel,
        grid_spec=pltpu.PrefetchScalarGridSpec(
            num_scalar_prefetch=1,
            grid=(1,),
            in_specs=[pl.BlockSpec((rows, w_out.shape[1]), lambda g, at: (at[3], 0))],
            out_specs=[whole, whole],
        ),
        out_shape=[piece, piece],
        cost_estimate=pl.CostEstimate(flops=0, bytes_accessed=2**20, transcendentals=0),
    )(at, after(w_out, *first))
    both = after(jnp.stack([keep, take(send, dz="pair")], axis=1), second)
    s1, s3, s2 = take(both[1], dy=1), take(both[3], dy=-1), take(both[2], dy=2)
    lines = after(jnp.stack([both[0], s1, s2, s3]), third)
    return lax.all_gather(lines, "seq", axis=0)


def shards(tokens, modality, norm_gain, w_qkv, qk_gain, w_out):
    row_count = tokens.shape[0]
    half = row_count // 2
    c, y, zh, zl, seq = (lax.axis_index(a) for a in AXES)
    z = 2 * zh + zl
    at = jnp.stack([c, y, z, seq]).astype(jnp.int32)
    modality = modality[None, :]

    arrays, direct = gather(tokens)
    w_cols = spread_w_out(at, w_out[0], direct, arrays[1], arrays[2])
    w_cols_other = take(w_cols, dc=1)

    w = w_qkv[0].transpose(1, 0, 2).reshape(3, 2, NY, NZ, HD, HD)
    gains = norm_gain.reshape(2, NY, NZ, HD)
    gain_other = take(lax.dynamic_index_in_dim(gains, 1 - c, axis=0, keepdims=False), dc=1)
    gain = lax.dynamic_index_in_dim(gains, c, axis=0, keepdims=False)
    w_other = take(lax.dynamic_slice_in_dim(after(w, direct[0]), 1 - c, 1, axis=1), dc=1)

    squared = [jnp.sum(jnp.square(a.astype(jnp.float32)), axis=(0, 2)) for a in arrays]
    squares = sum(squared)
    squares = squares + take(squares, dc=1)
    parts = project(at, squares[None, :], modality, gain, gain_other, w, w_other, arrays)
    parts = parts.reshape(2, half, 3 * HD)
    mine = lax.dynamic_index_in_dim(parts, c, axis=0, keepdims=False)
    theirs = lax.dynamic_index_in_dim(parts, 1 - c, axis=0, keepdims=False)
    projected = mine + take(theirs, dc=1)

    first = seq * row_count + c * half
    places = first + jnp.arange(half, dtype=jnp.int32)
    rates = 1.0 / 10000.0 ** (jnp.arange(HD // 2, dtype=jnp.float32) * (2.0 / HD))
    angles = places.astype(jnp.float32)[:, None] * rates[None, :]
    cosines, sines = jnp.cos(angles), jnp.sin(angles)
    queries = rotate(headnorm(projected[:, :HD], qk_gain[0]), cosines, sines).astype(jnp.bfloat16)
    keys = rotate(headnorm(projected[:, HD : 2 * HD], qk_gain[1]), cosines, sines).astype(jnp.bfloat16)
    values = projected[:, 2 * HD :].astype(jnp.bfloat16)

    own_keys = jnp.stack([keys, values])
    got = jnp.stack([own_keys] + [take(own_keys, dx=-d, wrap_x=False) for d in (1, 2, 3)])
    sibling = take(got, dc=1)
    never = 1 << 20
    begin = [jnp.where(seq >= d, (seq - d) * row_count, never) for d in range(NX)]
    bases = jnp.stack([b + c * half for b in begin] + [b + (1 - c) * half for b in begin]).astype(jnp.int32)
    heads_out = attention(bases, queries, [got, sibling])

    line = jnp.stack([heads_out, take(heads_out, dz="pair")])
    h1, h3, h2 = take(line, dy=1), take(line, dy=-1), take(line, dy=2)
    own_half = lax.dynamic_slice_in_dim(modality, c * half, half, axis=1)
    partial = out_part(at, own_half, w_cols, w_cols_other, [line, h1, h2, h3])
    spread = lax.all_to_all(partial, "zh", 0, 0)
    summed = jnp.sum(spread.astype(jnp.float32), axis=0).astype(jnp.bfloat16).reshape(half, 2, HD)
    keep = lax.dynamic_index_in_dim(summed, c, axis=1, keepdims=False)
    other = take(lax.dynamic_index_in_dim(summed, 1 - c, axis=1, keepdims=False), dc=1)
    return jnp.where(c == 0, jnp.concatenate([keep, other]), jnp.concatenate([other, keep]))


def solution(mesh):
    mesh = Mesh(mesh.devices.reshape(2, NY, NZ // 2, 2, NX), AXES)
    tp = ("y", "zh", "zl")
    placed = (
        P("seq", ("mod", *tp)),
        P("seq"),
        P("mod", None),
        P("mod", None, None, tp),
        P(None, tp),
        P("mod", tp, None),
    )
    return jax.shard_map(shards, mesh=mesh, in_specs=placed, out_specs=P("seq", ("mod", *tp)), check_vma=False)
```

```python
import math

import jax
import jax.numpy as jnp
from jax import lax
from jax.experimental import pallas as pl
from jax.experimental.pallas import tpu as pltpu
from jax.sharding import Mesh
from jax.sharding import PartitionSpec as P

HD = 128
EPS = 1e-05
MASKED = -1e30
NY = 4
NZ = 8
NX = 4
AXES = ("mod", "y", "zh", "zl", "seq")


def pairs(moves, wrap_x=True):
    out = []
    for c in range(2):
        if moves[c] is None:
            continue
        dc, dy, dz, dx = moves[c]
        for y in range(NY):
            for z in range(NZ):
                for x in range(NX):
                    if not wrap_x and not 0 <= x + dx < NX:
                        continue
                    from_z = z ^ 1 if dz == "pair" else (z + dz) % NZ
                    source = (((c + dc) % 2 * NY + (y + dy) % NY) * NZ + from_z) * NX + (x + dx) % NX
                    out.append((source, ((c * NY + y) * NZ + z) * NX + x))
    return out


def take(x, dc=0, dy=0, dz=0, dx=0, wrap_x=True):
    return lax.ppermute(x, AXES, pairs([(dc, dy, dz, dx)] * 2, wrap_x))


def take_by_core(x, on_y, on_z):
    return lax.ppermute(x, AXES, pairs([m and (0, *m, 0) for m in (on_y, on_z)]))


def gather(rows):
    k1 = take_by_core(rows, (1, 0), (0, 2))
    k2 = take_by_core(rows, (-1, 0), (0, -2))
    k3 = take_by_core(rows, (2, 0), (0, 4))
    g0 = jnp.stack([rows, k1, k2, k3])
    g1 = take_by_core(g0, (0, 1), (0, -1))
    x2 = take_by_core(g0, (0, -1), (-1, 0))
    x1 = take_by_core(g1, (0, 1), (1, 0))
    x4 = take_by_core(x2, (0, -1), (-1, 0))
    x3 = take_by_core(x1, (0, 1), (1, 0))
    x6 = take_by_core(x4, (0, -1), (-1, 0))
    x5 = take_by_core(x3, (0, 1), (1, 0))
    return [g0, g1, x1, x2, x3, x4, x5, x6], [k1, k2, k3]


OFFSETS = ((0, 0, 0), (1, 0, 7), (2, 1, 7), (7, 3, 0), (3, 2, 7), (6, 2, 0), (4, 3, 7), (5, 1, 0))


def place(at, k, step):
    turn = step ^ (step >> 1)
    dz0, dy1, dz1 = OFFSETS[k]
    dy = jnp.where(at[0] == 0, turn, dy1)
    dz = jnp.where(at[0] == 0, dz0, 2 * turn + dz1)
    return (at[1] + dy) & (NY - 1), (at[2] + dz) & (NZ - 1)


def columns(row):
    return jnp.broadcast_to(row, (HD, row.shape[1])).T


def qkv_kernel(at_ref, squares_ref, modality_ref, gain_ref, gain_other_ref, *rest):
    own_ws, other_ws, pieces = rest[:8], rest[8:16], rest[16:24]
    mine_ref, theirs_ref, acc, inv, own = rest[24:]
    step = pl.program_id(0)

    @pl.when(step == 0)
    def _():
        inv[...] = columns(lax.rsqrt(squares_ref[...] / (2 * NY * NZ * HD) + EPS))
        own[...] = columns((modality_ref[...] == at_ref[0]).astype(jnp.float32))

    inverse = inv[...]
    own_row = own[...] > 0
    normed, right = [], []
    for k, piece in enumerate(pieces):
        yi, zi = place(at_ref, k, step)
        gain = jnp.where(own_row, gain_ref[yi, pl.ds(zi, 1), :], gain_other_ref[yi, pl.ds(zi, 1), :])
        normed.append((piece[0].astype(jnp.float32) * inverse * gain).astype(jnp.bfloat16))
        right.append(jnp.concatenate([w[p, 0, 0, 0] for w in (own_ws[k], other_ws[k]) for p in range(3)], axis=1))
    part = jnp.dot(
        jnp.concatenate(normed, axis=1), jnp.concatenate(right, axis=0), preferred_element_type=jnp.float32
    )

    @pl.when(step == 0)
    def _():
        acc[...] = part

    @pl.when(step > 0)
    def _():
        acc[...] += part

    @pl.when(step == pl.num_programs(0) - 1)
    def _():
        half = acc.shape[0] // 2
        for ref, first in ((mine_ref, at_ref[0] * half), (theirs_ref, (1 - at_ref[0]) * half)):
            rows = pl.ds(pl.multiple_of(first, half), half)
            own_here = own[rows, :] > 0
            for p in range(3):
                low, high = acc[rows, p * HD : (p + 1) * HD], acc[rows, (3 + p) * HD : (4 + p) * HD]
                ref[:, p * HD : (p + 1) * HD] = jnp.where(own_here, low, high)


def project(at, squares, modality, gain, gain_other, w, w_other, arrays):
    rows = arrays[0].shape[1]
    block = (3, 1, 1, 1, HD, HD)
    whole = lambda shape: pl.BlockSpec(shape, lambda g, at: (0,) * len(shape))
    piece = pl.BlockSpec((1, rows, HD), lambda g, at: (g, 0, 0))
    weights = lambda k, other: pl.BlockSpec(
        block, lambda g, at: (0, 0 if other else at[0], *place(at, k, g), 0, 0)
    )
    return pl.pallas_call(
        qkv_kernel,
        grid_spec=pltpu.PrefetchScalarGridSpec(
            num_scalar_prefetch=1,
            grid=(4,),
            in_specs=[whole((1, rows)), whole((1, rows)), whole((NY, NZ, HD)), whole((NY, NZ, HD))]
            + [weights(k, False) for k in range(8)]
            + [weights(k, True) for k in range(8)]
            + [piece] * 8,
            out_specs=[whole((rows // 2, 3 * HD))] * 2,
            scratch_shapes=[pltpu.VMEM((rows, w), jnp.float32) for w in (6 * HD, HD, HD)],
        ),
        out_shape=[jax.ShapeDtypeStruct((rows // 2, 3 * HD), jnp.float32)] * 2,
        compiler_params=pltpu.CompilerParams(vmem_limit_bytes=56 * 2**20),
        cost_estimate=pl.CostEstimate(
            flops=2 * rows * 4096 * 6 * HD, bytes_accessed=11 * 2**20, transcendentals=0
        ),
    )(at, squares, modality, gain, gain_other, *[w] * 8, *[w_other] * 8, *arrays)


def squares_kernel(x_ref, y_ref, early_ref, out_ref, acc):
    step = pl.program_id(0)
    both = jnp.square(x_ref[0].astype(jnp.float32)) + jnp.square(y_ref[0].astype(jnp.float32))

    @pl.when(step == 0)
    def _():
        acc[...] = both

    @pl.when(step > 0)
    def _():
        acc[...] += both

    @pl.when(step == pl.num_programs(0) - 1)
    def _():
        out_ref[...] = early_ref[...] + jnp.sum(acc[...].T, axis=0, keepdims=True)


def last_squares(x, y, early):
    rows = x.shape[1]
    piece = pl.BlockSpec((1, rows, HD), lambda g: (g, 0, 0))
    row = pl.BlockSpec((1, rows), lambda g: (0, 0))
    return pl.pallas_call(
        squares_kernel,
        grid=(x.shape[0],),
        in_specs=[piece, piece, row],
        out_specs=row,
        scratch_shapes=[pltpu.VMEM((rows, HD), jnp.float32)],
        out_shape=jax.ShapeDtypeStruct((1, rows), jnp.float32),
        compiler_params=pltpu.CompilerParams(vmem_limit_bytes=56 * 2**20),
    )(x, y, early)


def finish_kernel(mine_ref, got_ref, gain_ref, cos_ref, sin_ref, q_ref, kv_ref):
    projected = mine_ref[...] + got_ref[...]
    half = HD // 2
    turned = []
    for p in range(2):
        x = projected[:, p * HD : (p + 1) * HD]
        centred = x - jnp.mean(x, axis=1, keepdims=True)
        variance = jnp.mean(centred * centred, axis=1, keepdims=True)
        x = centred * lax.rsqrt(variance + EPS) * gain_ref[p : p + 1, :]
        swapped = jnp.concatenate([x[:, half:], x[:, :half]], axis=1)
        turned.append((x * cos_ref[...] + swapped * sin_ref[...]).astype(jnp.bfloat16))
    q_ref[...] = turned[0]
    kv_ref[0] = turned[1]
    kv_ref[1] = projected[:, 2 * HD :].astype(jnp.bfloat16)


def finish(mine, got, qk_gain, cosines, sines):
    rows = mine.shape[0]
    vmem = pl.BlockSpec(memory_space=pltpu.VMEM)
    return pl.pallas_call(
        finish_kernel,
        in_specs=[vmem] * 5,
        out_specs=[vmem] * 2,
        out_shape=[
            jax.ShapeDtypeStruct((rows, HD), jnp.bfloat16),
            jax.ShapeDtypeStruct((2, rows, HD), jnp.bfloat16),
        ],
    )(mine, got, qk_gain, cosines, sines)


def attention_kernel(base_ref, q_ref, *rest):
    key_refs, out_ref = rest[:-1], rest[-1]
    rows = q_ref.shape[0]
    queries = q_ref[...]
    scale = 1.0 / math.sqrt(HD)
    row = base_ref[0] + lax.broadcasted_iota(jnp.int32, (rows, rows), 0)
    column = lax.broadcasted_iota(jnp.int32, (rows, rows), 1)
    blocks = [(ref, i) for ref in key_refs for i in range(ref.shape[0])]
    scores, seen = [], []
    for n, (ref, i) in enumerate(blocks):
        s = lax.dot_general(queries, ref[i, 0], (((1,), (1,)), ((), ())), preferred_element_type=jnp.float32)
        allowed = column + base_ref[n] <= row
        seen.append(allowed)
        scores.append(jnp.where(allowed, s * scale, MASKED))
    best = scores[0].max(axis=1, keepdims=True)
    for s in scores[1:]:
        best = jnp.maximum(best, s.max(axis=1, keepdims=True))
    total = jnp.zeros((rows, 1), jnp.float32)
    out = jnp.zeros((rows, HD), jnp.float32)
    for n, (ref, i) in enumerate(blocks):
        weights = jnp.where(seen[n], jnp.exp(scores[n] - best), 0.0)
        total += weights.sum(axis=1, keepdims=True)
        out += jnp.dot(weights.astype(jnp.bfloat16), ref[i, 1], preferred_element_type=jnp.float32)
    out_ref[...] = (out / total).astype(jnp.bfloat16)


def attention(bases, queries, keys):
    vmem = pl.BlockSpec(memory_space=pltpu.VMEM)
    return pl.pallas_call(
        attention_kernel,
        in_specs=[pl.BlockSpec(memory_space=pltpu.SMEM)] + [vmem] * (1 + len(keys)),
        out_specs=vmem,
        out_shape=jax.ShapeDtypeStruct(queries.shape, jnp.bfloat16),
        compiler_params=pltpu.CompilerParams(vmem_limit_bytes=40 * 2**20),
        cost_estimate=pl.CostEstimate(flops=2**28, bytes_accessed=2**20, transcendentals=2**19),
    )(bases, queries, *keys)


def out_kernel(at_ref, modality_ref, w_ref, other_ref, heads_ref, out_ref):
    heads = jnp.concatenate([heads_ref[i] for i in range(2 * NY)], axis=1)
    own_row = columns((modality_ref[...] == at_ref[0]).astype(jnp.float32)) > 0
    sections = []
    for ref in (w_ref, other_ref):
        w = jnp.concatenate([ref[x, i, 0] for i in range(2 * NY) for x in range(NX)], axis=0)
        sections.append(jnp.dot(heads, w, preferred_element_type=jnp.float32))
    for i in range(2):
        lanes = slice(i * HD, (i + 1) * HD)
        out_ref[0, :, lanes] = jnp.where(own_row, sections[0][:, lanes], sections[1][:, lanes]).astype(jnp.bfloat16)


def out_part(at, modality, w, w_other, heads):
    rows = heads.shape[1]
    steps = NZ // 2
    whole = lambda shape: pl.BlockSpec(shape, lambda g, at: (0,) * len(shape))
    weights = pl.BlockSpec((NX, 2 * NY, 1, HD // NX, 2 * HD), lambda g, at: (0, 0, g, 0, 0))
    return pl.pallas_call(
        out_kernel,
        grid_spec=pltpu.PrefetchScalarGridSpec(
            num_scalar_prefetch=1,
            grid=(steps,),
            in_specs=[whole((1, rows)), weights, weights, whole(heads.shape)],
            out_specs=pl.BlockSpec((1, rows, 2 * HD), lambda g, at: (g, 0, 0)),
        ),
        out_shape=jax.ShapeDtypeStruct((steps, rows, 2 * HD), jnp.bfloat16),
        compiler_params=pltpu.CompilerParams(vmem_limit_bytes=56 * 2**20),
        cost_estimate=pl.CostEstimate(
            flops=8 * rows * NY * HD * NZ * HD, bytes_accessed=5 * 2**20, transcendentals=0
        ),
    )(at, modality, w, w_other, heads)


def cut_kernel(at_ref, w_ref, out_ref):
    for y in range(NY):
        for odd in range(2):
            for zh in range(NZ // 2):
                for c in range(2):
                    first = ((c * NY + y) * NZ + 2 * zh + odd) * HD
                    out_ref[2 * y + odd, zh, :, c * HD : (c + 1) * HD] = w_ref[:, first : first + HD]


def spread_w_out(at, w_out):
    rows = HD // NX
    shape = (2 * NY, NZ // 2, rows, 2 * HD)
    pieces = pl.pallas_call(
        cut_kernel,
        grid_spec=pltpu.PrefetchScalarGridSpec(
            num_scalar_prefetch=1,
            grid=(1,),
            in_specs=[pl.BlockSpec((rows, w_out.shape[1]), lambda g, at: (at[3], 0))],
            out_specs=pl.BlockSpec(shape, lambda g, at: (0,) * 4),
        ),
        out_shape=jax.ShapeDtypeStruct(shape, jnp.bfloat16),
        cost_estimate=pl.CostEstimate(flops=0, bytes_accessed=2**20, transcendentals=0),
    )(at, w_out)
    lines = lax.all_to_all(pieces, ("y", "zl"), 0, 0)
    return lax.all_gather(lines, "seq", axis=0)


def shards(tokens, modality, norm_gain, w_qkv, qk_gain, w_out):
    row_count = tokens.shape[0]
    half = row_count // 2
    c, y, zh, zl, seq = (lax.axis_index(a) for a in AXES)
    z = 2 * zh + zl
    at = jnp.stack([c, y, z, seq]).astype(jnp.int32)
    modality = modality[None, :]

    w_cols = spread_w_out(at, w_out[0])
    arrays, direct = gather(tokens)
    w_cols_other = take(w_cols, dc=1)

    first = seq * row_count + c * half
    places = first + jnp.arange(half, dtype=jnp.int32)
    rates = 1.0 / 10000.0 ** (jnp.arange(HD // 2, dtype=jnp.float32) * (2.0 / HD))
    angles = places.astype(jnp.float32)[:, None] * rates[None, :]
    cosines, sines = jnp.cos(angles), jnp.sin(angles)
    cosines, sines = jnp.concatenate([cosines, cosines], axis=1), jnp.concatenate([-sines, sines], axis=1)

    w = w_qkv[0].transpose(1, 0, 2).reshape(3, 2, NY, NZ, HD, HD)
    w_other = take(lax.dynamic_slice_in_dim(w, 1 - c, 1, axis=1), dc=1)
    gains = norm_gain.reshape(2, NY * NZ * HD)
    gain_send = lax.dynamic_slice_in_dim(gains, 1 - c, 1, axis=0)
    gain = lax.dynamic_slice_in_dim(gains, c, 1, axis=0).reshape(NY, NZ, HD)

    early = sum(jnp.sum(jnp.square(a.astype(jnp.float32)), axis=(0, 2)) for a in arrays[:6])
    squares = last_squares(arrays[6], arrays[7], early[None, :])
    got = take(jnp.concatenate([squares, gain_send], axis=1), dc=1)
    squares, gain_other = squares + got[:, :row_count], got[:, row_count:].reshape(NY, NZ, HD)
    mine, theirs = project(at, squares, modality, gain, gain_other, w, w_other, arrays)
    queries, own_keys = finish(mine, take(theirs, dc=1), qk_gain, cosines, sines)

    moved = {d: take(own_keys, dx=-d, wrap_x=False) for d in (2, 3, 1)}
    got = jnp.stack([own_keys] + [moved[d] for d in (1, 2, 3)])
    sibling = take(got, dc=1)
    never = 1 << 20
    begin = [jnp.where(seq >= d, (seq - d) * row_count, never) for d in range(NX)]
    bases = jnp.stack([b + c * half for b in begin] + [b + (1 - c) * half for b in begin]).astype(jnp.int32)
    heads_out = attention(bases, queries, [got, sibling])

    heads = lax.all_to_all(jnp.broadcast_to(heads_out[None], (2 * NY, half, HD)), ("y", "zl"), 0, 0)
    own_half = lax.dynamic_slice_in_dim(modality, c * half, half, axis=1)
    partial = out_part(at, own_half, w_cols, w_cols_other, heads)
    spread = lax.all_to_all(partial, "zh", 0, 0)
    summed = jnp.sum(spread.astype(jnp.float32), axis=0).astype(jnp.bfloat16).reshape(half, 2, HD)
    keep = lax.dynamic_index_in_dim(summed, c, axis=1, keepdims=False)
    other = take(lax.dynamic_index_in_dim(summed, 1 - c, axis=1, keepdims=False), dc=1)
    return jnp.where(c == 0, jnp.concatenate([keep, other]), jnp.concatenate([other, keep]))


def solution(mesh):
    mesh = Mesh(mesh.devices.reshape(2, NY, NZ // 2, 2, NX), AXES)
    tp = ("y", "zh", "zl")
    placed = (
        P("seq", ("mod", *tp)),
        P("seq"),
        P("mod", None),
        P("mod", None, None, tp),
        P(None, tp),
        P("mod", tp, None),
    )
    return jax.shard_map(shards, mesh=mesh, in_specs=placed, out_specs=P("seq", ("mod", *tp)), check_vma=False)
```

```python
import math

import jax
import jax.numpy as jnp
from jax import lax
from jax.experimental import pallas as pl
from jax.experimental.pallas import tpu as pltpu
from jax.sharding import Mesh
from jax.sharding import PartitionSpec as P

HD = 128
EPS = 1e-05
MASKED = -1e30
NY = 4
NZ = 8
NX = 4
AXES = ("mod", "y", "zh", "zl", "seq")


def pairs(moves, wrap_x=True):
    out = []
    for c in range(2):
        if moves[c] is None:
            continue
        dc, dy, dz, dx = moves[c]
        for y in range(NY):
            for z in range(NZ):
                for x in range(NX):
                    if not wrap_x and not 0 <= x + dx < NX:
                        continue
                    from_z = z ^ 1 if dz == "pair" else (z + dz) % NZ
                    source = (((c + dc) % 2 * NY + (y + dy) % NY) * NZ + from_z) * NX + (x + dx) % NX
                    out.append((source, ((c * NY + y) * NZ + z) * NX + x))
    return out


def take(x, dc=0, dy=0, dz=0, dx=0, wrap_x=True):
    return lax.ppermute(x, AXES, pairs([(dc, dy, dz, dx)] * 2, wrap_x))


def take_by_core(x, on_y, on_z):
    return lax.ppermute(x, AXES, pairs([m and (0, *m, 0) for m in (on_y, on_z)]))


def gather(rows):
    k1 = take_by_core(rows, (1, 0), (0, 2))
    k2 = take_by_core(rows, (-1, 0), (0, -2))
    k3 = take_by_core(rows, (2, 0), (0, 4))
    g0 = jnp.stack([rows, k1, k2, k3])
    g1 = take_by_core(g0, (0, 1), (0, -1))
    x2 = take_by_core(g0, (0, -1), (-1, 0))
    x1 = take_by_core(g1, (0, 1), (1, 0))
    x4 = take_by_core(x2, (0, -1), (-1, 0))
    x3 = take_by_core(x1, (0, 1), (1, 0))
    x6 = take_by_core(x4, (0, -1), (-1, 0))
    x5 = take_by_core(x3, (0, 1), (1, 0))
    return [g0, g1, x1, x2, x3, x4, x5, x6], [k1, k2, k3]


OFFSETS = ((0, 0, 0), (1, 0, 7), (2, 1, 7), (7, 3, 0), (3, 2, 7), (6, 2, 0), (4, 3, 7), (5, 1, 0))


def place(at, k, step):
    turn = step ^ (step >> 1)
    dz0, dy1, dz1 = OFFSETS[k]
    dy = jnp.where(at[0] == 0, turn, dy1)
    dz = jnp.where(at[0] == 0, dz0, 2 * turn + dz1)
    return (at[1] + dy) & (NY - 1), (at[2] + dz) & (NZ - 1)


def columns(row):
    return jnp.broadcast_to(row, (HD, row.shape[1])).T


def qkv_kernel(ks, last, at_ref, squares_ref, modality_ref, gain_ref, gain_other_ref, *rest):
    n = len(ks)
    own_ws, other_ws, pieces = rest[:n], rest[n : 2 * n], rest[2 * n : 3 * n]
    rest = rest[3 * n :]
    if last:
        before_ref, mine_ref, theirs_ref, acc, inv, own = rest
    else:
        acc, inv, own = rest
    step = pl.program_id(0)

    @pl.when(step == 0)
    def _():
        inv[...] = columns(lax.rsqrt(squares_ref[...] / (2 * NY * NZ * HD) + EPS))
        own[...] = columns((modality_ref[...] == at_ref[0]).astype(jnp.float32))

    inverse = inv[...]
    own_row = own[...] > 0
    normed, right = [], []
    for i, piece in enumerate(pieces):
        yi, zi = place(at_ref, ks[i], step)
        gain = jnp.where(own_row, gain_ref[yi, pl.ds(zi, 1), :], gain_other_ref[yi, pl.ds(zi, 1), :])
        normed.append((piece[0].astype(jnp.float32) * inverse * gain).astype(jnp.bfloat16))
        right.append(jnp.concatenate([w[p, 0, 0, 0] for w in (own_ws[i], other_ws[i]) for p in range(3)], axis=1))
    part = jnp.dot(
        jnp.concatenate(normed, axis=1), jnp.concatenate(right, axis=0), preferred_element_type=jnp.float32
    )

    @pl.when(step == 0)
    def _():
        acc[...] = part + before_ref[...] if last else part

    @pl.when(step > 0)
    def _():
        acc[...] += part

    if last:

        @pl.when(step == pl.num_programs(0) - 1)
        def _():
            half = acc.shape[0] // 2
            for ref, first in ((mine_ref, at_ref[0] * half), (theirs_ref, (1 - at_ref[0]) * half)):
                rows = pl.ds(pl.multiple_of(first, half), half)
                own_here = own[rows, :] > 0
                for p in range(3):
                    low, high = acc[rows, p * HD : (p + 1) * HD], acc[rows, (3 + p) * HD : (4 + p) * HD]
                    ref[:, p * HD : (p + 1) * HD] = jnp.where(own_here, low, high)


def project(ks, before, at, squares, modality, gain, gain_other, w, w_other, arrays):
    last = before is not None
    rows, n = arrays[0].shape[1], len(ks)
    block = (3, 1, 1, 1, HD, HD)
    whole = lambda shape: pl.BlockSpec(shape, lambda g, at: (0,) * len(shape))
    piece = pl.BlockSpec((1, rows, HD), lambda g, at: (g, 0, 0))
    weights = lambda k, other: pl.BlockSpec(
        block, lambda g, at: (0, 0 if other else at[0], *place(at, k, g), 0, 0)
    )
    wide = (rows, 6 * HD)
    narrow = jax.ShapeDtypeStruct((rows // 2, 3 * HD), jnp.float32)
    vectors = [pltpu.VMEM((rows, HD), jnp.float32)] * 2

    def body(*refs):
        qkv_kernel(ks, last, *refs)

    return pl.pallas_call(
        body,
        grid_spec=pltpu.PrefetchScalarGridSpec(
            num_scalar_prefetch=1,
            grid=(4,),
            in_specs=[whole((1, rows)), whole((1, rows)), whole((NY, NZ, HD)), whole((NY, NZ, HD))]
            + [weights(k, False) for k in ks]
            + [weights(k, True) for k in ks]
            + [piece] * n
            + [whole(wide)] * last,
            out_specs=[whole(narrow.shape)] * 2 if last else whole(wide),
            scratch_shapes=[pltpu.VMEM(wide, jnp.float32)] * last + vectors,
        ),
        out_shape=[narrow] * 2 if last else jax.ShapeDtypeStruct(wide, jnp.float32),
        compiler_params=pltpu.CompilerParams(vmem_limit_bytes=56 * 2**20),
        cost_estimate=pl.CostEstimate(
            flops=2 * rows * n * 4 * HD * 6 * HD, bytes_accessed=n * 3 * 2**19, transcendentals=0
        ),
    )(at, squares, modality, gain, gain_other, *[w] * n, *[w_other] * n, *[arrays[k] for k in ks], *[before] * last)


def finish_kernel(mine_ref, got_ref, gain_ref, cos_ref, sin_ref, q_ref, kv_ref):
    projected = mine_ref[...] + got_ref[...]
    half = HD // 2
    turned = []
    for p in range(2):
        x = projected[:, p * HD : (p + 1) * HD]
        centred = x - jnp.mean(x, axis=1, keepdims=True)
        variance = jnp.mean(centred * centred, axis=1, keepdims=True)
        x = centred * lax.rsqrt(variance + EPS) * gain_ref[p : p + 1, :]
        swapped = jnp.concatenate([x[:, half:], x[:, :half]], axis=1)
        turned.append((x * cos_ref[...] + swapped * sin_ref[...]).astype(jnp.bfloat16))
    q_ref[...] = turned[0]
    kv_ref[0] = turned[1]
    kv_ref[1] = projected[:, 2 * HD :].astype(jnp.bfloat16)


def finish(mine, got, qk_gain, cosines, sines):
    rows = mine.shape[0]
    vmem = pl.BlockSpec(memory_space=pltpu.VMEM)
    return pl.pallas_call(
        finish_kernel,
        in_specs=[vmem] * 5,
        out_specs=[vmem] * 2,
        out_shape=[
            jax.ShapeDtypeStruct((rows, HD), jnp.bfloat16),
            jax.ShapeDtypeStruct((2, rows, HD), jnp.bfloat16),
        ],
    )(mine, got, qk_gain, cosines, sines)


def attention_kernel(base_ref, q_ref, *rest):
    key_refs, out_ref = rest[:-1], rest[-1]
    rows = q_ref.shape[0]
    queries = q_ref[...]
    scale = 1.0 / math.sqrt(HD)
    row = base_ref[0] + lax.broadcasted_iota(jnp.int32, (rows, rows), 0)
    column = lax.broadcasted_iota(jnp.int32, (rows, rows), 1)
    blocks = [(ref, i) for ref in key_refs for i in range(ref.shape[0])]
    scores, seen = [], []
    for n, (ref, i) in enumerate(blocks):
        s = lax.dot_general(queries, ref[i, 0], (((1,), (1,)), ((), ())), preferred_element_type=jnp.float32)
        allowed = column + base_ref[n] <= row
        seen.append(allowed)
        scores.append(jnp.where(allowed, s * scale, MASKED))
    best = scores[0].max(axis=1, keepdims=True)
    for s in scores[1:]:
        best = jnp.maximum(best, s.max(axis=1, keepdims=True))
    total = jnp.zeros((rows, 1), jnp.float32)
    out = jnp.zeros((rows, HD), jnp.float32)
    for n, (ref, i) in enumerate(blocks):
        weights = jnp.where(seen[n], jnp.exp(scores[n] - best), 0.0)
        total += weights.sum(axis=1, keepdims=True)
        out += jnp.dot(weights.astype(jnp.bfloat16), ref[i, 1], preferred_element_type=jnp.float32)
    result = (out / total).astype(jnp.bfloat16)
    for i in range(out_ref.shape[0]):
        out_ref[i] = result


def attention(bases, queries, keys):
    vmem = pl.BlockSpec(memory_space=pltpu.VMEM)
    return pl.pallas_call(
        attention_kernel,
        in_specs=[pl.BlockSpec(memory_space=pltpu.SMEM)] + [vmem] * (1 + len(keys)),
        out_specs=vmem,
        out_shape=jax.ShapeDtypeStruct((2 * NY, *queries.shape), jnp.bfloat16),
        compiler_params=pltpu.CompilerParams(vmem_limit_bytes=40 * 2**20),
        cost_estimate=pl.CostEstimate(flops=2**28, bytes_accessed=2**20, transcendentals=2**19),
    )(bases, queries, *keys)


def out_kernel(at_ref, modality_ref, w_ref, other_ref, heads_ref, out_ref):
    heads = jnp.concatenate([heads_ref[i] for i in range(2 * NY)], axis=1)
    own_row = columns((modality_ref[...] == at_ref[0]).astype(jnp.float32)) > 0
    sections = []
    for ref in (w_ref, other_ref):
        w = jnp.concatenate([ref[x, i, 0] for i in range(2 * NY) for x in range(NX)], axis=0)
        sections.append(jnp.dot(heads, w, preferred_element_type=jnp.float32))
    for i in range(2):
        lanes = slice(i * HD, (i + 1) * HD)
        out_ref[0, :, lanes] = jnp.where(own_row, sections[0][:, lanes], sections[1][:, lanes]).astype(jnp.bfloat16)


def out_part(at, modality, w, w_other, heads):
    rows = heads.shape[1]
    steps = NZ // 2
    whole = lambda shape: pl.BlockSpec(shape, lambda g, at: (0,) * len(shape))
    weights = pl.BlockSpec((NX, 2 * NY, 1, HD // NX, 2 * HD), lambda g, at: (0, 0, g, 0, 0))
    return pl.pallas_call(
        out_kernel,
        grid_spec=pltpu.PrefetchScalarGridSpec(
            num_scalar_prefetch=1,
            grid=(steps,),
            in_specs=[whole((1, rows)), weights, weights, whole(heads.shape)],
            out_specs=pl.BlockSpec((1, rows, 2 * HD), lambda g, at: (g, 0, 0)),
        ),
        out_shape=jax.ShapeDtypeStruct((steps, rows, 2 * HD), jnp.bfloat16),
        compiler_params=pltpu.CompilerParams(vmem_limit_bytes=56 * 2**20),
        cost_estimate=pl.CostEstimate(
            flops=8 * rows * NY * HD * NZ * HD, bytes_accessed=5 * 2**20, transcendentals=0
        ),
    )(at, modality, w, w_other, heads)


def cut_kernel(at_ref, w_ref, out_ref):
    for y in range(NY):
        for odd in range(2):
            for zh in range(NZ // 2):
                for c in range(2):
                    first = ((c * NY + y) * NZ + 2 * zh + odd) * HD
                    out_ref[2 * y + odd, zh, :, c * HD : (c + 1) * HD] = w_ref[:, first : first + HD]


def spread_w_out(at, w_out, *ahead):
    rows = HD // NX
    shape = (2 * NY, NZ // 2, rows, 2 * HD)
    pieces = pl.pallas_call(
        cut_kernel,
        grid_spec=pltpu.PrefetchScalarGridSpec(
            num_scalar_prefetch=1,
            grid=(1,),
            in_specs=[pl.BlockSpec((rows, w_out.shape[1]), lambda g, at: (at[3], 0))],
            out_specs=pl.BlockSpec(shape, lambda g, at: (0,) * 4),
        ),
        out_shape=jax.ShapeDtypeStruct(shape, jnp.bfloat16),
        cost_estimate=pl.CostEstimate(flops=0, bytes_accessed=2**20, transcendentals=0),
    )(at, w_out)
    lines = lax.all_to_all(pieces, ("y", "zl"), 0, 0)
    lines, *_ = lax.optimization_barrier((lines, *ahead))
    return lax.all_gather(lines, "seq", axis=0)


def share_vectors(tokens, norm_gain, at_tp):
    devices, rows = 2 * NY * NZ, tokens.shape[0] // HD
    squares = jnp.sum(jnp.square(tokens.astype(jnp.float32)), axis=1).reshape(1, rows, HD)
    own = lax.dynamic_index_in_dim(norm_gain.reshape(2, NY * NZ, HD), at_tp, axis=1, keepdims=True)
    own = jnp.broadcast_to(own[:, :, None], (2, NY * NZ, 1, HD)).reshape(devices, 1, HD)
    sent = jnp.concatenate([jnp.broadcast_to(squares, (devices, rows, HD)), own], axis=1)
    sent = jnp.pad(sent, ((0, 0), (0, 7 - rows), (0, 0)))
    got = lax.all_to_all(sent, AXES[:4], 0, 0)
    return jnp.sum(got[:, :rows], axis=0).reshape(1, rows * HD), got[:, rows].reshape(2, NY, NZ, HD)


def shards(tokens, modality, norm_gain, w_qkv, qk_gain, w_out):
    row_count = tokens.shape[0]
    half = row_count // 2
    c, y, zh, zl, seq = (lax.axis_index(a) for a in AXES)
    z = 2 * zh + zl
    at = jnp.stack([c, y, z, seq]).astype(jnp.int32)
    modality = modality[None, :]

    arrays, direct = gather(tokens)
    squares, gains = share_vectors(tokens, norm_gain, y * NZ + z)
    gain, gain_other = (lax.dynamic_index_in_dim(gains, i, axis=0, keepdims=False) for i in (c, 1 - c))
    w_qkv, w_out, squares, *_ = lax.optimization_barrier((w_qkv, w_out, squares, *direct))
    w_cols = spread_w_out(at, w_out[0], arrays[1], arrays[3])
    w_cols_other = take(w_cols, dc=1)

    first = seq * row_count + c * half
    places = first + jnp.arange(half, dtype=jnp.int32)
    rates = 1.0 / 10000.0 ** (jnp.arange(HD // 2, dtype=jnp.float32) * (2.0 / HD))
    angles = places.astype(jnp.float32)[:, None] * rates[None, :]
    cosines, sines = jnp.cos(angles), jnp.sin(angles)
    cosines, sines = jnp.concatenate([cosines, cosines], axis=1), jnp.concatenate([-sines, sines], axis=1)

    w = w_qkv[0].transpose(1, 0, 2).reshape(3, 2, NY, NZ, HD, HD)
    w_other = take(lax.dynamic_slice_in_dim(w, 1 - c, 1, axis=1), dc=1)

    common = (at, squares, modality, gain, gain_other, w, w_other, arrays)
    before = project(range(6), None, *common)
    mine, theirs = project(range(6, 8), before, *common)
    queries, own_keys = finish(mine, take(theirs, dc=1), qk_gain, cosines, sines)

    moved = {d: take(own_keys, dx=-d, wrap_x=False) for d in (2, 3, 1)}
    got = jnp.stack([own_keys] + [moved[d] for d in (1, 2, 3)])
    sibling = take(got, dc=1)
    never = 1 << 20
    begin = [jnp.where(seq >= d, (seq - d) * row_count, never) for d in range(NX)]
    bases = jnp.stack([b + c * half for b in begin] + [b + (1 - c) * half for b in begin]).astype(jnp.int32)
    heads_out = attention(bases, queries, [got, sibling])

    heads = lax.all_to_all(heads_out, ("y", "zl"), 0, 0)
    own_half = lax.dynamic_slice_in_dim(modality, c * half, half, axis=1)
    partial = out_part(at, own_half, w_cols, w_cols_other, heads)
    spread = lax.all_to_all(partial, "zh", 0, 0)
    summed = jnp.sum(spread.astype(jnp.float32), axis=0).astype(jnp.bfloat16).reshape(half, 2, HD)
    keep = lax.dynamic_index_in_dim(summed, c, axis=1, keepdims=False)
    other = take(lax.dynamic_index_in_dim(summed, 1 - c, axis=1, keepdims=False), dc=1)
    return jnp.where(c == 0, jnp.concatenate([keep, other]), jnp.concatenate([other, keep]))


def solution(mesh):
    mesh = Mesh(mesh.devices.reshape(2, NY, NZ // 2, 2, NX), AXES)
    tp = ("y", "zh", "zl")
    placed = (
        P("seq", ("mod", *tp)),
        P("seq"),
        P("mod", None),
        P("mod", None, None, tp),
        P(None, tp),
        P("mod", tp, None),
    )
    return jax.shard_map(shards, mesh=mesh, in_specs=placed, out_specs=P("seq", ("mod", *tp)), check_vma=False)
```

```python
import math

import jax
import jax.numpy as jnp
from jax import lax
from jax.experimental import pallas as pl
from jax.experimental.pallas import tpu as pltpu
from jax.sharding import Mesh
from jax.sharding import PartitionSpec as P

HD = 128
EPS = 1e-05
MASKED = -1e30
NY = 4
NZ = 8
NX = 4
AXES = ("mod", "y", "zh", "zl", "seq")


def pairs(moves, wrap_x=True):
    out = []
    for c in range(2):
        if moves[c] is None:
            continue
        dc, dy, dz, dx = moves[c]
        for y in range(NY):
            for z in range(NZ):
                for x in range(NX):
                    if not wrap_x and not 0 <= x + dx < NX:
                        continue
                    from_z = z ^ 1 if dz == "pair" else (z + dz) % NZ
                    source = (((c + dc) % 2 * NY + (y + dy) % NY) * NZ + from_z) * NX + (x + dx) % NX
                    out.append((source, ((c * NY + y) * NZ + z) * NX + x))
    return out


def take(x, dc=0, dy=0, dz=0, dx=0, wrap_x=True):
    return lax.ppermute(x, AXES, pairs([(dc, dy, dz, dx)] * 2, wrap_x))


def take_by_core(x, on_y, on_z):
    return lax.ppermute(x, AXES, pairs([m and (0, *m, 0) for m in (on_y, on_z)]))


def gather(rows):
    k1 = take_by_core(rows, (1, 0), (0, 2))
    k2 = take_by_core(rows, (-1, 0), (0, -2))
    k3 = take_by_core(rows, (2, 0), (0, 4))
    g0 = jnp.stack([rows, k1, k2, k3])
    g1 = take_by_core(g0, (0, 1), (0, -1))
    x2 = take_by_core(g0, (0, -1), (-1, 0))
    x1 = take_by_core(g1, (0, 1), (1, 0))
    x4 = take_by_core(x2, (0, -1), (-1, 0))
    x3 = take_by_core(x1, (0, 1), (1, 0))
    x6 = take_by_core(x4, (0, -1), (-1, 0))
    x5 = take_by_core(x3, (0, 1), (1, 0))
    return [g0, g1, x1, x2, x3, x4, x5, x6], [k1, k2, k3]


OFFSETS = ((0, 0, 0), (1, 0, 7), (2, 1, 7), (7, 3, 0), (3, 2, 7), (6, 2, 0), (4, 3, 7), (5, 1, 0))


def place(at, k, step):
    turn = step ^ (step >> 1)
    dz0, dy1, dz1 = OFFSETS[k]
    dy = jnp.where(at[0] == 0, turn, dy1)
    dz = jnp.where(at[0] == 0, dz0, 2 * turn + dz1)
    return (at[1] + dy) & (NY - 1), (at[2] + dz) & (NZ - 1)


def columns(row):
    return jnp.broadcast_to(row, (HD, row.shape[1])).T


def qkv_kernel(at_ref, row_ref, got_ref, modality_ref, gain_ref, *rest):
    own_ws, other_ws, pieces = rest[:8], rest[8:16], rest[16:24]
    mine_ref, theirs_ref, acc, inv, own = rest[24:]
    step = pl.program_id(0)

    @pl.when(step == 0)
    def _():
        count = inv.shape[0]
        squares = row_ref[:, :count] + got_ref[:, :count]
        inv[...] = columns(lax.rsqrt(squares / (2 * NY * NZ * HD) + EPS))
        own[...] = columns((modality_ref[...] == at_ref[0]).astype(jnp.float32))

    inverse = inv[...]
    own_row = own[...] > 0
    normed, right = [], []
    for k, piece in enumerate(pieces):
        yi, zi = place(at_ref, k, step)
        first = pl.multiple_of(inv.shape[0] + (yi * NZ + zi) * HD, HD)
        gain = jnp.where(own_row, gain_ref[yi, pl.ds(zi, 1), :], got_ref[:, pl.ds(first, HD)])
        normed.append((piece[0].astype(jnp.float32) * inverse * gain).astype(jnp.bfloat16))
        right.append(jnp.concatenate([w[p, 0, 0, 0] for w in (own_ws[k], other_ws[k]) for p in range(3)], axis=1))
    part = jnp.dot(
        jnp.concatenate(normed, axis=1), jnp.concatenate(right, axis=0), preferred_element_type=jnp.float32
    )

    @pl.when(step == 0)
    def _():
        acc[...] = part

    @pl.when(step > 0)
    def _():
        acc[...] += part

    @pl.when(step == pl.num_programs(0) - 1)
    def _():
        half = acc.shape[0] // 2
        for ref, first in ((mine_ref, at_ref[0] * half), (theirs_ref, (1 - at_ref[0]) * half)):
            rows = pl.ds(pl.multiple_of(first, half), half)
            own_here = own[rows, :] > 0
            for p in range(3):
                low, high = acc[rows, p * HD : (p + 1) * HD], acc[rows, (3 + p) * HD : (4 + p) * HD]
                ref[:, p * HD : (p + 1) * HD] = jnp.where(own_here, low, high)


def project(at, row, got, modality, gain, w, w_other, arrays):
    rows = arrays[0].shape[1]
    block = (3, 1, 1, 1, HD, HD)
    whole = lambda shape: pl.BlockSpec(shape, lambda g, at: (0,) * len(shape))
    piece = pl.BlockSpec((1, rows, HD), lambda g, at: (g, 0, 0))
    weights = lambda k, other: pl.BlockSpec(
        block, lambda g, at: (0, 0 if other else at[0], *place(at, k, g), 0, 0)
    )
    return pl.pallas_call(
        qkv_kernel,
        grid_spec=pltpu.PrefetchScalarGridSpec(
            num_scalar_prefetch=1,
            grid=(4,),
            in_specs=[whole(row.shape), whole(got.shape), whole((1, rows)), whole((NY, NZ, HD))]
            + [weights(k, False) for k in range(8)]
            + [weights(k, True) for k in range(8)]
            + [piece] * 8,
            out_specs=[whole((rows // 2, 3 * HD))] * 2,
            scratch_shapes=[pltpu.VMEM((rows, w), jnp.float32) for w in (6 * HD, HD, HD)],
        ),
        out_shape=[jax.ShapeDtypeStruct((rows // 2, 3 * HD), jnp.float32)] * 2,
        compiler_params=pltpu.CompilerParams(vmem_limit_bytes=61 * 2**20),
        cost_estimate=pl.CostEstimate(
            flops=2 * rows * 4096 * 6 * HD, bytes_accessed=11 * 2**20, transcendentals=0
        ),
    )(at, row, got, modality, gain, *[w] * 8, *[w_other] * 8, *arrays)


def finish_kernel(mine_ref, got_ref, gain_ref, cos_ref, sin_ref, q_ref, kv_ref):
    projected = mine_ref[...] + got_ref[...]
    half = HD // 2
    turned = []
    for p in range(2):
        x = projected[:, p * HD : (p + 1) * HD]
        centred = x - jnp.mean(x, axis=1, keepdims=True)
        variance = jnp.mean(centred * centred, axis=1, keepdims=True)
        x = centred * lax.rsqrt(variance + EPS) * gain_ref[p : p + 1, :]
        swapped = jnp.concatenate([x[:, half:], x[:, :half]], axis=1)
        turned.append((x * cos_ref[...] + swapped * sin_ref[...]).astype(jnp.bfloat16))
    q_ref[...] = turned[0]
    kv_ref[0] = turned[1]
    kv_ref[1] = projected[:, 2 * HD :].astype(jnp.bfloat16)


def finish(mine, got, qk_gain, cosines, sines):
    rows = mine.shape[0]
    vmem = pl.BlockSpec(memory_space=pltpu.VMEM)
    return pl.pallas_call(
        finish_kernel,
        in_specs=[vmem] * 5,
        out_specs=[vmem] * 2,
        out_shape=[
            jax.ShapeDtypeStruct((rows, HD), jnp.bfloat16),
            jax.ShapeDtypeStruct((2, rows, HD), jnp.bfloat16),
        ],
    )(mine, got, qk_gain, cosines, sines)


def attention_kernel(base_ref, q_ref, *rest):
    key_refs, out_ref = rest[:-1], rest[-1]
    rows = q_ref.shape[0]
    queries = q_ref[...]
    scale = 1.0 / math.sqrt(HD)
    row = base_ref[0] + lax.broadcasted_iota(jnp.int32, (rows, rows), 0)
    column = lax.broadcasted_iota(jnp.int32, (rows, rows), 1)
    blocks = [(ref, i) for ref in key_refs for i in range(ref.shape[0])]
    scores, seen = [], []
    for n, (ref, i) in enumerate(blocks):
        s = lax.dot_general(queries, ref[i, 0], (((1,), (1,)), ((), ())), preferred_element_type=jnp.float32)
        allowed = column + base_ref[n] <= row
        seen.append(allowed)
        scores.append(jnp.where(allowed, s * scale, MASKED))
    best = scores[0].max(axis=1, keepdims=True)
    for s in scores[1:]:
        best = jnp.maximum(best, s.max(axis=1, keepdims=True))
    total = jnp.zeros((rows, 1), jnp.float32)
    out = jnp.zeros((rows, HD), jnp.float32)
    for n, (ref, i) in enumerate(blocks):
        weights = jnp.where(seen[n], jnp.exp(scores[n] - best), 0.0)
        total += weights.sum(axis=1, keepdims=True)
        out += jnp.dot(weights.astype(jnp.bfloat16), ref[i, 1], preferred_element_type=jnp.float32)
    result = (out / total).astype(jnp.bfloat16)
    for i in range(out_ref.shape[0]):
        out_ref[i] = result


def attention(bases, queries, keys):
    vmem = pl.BlockSpec(memory_space=pltpu.VMEM)
    return pl.pallas_call(
        attention_kernel,
        in_specs=[pl.BlockSpec(memory_space=pltpu.SMEM)] + [vmem] * (1 + len(keys)),
        out_specs=vmem,
        out_shape=jax.ShapeDtypeStruct((2 * NY, *queries.shape), jnp.bfloat16),
        compiler_params=pltpu.CompilerParams(vmem_limit_bytes=40 * 2**20),
        cost_estimate=pl.CostEstimate(flops=2**28, bytes_accessed=2**20, transcendentals=2**19),
    )(bases, queries, *keys)


def out_kernel(at_ref, modality_ref, w_ref, other_ref, heads_ref, out_ref):
    heads = jnp.concatenate([heads_ref[i] for i in range(2 * NY)], axis=1)
    own_row = columns((modality_ref[...] == at_ref[0]).astype(jnp.float32)) > 0
    sections = []
    for ref in (w_ref, other_ref):
        w = jnp.concatenate([ref[x, i, 0] for i in range(2 * NY) for x in range(NX)], axis=0)
        sections.append(jnp.dot(heads, w, preferred_element_type=jnp.float32))
    for i in range(2):
        lanes = slice(i * HD, (i + 1) * HD)
        out_ref[0, :, lanes] = jnp.where(own_row, sections[0][:, lanes], sections[1][:, lanes]).astype(jnp.bfloat16)


def out_part(at, modality, w, w_other, heads):
    rows = heads.shape[1]
    steps = NZ // 2
    whole = lambda shape: pl.BlockSpec(shape, lambda g, at: (0,) * len(shape))
    weights = pl.BlockSpec((NX, 2 * NY, 1, HD // NX, 2 * HD), lambda g, at: (0, 0, g, 0, 0))
    return pl.pallas_call(
        out_kernel,
        grid_spec=pltpu.PrefetchScalarGridSpec(
            num_scalar_prefetch=1,
            grid=(steps,),
            in_specs=[whole((1, rows)), weights, weights, whole(heads.shape)],
            out_specs=pl.BlockSpec((1, rows, 2 * HD), lambda g, at: (g, 0, 0)),
        ),
        out_shape=jax.ShapeDtypeStruct((steps, rows, 2 * HD), jnp.bfloat16),
        compiler_params=pltpu.CompilerParams(vmem_limit_bytes=61 * 2**20),
        cost_estimate=pl.CostEstimate(
            flops=8 * rows * NY * HD * NZ * HD, bytes_accessed=5 * 2**20, transcendentals=0
        ),
    )(at, modality, w, w_other, heads)


def cut_kernel(at_ref, w_ref, out_ref):
    for y in range(NY):
        for odd in range(2):
            for zh in range(NZ // 2):
                for c in range(2):
                    first = ((c * NY + y) * NZ + 2 * zh + odd) * HD
                    out_ref[2 * y + odd, zh, :, c * HD : (c + 1) * HD] = w_ref[:, first : first + HD]


def spread_w_out(at, w_out, *ahead):
    rows = HD // NX
    shape = (2 * NY, NZ // 2, rows, 2 * HD)
    pieces = pl.pallas_call(
        cut_kernel,
        grid_spec=pltpu.PrefetchScalarGridSpec(
            num_scalar_prefetch=1,
            grid=(1,),
            in_specs=[pl.BlockSpec((rows, w_out.shape[1]), lambda g, at: (at[3], 0))],
            out_specs=pl.BlockSpec(shape, lambda g, at: (0,) * 4),
        ),
        out_shape=jax.ShapeDtypeStruct(shape, jnp.bfloat16),
        cost_estimate=pl.CostEstimate(flops=0, bytes_accessed=2**20, transcendentals=0),
    )(at, w_out)
    lines = lax.all_to_all(pieces, ("y", "zl"), 0, 0)
    lines, *_ = lax.optimization_barrier((lines, *ahead))
    return lax.all_gather(lines, "seq", axis=0)


def shards(tokens, modality, norm_gain, w_qkv, qk_gain, w_out):
    row_count = tokens.shape[0]
    half = row_count // 2
    c, y, zh, zl, seq = (lax.axis_index(a) for a in AXES)
    z = 2 * zh + zl
    at = jnp.stack([c, y, z, seq]).astype(jnp.int32)
    modality = modality[None, :]

    arrays, direct = gather(tokens)
    w_out, *_ = lax.optimization_barrier((w_out, *direct))
    w_cols = spread_w_out(at, w_out[0], arrays[2], arrays[5])
    w_cols_other = take(w_cols, dc=1)

    first = seq * row_count + c * half
    places = first + jnp.arange(half, dtype=jnp.int32)
    rates = 1.0 / 10000.0 ** (jnp.arange(HD // 2, dtype=jnp.float32) * (2.0 / HD))
    angles = places.astype(jnp.float32)[:, None] * rates[None, :]
    cosines, sines = jnp.cos(angles), jnp.sin(angles)
    cosines, sines = jnp.concatenate([cosines, cosines], axis=1), jnp.concatenate([-sines, sines], axis=1)

    w = w_qkv[0].transpose(1, 0, 2).reshape(3, 2, NY, NZ, HD, HD)
    w_other = take(lax.dynamic_slice_in_dim(w, 1 - c, 1, axis=1), dc=1)
    gains = norm_gain.reshape(2, NY * NZ * HD)
    gain_send = lax.dynamic_slice_in_dim(gains, 1 - c, 1, axis=0)
    gain = lax.dynamic_slice_in_dim(gains, c, 1, axis=0).reshape(NY, NZ, HD)

    squares = sum(jnp.sum(jnp.square(a.astype(jnp.float32)), axis=(0, 2)) for a in arrays)
    row = jnp.concatenate([squares[None, :], gain_send], axis=1)
    mine, theirs = project(at, row, take(row, dc=1), modality, gain, w, w_other, arrays)
    queries, own_keys = finish(mine, take(theirs, dc=1), qk_gain, cosines, sines)

    moved = {d: take(own_keys, dx=-d, wrap_x=False) for d in (2, 3, 1)}
    got = jnp.stack([own_keys] + [moved[d] for d in (1, 2, 3)])
    sibling = take(got, dc=1)
    never = 1 << 20
    begin = [jnp.where(seq >= d, (seq - d) * row_count, never) for d in range(NX)]
    bases = jnp.stack([b + c * half for b in begin] + [b + (1 - c) * half for b in begin]).astype(jnp.int32)
    heads_out = attention(bases, queries, [got, sibling])

    heads = lax.all_to_all(heads_out, ("y", "zl"), 0, 0)
    own_half = lax.dynamic_slice_in_dim(modality, c * half, half, axis=1)
    partial = out_part(at, own_half, w_cols, w_cols_other, heads)
    spread = lax.all_to_all(partial, "zh", 0, 0)
    summed = jnp.sum(spread.astype(jnp.float32), axis=0).astype(jnp.bfloat16).reshape(half, 2, HD)
    keep = lax.dynamic_index_in_dim(summed, c, axis=1, keepdims=False)
    other = take(lax.dynamic_index_in_dim(summed, 1 - c, axis=1, keepdims=False), dc=1)
    return jnp.where(c == 0, jnp.concatenate([keep, other]), jnp.concatenate([other, keep]))


def solution(mesh):
    mesh = Mesh(mesh.devices.reshape(2, NY, NZ // 2, 2, NX), AXES)
    tp = ("y", "zh", "zl")
    placed = (
        P("seq", ("mod", *tp)),
        P("seq"),
        P("mod", None),
        P("mod", None, None, tp),
        P(None, tp),
        P("mod", tp, None),
    )
    return jax.shard_map(shards, mesh=mesh, in_specs=placed, out_specs=P("seq", ("mod", *tp)), check_vma=False)
```

```python
import math

import jax
import jax.numpy as jnp
import numpy as np
from jax import lax
from jax.experimental import pallas as pl
from jax.experimental.pallas import tpu as pltpu
from jax.sharding import Mesh
from jax.sharding import PartitionSpec as P

HD = 128
EPS = 1e-05
MASKED = -1e30
NY = 4
NZ = 8
NX = 4
AXES = ("mod", "y", "zh", "zl", "seq")


def pairs(moves, wrap_x=True):
    out = []
    for c in range(2):
        if moves[c] is None:
            continue
        dc, dy, dz, dx = moves[c]
        for y in range(NY):
            for z in range(NZ):
                for x in range(NX):
                    if not wrap_x and not 0 <= x + dx < NX:
                        continue
                    from_z = z ^ 1 if dz == "pair" else (z + dz) % NZ
                    source = (((c + dc) % 2 * NY + (y + dy) % NY) * NZ + from_z) * NX + (x + dx) % NX
                    out.append((source, ((c * NY + y) * NZ + z) * NX + x))
    return out


def take(x, dc=0, dy=0, dz=0, dx=0, wrap_x=True):
    return lax.ppermute(x, AXES, pairs([(dc, dy, dz, dx)] * 2, wrap_x))


def take_by_core(x, on_y, on_z):
    return lax.ppermute(x, AXES, pairs([m and (0, *m, 0) for m in (on_y, on_z)]))


def gather(rows, beside):
    k1 = take_by_core(rows, (1, 0), (0, 2))
    k2 = take_by_core(rows, (-1, 0), (0, -2))
    k3 = take_by_core(rows, (2, 0), (0, 4))
    k1, k2, k3, beside = lax.optimization_barrier((k1, k2, k3, beside))
    g0 = jnp.stack([rows, k1, k2, k3])
    g1 = take_by_core(g0, (0, 1), (0, -1))
    x2 = take_by_core(g0, (0, -1), (-1, 0))
    x1 = take_by_core(g1, (0, 1), (1, 0))
    x4 = take_by_core(x2, (0, -1), (-1, 0))
    x3 = take_by_core(x1, (0, 1), (1, 0))
    x6 = take_by_core(x4, (0, -1), (-1, 0))
    x5 = take_by_core(x3, (0, 1), (1, 0))
    return [g0, g1, x1, x2, x3, x4, x5, x6], beside


OFFSETS = ((0, 0, 0), (1, 0, 7), (2, 1, 7), (7, 3, 0), (3, 2, 7), (6, 2, 0), (4, 3, 7), (5, 1, 0))


def piece_places(c, y, z):
    turn = np.tile(np.array([0, 1, 3, 2], np.int32), len(OFFSETS))
    dz0, dy1, dz1 = (np.repeat(np.array(o, np.int32), 4) for o in zip(*OFFSETS))
    dy = jnp.where(c == 0, turn, dy1)
    dz = jnp.where(c == 0, dz0, 2 * turn + dz1)
    return (y + dy) & (NY - 1), (z + dz) & (NZ - 1)


def columns(row):
    return jnp.broadcast_to(row, (HD, row.shape[1])).T


def qkv_kernel(at_ref, y_ref, z_ref, row_ref, got_ref, modality_ref, gain_ref, *rest):
    own_ws, other_ws, pieces = rest[:8], rest[8:16], rest[16:24]
    mine_ref, theirs_ref, acc, inv, own = rest[24:]
    step = pl.program_id(0)

    @pl.when(step == 0)
    def _():
        count = inv.shape[0]
        squares = row_ref[:, :count] + got_ref[:, :count]
        inv[...] = columns(lax.rsqrt(squares / (2 * NY * NZ * HD) + EPS))
        own[...] = columns((modality_ref[...] == at_ref[0]).astype(jnp.float32))

    inverse = inv[...]
    own_row = own[...] > 0
    normed, right = [], []
    for k, piece in enumerate(pieces):
        yi, zi = y_ref[4 * k + step], z_ref[4 * k + step]
        first = pl.multiple_of(inv.shape[0] + (yi * NZ + zi) * HD, HD)
        gain = jnp.where(own_row, gain_ref[yi, pl.ds(zi, 1), :], got_ref[:, pl.ds(first, HD)])
        normed.append((piece[0].astype(jnp.float32) * inverse * gain).astype(jnp.bfloat16))
        right.append(jnp.concatenate([w[p, 0, 0, 0] for w in (own_ws[k], other_ws[k]) for p in range(3)], axis=1))
    part = jnp.dot(
        jnp.concatenate(normed, axis=1), jnp.concatenate(right, axis=0), preferred_element_type=jnp.float32
    )

    @pl.when(step == 0)
    def _():
        acc[...] = part

    @pl.when(step > 0)
    def _():
        acc[...] += part

    @pl.when(step == pl.num_programs(0) - 1)
    def _():
        half = acc.shape[0] // 2
        for ref, first in ((mine_ref, at_ref[0] * half), (theirs_ref, (1 - at_ref[0]) * half)):
            rows = pl.ds(pl.multiple_of(first, half), half)
            own_here = own[rows, :] > 0
            for p in range(3):
                low, high = acc[rows, p * HD : (p + 1) * HD], acc[rows, (3 + p) * HD : (4 + p) * HD]
                ref[:, p * HD : (p + 1) * HD] = jnp.where(own_here, low, high)


def project(at, ys, zs, row, got, modality, gain, w, w_other, arrays):
    rows = arrays[0].shape[1]
    block = (3, 1, 1, 1, HD, HD)
    whole = lambda shape: pl.BlockSpec(shape, lambda g, *_: (0,) * len(shape))
    piece = pl.BlockSpec((1, rows, HD), lambda g, *_: (g, 0, 0))
    weights = lambda k, other: pl.BlockSpec(
        block, lambda g, at, ys, zs: (0, 0 if other else at[0], ys[4 * k + g], zs[4 * k + g], 0, 0)
    )
    return pl.pallas_call(
        qkv_kernel,
        grid_spec=pltpu.PrefetchScalarGridSpec(
            num_scalar_prefetch=3,
            grid=(4,),
            in_specs=[whole(row.shape), whole(got.shape), whole((1, rows)), whole((NY, NZ, HD))]
            + [weights(k, False) for k in range(8)]
            + [weights(k, True) for k in range(8)]
            + [piece] * 8,
            out_specs=[whole((rows // 2, 3 * HD))] * 2,
            scratch_shapes=[pltpu.VMEM((rows, w), jnp.float32) for w in (6 * HD, HD, HD)],
        ),
        out_shape=[jax.ShapeDtypeStruct((rows // 2, 3 * HD), jnp.float32)] * 2,
        compiler_params=pltpu.CompilerParams(vmem_limit_bytes=61 * 2**20),
        cost_estimate=pl.CostEstimate(
            flops=2 * rows * 4096 * 6 * HD, bytes_accessed=11 * 2**20, transcendentals=0
        ),
    )(at, ys, zs, row, got, modality, gain, *[w] * 8, *[w_other] * 8, *arrays)


def finish_kernel(mine_ref, got_ref, gain_ref, cos_ref, sin_ref, q_ref, kv_ref):
    projected = mine_ref[...] + got_ref[...]
    half = HD // 2
    turned = []
    for p in range(2):
        x = projected[:, p * HD : (p + 1) * HD]
        centred = x - jnp.mean(x, axis=1, keepdims=True)
        variance = jnp.mean(centred * centred, axis=1, keepdims=True)
        x = centred * lax.rsqrt(variance + EPS) * gain_ref[p : p + 1, :]
        swapped = jnp.concatenate([x[:, half:], x[:, :half]], axis=1)
        turned.append((x * cos_ref[...] + swapped * sin_ref[...]).astype(jnp.bfloat16))
    q_ref[...] = turned[0]
    kv_ref[0] = turned[1]
    kv_ref[1] = projected[:, 2 * HD :].astype(jnp.bfloat16)


def finish(mine, got, qk_gain, cosines, sines):
    rows = mine.shape[0]
    vmem = pl.BlockSpec(memory_space=pltpu.VMEM)
    return pl.pallas_call(
        finish_kernel,
        in_specs=[vmem] * 5,
        out_specs=[vmem] * 2,
        out_shape=[
            jax.ShapeDtypeStruct((rows, HD), jnp.bfloat16),
            jax.ShapeDtypeStruct((2, rows, HD), jnp.bfloat16),
        ],
    )(mine, got, qk_gain, cosines, sines)


def attention_kernel(base_ref, q_ref, *rest):
    key_refs, out_ref = rest[:-1], rest[-1]
    rows = q_ref.shape[0]
    queries = q_ref[...]
    scale = 1.0 / math.sqrt(HD)
    row = base_ref[0] + lax.broadcasted_iota(jnp.int32, (rows, rows), 0)
    column = lax.broadcasted_iota(jnp.int32, (rows, rows), 1)
    blocks = [(ref, i) for ref in key_refs for i in range(ref.shape[0])]
    scores, seen = [], []
    for n, (ref, i) in enumerate(blocks):
        s = lax.dot_general(queries, ref[i, 0], (((1,), (1,)), ((), ())), preferred_element_type=jnp.float32)
        allowed = column + base_ref[n] <= row
        seen.append(allowed)
        scores.append(jnp.where(allowed, s * scale, MASKED))
    best = scores[0].max(axis=1, keepdims=True)
    for s in scores[1:]:
        best = jnp.maximum(best, s.max(axis=1, keepdims=True))
    total = jnp.zeros((rows, 1), jnp.float32)
    out = jnp.zeros((rows, HD), jnp.float32)
    for n, (ref, i) in enumerate(blocks):
        weights = jnp.where(seen[n], jnp.exp(scores[n] - best), 0.0)
        total += weights.sum(axis=1, keepdims=True)
        out += jnp.dot(weights.astype(jnp.bfloat16), ref[i, 1], preferred_element_type=jnp.float32)
    result = (out / total).astype(jnp.bfloat16)
    for i in range(out_ref.shape[0]):
        out_ref[i] = result


def attention(bases, queries, keys):
    vmem = pl.BlockSpec(memory_space=pltpu.VMEM)
    return pl.pallas_call(
        attention_kernel,
        in_specs=[pl.BlockSpec(memory_space=pltpu.SMEM)] + [vmem] * (1 + len(keys)),
        out_specs=vmem,
        out_shape=jax.ShapeDtypeStruct((2 * NY, *queries.shape), jnp.bfloat16),
        compiler_params=pltpu.CompilerParams(vmem_limit_bytes=40 * 2**20),
        cost_estimate=pl.CostEstimate(flops=2**28, bytes_accessed=2**20, transcendentals=2**19),
    )(bases, queries, *keys)


def out_kernel(at_ref, modality_ref, w_ref, other_ref, heads_ref, out_ref):
    heads = jnp.concatenate([heads_ref[i] for i in range(2 * NY)], axis=1)
    own_row = columns((modality_ref[...] == at_ref[0]).astype(jnp.float32)) > 0
    n = out_ref.shape[0]
    parts = []
    for ref in (w_ref, other_ref):
        for j in range(n):
            parts.append(jnp.concatenate([ref[x, i, j] for i in range(2 * NY) for x in range(NX)], axis=0))
    sums = jnp.dot(heads, jnp.concatenate(parts, axis=1), preferred_element_type=jnp.float32)
    for j in range(n):
        for i in range(2):
            own, other = ((2 * (n * m + j) + i) * HD for m in range(2))
            chosen = jnp.where(own_row, sums[:, own : own + HD], sums[:, other : other + HD])
            out_ref[j, :, i * HD : (i + 1) * HD] = chosen.astype(jnp.bfloat16)


def out_part(at, modality, w, w_other, heads):
    rows = heads.shape[1]
    steps = 2
    each = NZ // 2 // steps
    whole = lambda shape: pl.BlockSpec(shape, lambda g, at: (0,) * len(shape))
    weights = pl.BlockSpec((NX, 2 * NY, each, HD // NX, 2 * HD), lambda g, at: (0, 0, g, 0, 0))
    return pl.pallas_call(
        out_kernel,
        grid_spec=pltpu.PrefetchScalarGridSpec(
            num_scalar_prefetch=1,
            grid=(steps,),
            in_specs=[whole((1, rows)), weights, weights, whole(heads.shape)],
            out_specs=pl.BlockSpec((each, rows, 2 * HD), lambda g, at: (g, 0, 0)),
        ),
        out_shape=jax.ShapeDtypeStruct((NZ // 2, rows, 2 * HD), jnp.bfloat16),
        compiler_params=pltpu.CompilerParams(vmem_limit_bytes=61 * 2**20),
        cost_estimate=pl.CostEstimate(
            flops=8 * rows * NY * HD * NZ * HD, bytes_accessed=5 * 2**20, transcendentals=0
        ),
    )(at, modality, w, w_other, heads)


def cut_kernel(at_ref, w_ref, out_ref):
    for y in range(NY):
        for odd in range(2):
            for zh in range(NZ // 2):
                for c in range(2):
                    first = ((c * NY + y) * NZ + 2 * zh + odd) * HD
                    out_ref[2 * y + odd, zh, :, c * HD : (c + 1) * HD] = w_ref[:, first : first + HD]


def cut_w_out(at, w_out):
    rows = HD // NX
    shape = (2 * NY, NZ // 2, rows, 2 * HD)
    return pl.pallas_call(
        cut_kernel,
        grid_spec=pltpu.PrefetchScalarGridSpec(
            num_scalar_prefetch=1,
            grid=(1,),
            in_specs=[pl.BlockSpec((rows, w_out.shape[1]), lambda g, at: (at[3], 0))],
            out_specs=pl.BlockSpec(shape, lambda g, at: (0,) * 4),
        ),
        out_shape=jax.ShapeDtypeStruct(shape, jnp.bfloat16),
        cost_estimate=pl.CostEstimate(flops=0, bytes_accessed=2**20, transcendentals=0),
    )(at, w_out)


def spread_w_out(pieces, *ahead):
    lines = lax.all_to_all(pieces, ("y", "zl"), 0, 0)
    lines, *_ = lax.optimization_barrier((lines, *ahead))
    return lax.all_gather(lines, "seq", axis=0)


def shards(tokens, modality, norm_gain, w_qkv, qk_gain, w_out):
    row_count = tokens.shape[0]
    half = row_count // 2
    c, y, zh, zl, seq = (lax.axis_index(a) for a in AXES)
    z = 2 * zh + zl
    at = jnp.stack([c, y, z, seq]).astype(jnp.int32)
    modality = modality[None, :]
    ys, zs = piece_places(c.astype(jnp.int32), y.astype(jnp.int32), z.astype(jnp.int32))

    arrays, pieces = gather(tokens, cut_w_out(at, w_out[0]))
    w_cols = spread_w_out(pieces, arrays[2], arrays[5])
    w_cols_other = take(w_cols, dc=1)

    first = seq * row_count + c * half
    places = first + jnp.arange(half, dtype=jnp.int32)
    rates = 1.0 / 10000.0 ** (jnp.arange(HD // 2, dtype=jnp.float32) * (2.0 / HD))
    angles = places.astype(jnp.float32)[:, None] * rates[None, :]
    cosines, sines = jnp.cos(angles), jnp.sin(angles)
    cosines, sines = jnp.concatenate([cosines, cosines], axis=1), jnp.concatenate([-sines, sines], axis=1)

    w = w_qkv[0].transpose(1, 0, 2).reshape(3, 2, NY, NZ, HD, HD)
    w_other = take(lax.dynamic_slice_in_dim(w, 1 - c, 1, axis=1), dc=1)
    gains = norm_gain.reshape(2, NY * NZ * HD)
    gain_send = lax.dynamic_slice_in_dim(gains, 1 - c, 1, axis=0)
    gain = lax.dynamic_slice_in_dim(gains, c, 1, axis=0).reshape(NY, NZ, HD)

    squares = sum(jnp.sum(jnp.square(a.astype(jnp.float32)), axis=(0, 2)) for a in arrays)
    row = jnp.concatenate([squares[None, :], gain_send], axis=1)
    mine, theirs = project(at, ys, zs, row, take(row, dc=1), modality, gain, w, w_other, arrays)
    queries, own_keys = finish(mine, take(theirs, dc=1), qk_gain, cosines, sines)

    moved = {d: take(own_keys, dx=-d, wrap_x=False) for d in (2, 3, 1)}
    got = jnp.stack([own_keys] + [moved[d] for d in (1, 2, 3)])
    sibling = take(got, dc=1)
    never = 1 << 20
    begin = [jnp.where(seq >= d, (seq - d) * row_count, never) for d in range(NX)]
    bases = jnp.stack([b + c * half for b in begin] + [b + (1 - c) * half for b in begin]).astype(jnp.int32)
    heads_out = attention(bases, queries, [got, sibling])

    heads = lax.all_to_all(heads_out, ("y", "zl"), 0, 0)
    own_half = lax.dynamic_slice_in_dim(modality, c * half, half, axis=1)
    partial = out_part(at, own_half, w_cols, w_cols_other, heads)
    spread = lax.all_to_all(partial, "zh", 0, 0)
    summed = jnp.sum(spread.astype(jnp.float32), axis=0).astype(jnp.bfloat16).reshape(half, 2, HD)
    keep = lax.dynamic_index_in_dim(summed, c, axis=1, keepdims=False)
    other = take(lax.dynamic_index_in_dim(summed, 1 - c, axis=1, keepdims=False), dc=1)
    return jnp.where(c == 0, jnp.concatenate([keep, other]), jnp.concatenate([other, keep]))


def solution(mesh):
    mesh = Mesh(mesh.devices.reshape(2, NY, NZ // 2, 2, NX), AXES)
    tp = ("y", "zh", "zl")
    placed = (
        P("seq", ("mod", *tp)),
        P("seq"),
        P("mod", None),
        P("mod", None, None, tp),
        P(None, tp),
        P("mod", tp, None),
    )
    return jax.shard_map(shards, mesh=mesh, in_specs=placed, out_specs=P("seq", ("mod", *tp)), check_vma=False)
```

```python
import math

import jax
import jax.numpy as jnp
import numpy as np
from jax import lax
from jax.experimental import pallas as pl
from jax.experimental.pallas import tpu as pltpu
from jax.sharding import Mesh
from jax.sharding import PartitionSpec as P

HD = 128
EPS = 1e-05
MASKED = -1e30
NY = 4
NZ = 8
NX = 4
AXES = ("mod", "y", "zh", "zl", "seq")


def pairs(moves, wrap_x=True):
    out = []
    for c in range(2):
        if moves[c] is None:
            continue
        dc, dy, dz, dx = moves[c]
        for y in range(NY):
            for z in range(NZ):
                for x in range(NX):
                    if not wrap_x and not 0 <= x + dx < NX:
                        continue
                    from_z = z ^ 1 if dz == "pair" else (z + dz) % NZ
                    source = (((c + dc) % 2 * NY + (y + dy) % NY) * NZ + from_z) * NX + (x + dx) % NX
                    out.append((source, ((c * NY + y) * NZ + z) * NX + x))
    return out


def take(x, dc=0, dy=0, dz=0, dx=0, wrap_x=True):
    return lax.ppermute(x, AXES, pairs([(dc, dy, dz, dx)] * 2, wrap_x))


def take_by_core(x, on_y, on_z):
    return lax.ppermute(x, AXES, pairs([m and (0, *m, 0) for m in (on_y, on_z)]))


def gather(rows, beside):
    k1 = take_by_core(rows, (1, 0), (0, 2))
    k2 = take_by_core(rows, (-1, 0), (0, -2))
    k3 = take_by_core(rows, (2, 0), (0, 4))
    k1, k2, k3, beside = lax.optimization_barrier((k1, k2, k3, beside))
    g0 = jnp.stack([rows, k1, k2, k3])
    g1 = take_by_core(g0, (0, 1), (0, -1))
    x2 = take_by_core(g0, (0, -1), (-1, 0))
    x1 = take_by_core(g1, (0, 1), (1, 0))
    x4 = take_by_core(x2, (0, -1), (-1, 0))
    x3 = take_by_core(x1, (0, 1), (1, 0))
    x6 = take_by_core(x4, (0, -1), (-1, 0))
    x5 = take_by_core(x3, (0, 1), (1, 0))
    return [g0, g1, x1, x2, x3, x4, x5, x6], beside


OFFSETS = ((0, 0, 0), (1, 0, 7), (2, 1, 7), (7, 3, 0), (3, 2, 7), (6, 2, 0), (4, 3, 7), (5, 1, 0))


def piece_places(c, y, z):
    turn = np.tile(np.array([0, 1, 3, 2], np.int32), len(OFFSETS))
    dz0, dy1, dz1 = (np.repeat(np.array(o, np.int32), 4) for o in zip(*OFFSETS))
    dy = jnp.where(c == 0, turn, dy1)
    dz = jnp.where(c == 0, dz0, 2 * turn + dz1)
    return (y + dy) & (NY - 1), (z + dz) & (NZ - 1)


def columns(row):
    return jnp.broadcast_to(row, (HD, row.shape[1])).T


def qkv_kernel(at_ref, y_ref, z_ref, row_ref, got_ref, modality_ref, gain_ref, *rest):
    own_ws, other_ws, pieces = rest[:8], rest[8:16], rest[16:24]
    mine_ref, theirs_ref, acc, inv, own = rest[24:]
    step = pl.program_id(0)

    @pl.when(step == 0)
    def _():
        count = inv.shape[0]
        squares = row_ref[:, :count] + got_ref[:, :count]
        inv[...] = columns(lax.rsqrt(squares / (2 * NY * NZ * HD) + EPS))
        own[...] = columns((modality_ref[...] == at_ref[0]).astype(jnp.float32))

    inverse = inv[...]
    own_row = own[...] > 0
    normed, right = [], []
    for k, piece in enumerate(pieces):
        yi, zi = y_ref[4 * k + step], z_ref[4 * k + step]
        first = pl.multiple_of(inv.shape[0] + (yi * NZ + zi) * HD, HD)
        gain = jnp.where(own_row, gain_ref[yi, pl.ds(zi, 1), :], got_ref[:, pl.ds(first, HD)])
        normed.append((piece[0].astype(jnp.float32) * inverse * gain).astype(jnp.bfloat16))
        right.append(jnp.concatenate([w[p, 0, 0, 0] for w in (own_ws[k], other_ws[k]) for p in range(3)], axis=1))
    part = jnp.dot(
        jnp.concatenate(normed, axis=1), jnp.concatenate(right, axis=0), preferred_element_type=jnp.float32
    )

    @pl.when(step == 0)
    def _():
        acc[...] = part

    @pl.when(step > 0)
    def _():
        acc[...] += part

    @pl.when(step == pl.num_programs(0) - 1)
    def _():
        half = acc.shape[0] // 2
        for ref, first in ((mine_ref, at_ref[0] * half), (theirs_ref, (1 - at_ref[0]) * half)):
            rows = pl.ds(pl.multiple_of(first, half), half)
            own_here = own[rows, :] > 0
            for p in range(3):
                low, high = acc[rows, p * HD : (p + 1) * HD], acc[rows, (3 + p) * HD : (4 + p) * HD]
                ref[:, p * HD : (p + 1) * HD] = jnp.where(own_here, low, high)


def project(at, ys, zs, row, got, modality, gain, w, w_other, arrays):
    rows = arrays[0].shape[1]
    block = (3, 1, 1, 1, HD, HD)
    whole = lambda shape: pl.BlockSpec(shape, lambda g, *_: (0,) * len(shape))
    piece = pl.BlockSpec((1, rows, HD), lambda g, *_: (g, 0, 0))
    weights = lambda k, other: pl.BlockSpec(
        block, lambda g, at, ys, zs: (0, 0 if other else at[0], ys[4 * k + g], zs[4 * k + g], 0, 0)
    )
    return pl.pallas_call(
        qkv_kernel,
        grid_spec=pltpu.PrefetchScalarGridSpec(
            num_scalar_prefetch=3,
            grid=(4,),
            in_specs=[whole(row.shape), whole(got.shape), whole((1, rows)), whole((NY, NZ, HD))]
            + [weights(k, False) for k in range(8)]
            + [weights(k, True) for k in range(8)]
            + [piece] * 8,
            out_specs=[whole((rows // 2, 3 * HD))] * 2,
            scratch_shapes=[pltpu.VMEM((rows, w), jnp.float32) for w in (6 * HD, HD, HD)],
        ),
        out_shape=[jax.ShapeDtypeStruct((rows // 2, 3 * HD), jnp.float32)] * 2,
        compiler_params=pltpu.CompilerParams(vmem_limit_bytes=61 * 2**20),
        cost_estimate=pl.CostEstimate(
            flops=2 * rows * 4096 * 6 * HD, bytes_accessed=11 * 2**20, transcendentals=0
        ),
    )(at, ys, zs, row, got, modality, gain, *[w] * 8, *[w_other] * 8, *arrays)


def finish_kernel(mine_ref, got_ref, gain_ref, cos_ref, sin_ref, q_ref, kv_ref):
    projected = mine_ref[...] + got_ref[...]
    half = HD // 2
    turned = []
    for p in range(2):
        x = projected[:, p * HD : (p + 1) * HD]
        centred = x - jnp.mean(x, axis=1, keepdims=True)
        variance = jnp.mean(centred * centred, axis=1, keepdims=True)
        x = centred * lax.rsqrt(variance + EPS) * gain_ref[p : p + 1, :]
        swapped = jnp.concatenate([x[:, half:], x[:, :half]], axis=1)
        turned.append((x * cos_ref[...] + swapped * sin_ref[...]).astype(jnp.bfloat16))
    q_ref[...] = turned[0]
    kv_ref[0] = turned[1]
    kv_ref[1] = projected[:, 2 * HD :].astype(jnp.bfloat16)


def finish(mine, got, qk_gain, cosines, sines):
    rows = mine.shape[0]
    vmem = pl.BlockSpec(memory_space=pltpu.VMEM)
    return pl.pallas_call(
        finish_kernel,
        in_specs=[vmem] * 5,
        out_specs=[vmem] * 2,
        out_shape=[
            jax.ShapeDtypeStruct((rows, HD), jnp.bfloat16),
            jax.ShapeDtypeStruct((2, rows, HD), jnp.bfloat16),
        ],
    )(mine, got, qk_gain, cosines, sines)


def attention_kernel(base_ref, q_ref, *rest):
    key_refs, out_ref = rest[:-1], rest[-1]
    rows = q_ref.shape[0]
    queries = q_ref[...]
    scale = 1.0 / math.sqrt(HD)
    row = base_ref[0] + lax.broadcasted_iota(jnp.int32, (rows, rows), 0)
    column = lax.broadcasted_iota(jnp.int32, (rows, rows), 1)
    blocks = [(ref, i) for ref in key_refs for i in range(ref.shape[0])]
    scores, seen = [], []
    for n, (ref, i) in enumerate(blocks):
        s = lax.dot_general(queries, ref[i, 0], (((1,), (1,)), ((), ())), preferred_element_type=jnp.float32)
        allowed = column + base_ref[n] <= row
        seen.append(allowed)
        scores.append(jnp.where(allowed, s * scale, MASKED))
    best = scores[0].max(axis=1, keepdims=True)
    for s in scores[1:]:
        best = jnp.maximum(best, s.max(axis=1, keepdims=True))
    total = jnp.zeros((rows, 1), jnp.float32)
    out = jnp.zeros((rows, HD), jnp.float32)
    for n, (ref, i) in enumerate(blocks):
        weights = jnp.where(seen[n], jnp.exp(scores[n] - best), 0.0)
        total += weights.sum(axis=1, keepdims=True)
        out += jnp.dot(weights.astype(jnp.bfloat16), ref[i, 1], preferred_element_type=jnp.float32)
    result = (out / total).astype(jnp.bfloat16)
    for i in range(out_ref.shape[0]):
        out_ref[i] = result


def attention(bases, queries, keys):
    vmem = pl.BlockSpec(memory_space=pltpu.VMEM)
    return pl.pallas_call(
        attention_kernel,
        in_specs=[pl.BlockSpec(memory_space=pltpu.SMEM)] + [vmem] * (1 + len(keys)),
        out_specs=vmem,
        out_shape=jax.ShapeDtypeStruct((2 * NY, *queries.shape), jnp.bfloat16),
        compiler_params=pltpu.CompilerParams(vmem_limit_bytes=40 * 2**20),
        cost_estimate=pl.CostEstimate(flops=2**28, bytes_accessed=2**20, transcendentals=2**19),
    )(bases, queries, *keys)


def out_kernel(at_ref, modality_ref, w_ref, other_ref, heads_ref, out_ref):
    heads = jnp.concatenate([heads_ref[i] for i in range(2 * NY)], axis=1)
    own_row = columns((modality_ref[...] == at_ref[0]).astype(jnp.float32)) > 0
    n = out_ref.shape[0]
    parts = []
    for ref in (w_ref, other_ref):
        for j in range(n):
            parts.append(jnp.concatenate([ref[x, i, j] for i in range(2 * NY) for x in range(NX)], axis=0))
    sums = jnp.dot(heads, jnp.concatenate(parts, axis=1), preferred_element_type=jnp.float32)
    for j in range(n):
        for i in range(2):
            own, other = ((2 * (n * m + j) + i) * HD for m in range(2))
            chosen = jnp.where(own_row, sums[:, own : own + HD], sums[:, other : other + HD])
            out_ref[j, :, i * HD : (i + 1) * HD] = chosen.astype(jnp.bfloat16)


def out_part(at, modality, w, w_other, heads):
    rows = heads.shape[1]
    steps = 2
    each = NZ // 2 // steps
    whole = lambda shape: pl.BlockSpec(shape, lambda g, at: (0,) * len(shape))
    weights = pl.BlockSpec((NX, 2 * NY, each, HD // NX, 2 * HD), lambda g, at: (0, 0, g, 0, 0))
    return pl.pallas_call(
        out_kernel,
        grid_spec=pltpu.PrefetchScalarGridSpec(
            num_scalar_prefetch=1,
            grid=(steps,),
            in_specs=[whole((1, rows)), weights, weights, whole(heads.shape)],
            out_specs=pl.BlockSpec((each, rows, 2 * HD), lambda g, at: (g, 0, 0)),
        ),
        out_shape=jax.ShapeDtypeStruct((NZ // 2, rows, 2 * HD), jnp.bfloat16),
        compiler_params=pltpu.CompilerParams(vmem_limit_bytes=61 * 2**20),
        cost_estimate=pl.CostEstimate(
            flops=8 * rows * NY * HD * NZ * HD, bytes_accessed=5 * 2**20, transcendentals=0
        ),
    )(at, modality, w, w_other, heads)


GROUPS = [[2 * p + (which ^ (p >> 1)) for p in range(NZ // 2)] for which in range(2)]


def cut_kernel(at_ref, w_ref, out_ref):
    upper = (at_ref[2] >> 2) & 1
    for y in range(NY):
        for odd in range(2):
            for p in range(NZ // 2):
                for c in range(2):
                    first = (c * NY + y) * NZ + 2 * p + ((odd ^ (p >> 1)) ^ upper)
                    piece = w_ref[:, pl.ds(pl.multiple_of(first * HD, HD), HD)]
                    out_ref[2 * y + odd, p, :, c * HD : (c + 1) * HD] = piece


def cut_w_out(at, w_out):
    rows = HD // NX
    shape = (2 * NY, NZ // 2, rows, 2 * HD)
    return pl.pallas_call(
        cut_kernel,
        grid_spec=pltpu.PrefetchScalarGridSpec(
            num_scalar_prefetch=1,
            grid=(1,),
            in_specs=[pl.BlockSpec((rows, w_out.shape[1]), lambda g, at: (at[3], 0))],
            out_specs=pl.BlockSpec(shape, lambda g, at: (0,) * 4),
        ),
        out_shape=jax.ShapeDtypeStruct(shape, jnp.bfloat16),
        cost_estimate=pl.CostEstimate(flops=0, bytes_accessed=2**20, transcendentals=0),
    )(at, w_out)


def spread_w_out(pieces, *ahead):
    lines = lax.all_to_all(pieces, ("y", "zl"), 0, 0)
    lines, *_ = lax.optimization_barrier((lines, *ahead))
    return lax.all_gather(lines, "seq", axis=0)


def shards(tokens, modality, norm_gain, w_qkv, qk_gain, w_out):
    row_count = tokens.shape[0]
    half = row_count // 2
    c, y, zh, zl, seq = (lax.axis_index(a) for a in AXES)
    z = 2 * zh + zl
    at = jnp.stack([c, y, z, seq]).astype(jnp.int32)
    modality = modality[None, :]
    ys, zs = piece_places(c.astype(jnp.int32), y.astype(jnp.int32), z.astype(jnp.int32))

    arrays, pieces = gather(tokens, cut_w_out(at, w_out[0]))
    w_cols = spread_w_out(pieces, arrays[2], arrays[3])
    w_cols_other = take(w_cols, dc=1)

    first = seq * row_count + c * half
    places = first + jnp.arange(half, dtype=jnp.int32)
    rates = 1.0 / 10000.0 ** (jnp.arange(HD // 2, dtype=jnp.float32) * (2.0 / HD))
    angles = places.astype(jnp.float32)[:, None] * rates[None, :]
    cosines, sines = jnp.cos(angles), jnp.sin(angles)
    cosines, sines = jnp.concatenate([cosines, cosines], axis=1), jnp.concatenate([-sines, sines], axis=1)

    w = w_qkv[0].transpose(1, 0, 2).reshape(3, 2, NY, NZ, HD, HD)
    w_other = take(lax.dynamic_slice_in_dim(w, 1 - c, 1, axis=1), dc=1)
    gains = norm_gain.reshape(2, NY * NZ * HD)
    gain_send = lax.dynamic_slice_in_dim(gains, 1 - c, 1, axis=0)
    gain = lax.dynamic_slice_in_dim(gains, c, 1, axis=0).reshape(NY, NZ, HD)

    squares = sum(jnp.sum(jnp.square(a.astype(jnp.float32)), axis=(0, 2)) for a in arrays)
    row = jnp.concatenate([squares[None, :], gain_send], axis=1)
    mine, theirs = project(at, ys, zs, row, take(row, dc=1), modality, gain, w, w_other, arrays)
    queries, own_keys = finish(mine, take(theirs, dc=1), qk_gain, cosines, sines)

    moved = {d: take(own_keys, dx=-d, wrap_x=False) for d in (2, 3, 1)}
    got = jnp.stack([own_keys] + [moved[d] for d in (1, 2, 3)])
    sibling = take(got, dc=1)
    never = 1 << 20
    begin = [jnp.where(seq >= d, (seq - d) * row_count, never) for d in range(NX)]
    bases = jnp.stack([b + c * half for b in begin] + [b + (1 - c) * half for b in begin]).astype(jnp.int32)
    heads_out = attention(bases, queries, [got, sibling])

    heads = lax.all_to_all(heads_out, ("y", "zl"), 0, 0)
    own_half = lax.dynamic_slice_in_dim(modality, c * half, half, axis=1)
    partial = out_part(at, own_half, w_cols, w_cols_other, heads)
    spread = lax.all_to_all(partial, ("zh", "zl"), 0, 0, axis_index_groups=GROUPS)
    summed = jnp.sum(spread.astype(jnp.float32), axis=0).astype(jnp.bfloat16).reshape(half, 2, HD)
    keep = lax.dynamic_index_in_dim(summed, c, axis=1, keepdims=False)
    other = take(lax.dynamic_index_in_dim(summed, 1 - c, axis=1, keepdims=False), dc=1)
    return jnp.where(c == 0, jnp.concatenate([keep, other]), jnp.concatenate([other, keep]))


def solution(mesh):
    mesh = Mesh(mesh.devices.reshape(2, NY, NZ // 2, 2, NX), AXES)
    tp = ("y", "zh", "zl")
    placed = (
        P("seq", ("mod", *tp)),
        P("seq"),
        P("mod", None),
        P("mod", None, None, tp),
        P(None, tp),
        P("mod", tp, None),
    )
    return jax.shard_map(shards, mesh=mesh, in_specs=placed, out_specs=P("seq", ("mod", *tp)), check_vma=False)
```

```python
import math

import jax
import jax.numpy as jnp
import numpy as np
from jax import lax
from jax.experimental import pallas as pl
from jax.experimental.pallas import tpu as pltpu
from jax.sharding import Mesh
from jax.sharding import PartitionSpec as P

HD = 128
EPS = 1e-05
MASKED = -1e30
NY = 4
NZ = 8
NX = 4
AXES = ("mod", "y", "zh", "zl", "seq")


def pairs(moves, wrap_x=True):
    out = []
    for c in range(2):
        if moves[c] is None:
            continue
        dc, dy, dz, dx = moves[c]
        for y in range(NY):
            for z in range(NZ):
                for x in range(NX):
                    if not wrap_x and not 0 <= x + dx < NX:
                        continue
                    from_z = z ^ 1 if dz == "pair" else (z + dz) % NZ
                    source = (((c + dc) % 2 * NY + (y + dy) % NY) * NZ + from_z) * NX + (x + dx) % NX
                    out.append((source, ((c * NY + y) * NZ + z) * NX + x))
    return out


def take(x, dc=0, dy=0, dz=0, dx=0, wrap_x=True):
    return lax.ppermute(x, AXES, pairs([(dc, dy, dz, dx)] * 2, wrap_x))


def take_by_core(x, on_y, on_z):
    return lax.ppermute(x, AXES, pairs([m and (0, *m, 0) for m in (on_y, on_z)]))


def gather(rows, beside):
    k1 = take_by_core(rows, (1, 0), (0, 2))
    k2 = take_by_core(rows, (-1, 0), (0, -2))
    k3 = take_by_core(rows, (2, 0), (0, 4))
    k1, k2, k3, beside = lax.optimization_barrier((k1, k2, k3, beside))
    g0 = jnp.stack([rows, k1, k2, k3])
    g1 = take_by_core(g0, (0, 1), (0, -1))
    x2 = take_by_core(g0, (0, -1), (-1, 0))
    x1 = take_by_core(g1, (0, 1), (1, 0))
    x4 = take_by_core(x2, (0, -1), (-1, 0))
    x3 = take_by_core(x1, (0, 1), (1, 0))
    x6 = take_by_core(x4, (0, -1), (-1, 0))
    x5 = take_by_core(x3, (0, 1), (1, 0))
    return [g0, g1, x1, x2, x3, x4, x5, x6], beside


OFFSETS = ((0, 0, 0), (1, 0, 7), (2, 1, 7), (7, 3, 0), (3, 2, 7), (6, 2, 0), (4, 3, 7), (5, 1, 0))


def piece_places(c, y, z):
    turn = np.tile(np.array([0, 1, 3, 2], np.int32), len(OFFSETS))
    dz0, dy1, dz1 = (np.repeat(np.array(o, np.int32), 4) for o in zip(*OFFSETS))
    dy = jnp.where(c == 0, turn, dy1)
    dz = jnp.where(c == 0, dz0, 2 * turn + dz1)
    return (y + dy) & (NY - 1), (z + dz) & (NZ - 1)


def columns(row):
    return jnp.broadcast_to(row, (HD, row.shape[1])).T


def qkv_kernel(at_ref, y_ref, z_ref, row_ref, got_ref, modality_ref, gain_ref, *rest):
    own_ws, other_ws, pieces = rest[:8], rest[8:16], rest[16:24]
    mine_ref, theirs_ref, acc, inv, own = rest[24:]
    step = pl.program_id(0)

    @pl.when(step == 0)
    def _():
        count = inv.shape[0]
        squares = row_ref[:, :count] + got_ref[:, :count]
        inv[...] = columns(lax.rsqrt(squares / (2 * NY * NZ * HD) + EPS))
        own[...] = columns((modality_ref[...] == at_ref[0]).astype(jnp.float32))

    inverse = inv[...]
    own_row = own[...] > 0
    normed, right = [], []
    for k, piece in enumerate(pieces):
        yi, zi = y_ref[4 * k + step], z_ref[4 * k + step]
        first = pl.multiple_of(inv.shape[0] + (yi * NZ + zi) * HD, HD)
        gain = jnp.where(own_row, gain_ref[yi, pl.ds(zi, 1), :], got_ref[:, pl.ds(first, HD)])
        normed.append((piece[0].astype(jnp.float32) * inverse * gain).astype(jnp.bfloat16))
        right.append(jnp.concatenate([w[p, 0, 0, 0] for w in (own_ws[k], other_ws[k]) for p in range(3)], axis=1))
    part = jnp.dot(
        jnp.concatenate(normed, axis=1), jnp.concatenate(right, axis=0), preferred_element_type=jnp.float32
    )

    @pl.when(step == 0)
    def _():
        acc[...] = part

    @pl.when(step > 0)
    def _():
        acc[...] += part

    @pl.when(step == pl.num_programs(0) - 1)
    def _():
        half = acc.shape[0] // 2
        for ref, first in ((mine_ref, at_ref[0] * half), (theirs_ref, (1 - at_ref[0]) * half)):
            rows = pl.ds(pl.multiple_of(first, half), half)
            own_here = own[rows, :] > 0
            for p in range(3):
                low, high = acc[rows, p * HD : (p + 1) * HD], acc[rows, (3 + p) * HD : (4 + p) * HD]
                ref[:, p * HD : (p + 1) * HD] = jnp.where(own_here, low, high)


def project(at, ys, zs, row, got, modality, gain, w, w_other, arrays):
    rows = arrays[0].shape[1]
    block = (3, 1, 1, 1, HD, HD)
    whole = lambda shape: pl.BlockSpec(shape, lambda g, *_: (0,) * len(shape))
    piece = pl.BlockSpec((1, rows, HD), lambda g, *_: (g, 0, 0))
    weights = lambda k, other: pl.BlockSpec(
        block, lambda g, at, ys, zs: (0, 0 if other else at[0], ys[4 * k + g], zs[4 * k + g], 0, 0)
    )
    return pl.pallas_call(
        qkv_kernel,
        grid_spec=pltpu.PrefetchScalarGridSpec(
            num_scalar_prefetch=3,
            grid=(4,),
            in_specs=[whole(row.shape), whole(got.shape), whole((1, rows)), whole((NY, NZ, HD))]
            + [weights(k, False) for k in range(8)]
            + [weights(k, True) for k in range(8)]
            + [piece] * 8,
            out_specs=[whole((rows // 2, 3 * HD))] * 2,
            scratch_shapes=[pltpu.VMEM((rows, w), jnp.float32) for w in (6 * HD, HD, HD)],
        ),
        out_shape=[jax.ShapeDtypeStruct((rows // 2, 3 * HD), jnp.float32)] * 2,
        compiler_params=pltpu.CompilerParams(vmem_limit_bytes=61 * 2**20),
        cost_estimate=pl.CostEstimate(
            flops=2 * rows * 4096 * 6 * HD, bytes_accessed=11 * 2**20, transcendentals=0
        ),
    )(at, ys, zs, row, got, modality, gain, *[w] * 8, *[w_other] * 8, *arrays)


def finish_kernel(mine_ref, got_ref, gain_ref, cos_ref, sin_ref, q_ref, kv_ref):
    projected = mine_ref[...] + got_ref[...]
    half = HD // 2
    turned = []
    for p in range(2):
        x = projected[:, p * HD : (p + 1) * HD]
        centred = x - jnp.mean(x, axis=1, keepdims=True)
        variance = jnp.mean(centred * centred, axis=1, keepdims=True)
        x = centred * lax.rsqrt(variance + EPS) * gain_ref[p : p + 1, :]
        swapped = jnp.concatenate([x[:, half:], x[:, :half]], axis=1)
        turned.append((x * cos_ref[...] + swapped * sin_ref[...]).astype(jnp.bfloat16))
    q_ref[...] = turned[0]
    values = projected[:, 2 * HD :].astype(jnp.bfloat16)
    for x in range(NX):
        kv_ref[x, 0] = turned[1]
        kv_ref[x, 1] = values


def finish(mine, got, qk_gain, cosines, sines):
    rows = mine.shape[0]
    vmem = pl.BlockSpec(memory_space=pltpu.VMEM)
    return pl.pallas_call(
        finish_kernel,
        in_specs=[vmem] * 5,
        out_specs=[vmem] * 2,
        out_shape=[
            jax.ShapeDtypeStruct((rows, HD), jnp.bfloat16),
            jax.ShapeDtypeStruct((NX, 2, rows, HD), jnp.bfloat16),
        ],
    )(mine, got, qk_gain, cosines, sines)


def attention_kernel(base_ref, q_ref, *rest):
    key_refs, out_ref = rest[:-1], rest[-1]
    rows = q_ref.shape[0]
    queries = q_ref[...]
    scale = 1.0 / math.sqrt(HD)
    row = base_ref[2 * NX] + lax.broadcasted_iota(jnp.int32, (rows, rows), 0)
    column = lax.broadcasted_iota(jnp.int32, (rows, rows), 1)
    blocks = [(ref, i) for ref in key_refs for i in range(ref.shape[0])]
    scores, seen = [], []
    for n, (ref, i) in enumerate(blocks):
        s = lax.dot_general(queries, ref[i, 0], (((1,), (1,)), ((), ())), preferred_element_type=jnp.float32)
        allowed = column + base_ref[n] <= row
        seen.append(allowed)
        scores.append(jnp.where(allowed, s * scale, MASKED))
    best = scores[0].max(axis=1, keepdims=True)
    for s in scores[1:]:
        best = jnp.maximum(best, s.max(axis=1, keepdims=True))
    total = jnp.zeros((rows, 1), jnp.float32)
    out = jnp.zeros((rows, HD), jnp.float32)
    for n, (ref, i) in enumerate(blocks):
        weights = jnp.where(seen[n], jnp.exp(scores[n] - best), 0.0)
        total += weights.sum(axis=1, keepdims=True)
        out += jnp.dot(weights.astype(jnp.bfloat16), ref[i, 1], preferred_element_type=jnp.float32)
    result = (out / total).astype(jnp.bfloat16)
    for i in range(out_ref.shape[0]):
        out_ref[i] = result


def attention(bases, queries, keys):
    vmem = pl.BlockSpec(memory_space=pltpu.VMEM)
    return pl.pallas_call(
        attention_kernel,
        in_specs=[pl.BlockSpec(memory_space=pltpu.SMEM)] + [vmem] * (1 + len(keys)),
        out_specs=vmem,
        out_shape=jax.ShapeDtypeStruct((2 * NY, *queries.shape), jnp.bfloat16),
        compiler_params=pltpu.CompilerParams(vmem_limit_bytes=40 * 2**20),
        cost_estimate=pl.CostEstimate(flops=2**28, bytes_accessed=2**20, transcendentals=2**19),
    )(bases, queries, *keys)


def out_kernel(at_ref, modality_ref, w_ref, other_ref, heads_ref, out_ref):
    heads = jnp.concatenate([heads_ref[i] for i in range(2 * NY)], axis=1)
    own_row = columns((modality_ref[...] == at_ref[0]).astype(jnp.float32)) > 0
    n = out_ref.shape[0]
    parts = []
    for ref in (w_ref, other_ref):
        for j in range(n):
            parts.append(jnp.concatenate([ref[x, i, j] for i in range(2 * NY) for x in range(NX)], axis=0))
    sums = jnp.dot(heads, jnp.concatenate(parts, axis=1), preferred_element_type=jnp.float32)
    for j in range(n):
        for i in range(2):
            own, other = ((2 * (n * m + j) + i) * HD for m in range(2))
            chosen = jnp.where(own_row, sums[:, own : own + HD], sums[:, other : other + HD])
            out_ref[j, :, i * HD : (i + 1) * HD] = chosen.astype(jnp.bfloat16)


def out_part(at, modality, w, w_other, heads):
    rows = heads.shape[1]
    steps = 2
    each = NZ // 2 // steps
    whole = lambda shape: pl.BlockSpec(shape, lambda g, at: (0,) * len(shape))
    weights = pl.BlockSpec((NX, 2 * NY, each, HD // NX, 2 * HD), lambda g, at: (0, 0, g, 0, 0))
    return pl.pallas_call(
        out_kernel,
        grid_spec=pltpu.PrefetchScalarGridSpec(
            num_scalar_prefetch=1,
            grid=(steps,),
            in_specs=[whole((1, rows)), weights, weights, whole(heads.shape)],
            out_specs=pl.BlockSpec((each, rows, 2 * HD), lambda g, at: (g, 0, 0)),
        ),
        out_shape=jax.ShapeDtypeStruct((NZ // 2, rows, 2 * HD), jnp.bfloat16),
        compiler_params=pltpu.CompilerParams(vmem_limit_bytes=61 * 2**20),
        cost_estimate=pl.CostEstimate(
            flops=8 * rows * NY * HD * NZ * HD, bytes_accessed=5 * 2**20, transcendentals=0
        ),
    )(at, modality, w, w_other, heads)


GROUPS = [[2 * p + (which ^ (p >> 1)) for p in range(NZ // 2)] for which in range(2)]


def cut_kernel(at_ref, w_ref, out_ref):
    upper = (at_ref[2] >> 2) & 1
    for y in range(NY):
        for odd in range(2):
            for p in range(NZ // 2):
                for c in range(2):
                    first = (c * NY + y) * NZ + 2 * p + ((odd ^ (p >> 1)) ^ upper)
                    piece = w_ref[:, pl.ds(pl.multiple_of(first * HD, HD), HD)]
                    out_ref[2 * y + odd, p, :, c * HD : (c + 1) * HD] = piece


def cut_w_out(at, w_out):
    rows = HD // NX
    shape = (2 * NY, NZ // 2, rows, 2 * HD)
    return pl.pallas_call(
        cut_kernel,
        grid_spec=pltpu.PrefetchScalarGridSpec(
            num_scalar_prefetch=1,
            grid=(1,),
            in_specs=[pl.BlockSpec((rows, w_out.shape[1]), lambda g, at: (at[3], 0))],
            out_specs=pl.BlockSpec(shape, lambda g, at: (0,) * 4),
        ),
        out_shape=jax.ShapeDtypeStruct(shape, jnp.bfloat16),
        cost_estimate=pl.CostEstimate(flops=0, bytes_accessed=2**20, transcendentals=0),
    )(at, w_out)


def spread_w_out(pieces, *ahead):
    lines = lax.all_to_all(pieces, ("y", "zl"), 0, 0)
    lines, *_ = lax.optimization_barrier((lines, *ahead))
    return lax.all_gather(lines, "seq", axis=0)


def shards(tokens, modality, norm_gain, w_qkv, qk_gain, w_out):
    row_count = tokens.shape[0]
    half = row_count // 2
    c, y, zh, zl, seq = (lax.axis_index(a) for a in AXES)
    z = 2 * zh + zl
    at = jnp.stack([c, y, z, seq]).astype(jnp.int32)
    modality = modality[None, :]
    ys, zs = piece_places(c.astype(jnp.int32), y.astype(jnp.int32), z.astype(jnp.int32))

    w = w_qkv[0].transpose(1, 0, 2).reshape(3, 2, NY, NZ, HD, HD)
    w_send = lax.dynamic_slice_in_dim(w, 1 - c, 1, axis=1)
    arrays, (pieces, w_send) = gather(tokens, (cut_w_out(at, w_out[0]), w_send))
    w_cols = spread_w_out(pieces, arrays[2], arrays[3])
    w_cols_other = take(w_cols, dc=1)

    first = seq * row_count + c * half
    places = first + jnp.arange(half, dtype=jnp.int32)
    rates = 1.0 / 10000.0 ** (jnp.arange(HD // 2, dtype=jnp.float32) * (2.0 / HD))
    angles = places.astype(jnp.float32)[:, None] * rates[None, :]
    cosines, sines = jnp.cos(angles), jnp.sin(angles)
    cosines, sines = jnp.concatenate([cosines, cosines], axis=1), jnp.concatenate([-sines, sines], axis=1)

    w_other = take(w_send, dc=1)
    gains = norm_gain.reshape(2, NY * NZ * HD)
    gain_send = lax.dynamic_slice_in_dim(gains, 1 - c, 1, axis=0)
    gain = lax.dynamic_slice_in_dim(gains, c, 1, axis=0).reshape(NY, NZ, HD)

    squares = sum(jnp.sum(jnp.square(a.astype(jnp.float32)), axis=(0, 2)) for a in arrays)
    row = jnp.concatenate([squares[None, :], gain_send], axis=1)
    mine, theirs = project(at, ys, zs, row, take(row, dc=1), modality, gain, w, w_other, arrays)
    queries, own_keys = finish(mine, take(theirs, dc=1), qk_gain, cosines, sines)

    got = lax.all_to_all(own_keys, "seq", 0, 0)
    sibling = take(got, dc=1)
    starts = jnp.concatenate([jnp.arange(NX) * row_count + part * half for part in (c, 1 - c)])
    bases = jnp.concatenate([starts, first[None]]).astype(jnp.int32)
    heads_out = attention(bases, queries, [got, sibling])

    heads = lax.all_to_all(heads_out, ("y", "zl"), 0, 0)
    own_half = lax.dynamic_slice_in_dim(modality, c * half, half, axis=1)
    partial = out_part(at, own_half, w_cols, w_cols_other, heads)
    spread = lax.all_to_all(partial, ("zh", "zl"), 0, 0, axis_index_groups=GROUPS)
    summed = jnp.sum(spread.astype(jnp.float32), axis=0).astype(jnp.bfloat16).reshape(half, 2, HD)
    keep = lax.dynamic_index_in_dim(summed, c, axis=1, keepdims=False)
    other = take(lax.dynamic_index_in_dim(summed, 1 - c, axis=1, keepdims=False), dc=1)
    return jnp.where(c == 0, jnp.concatenate([keep, other]), jnp.concatenate([other, keep]))


def solution(mesh):
    mesh = Mesh(mesh.devices.reshape(2, NY, NZ // 2, 2, NX), AXES)
    tp = ("y", "zh", "zl")
    placed = (
        P("seq", ("mod", *tp)),
        P("seq"),
        P("mod", None),
        P("mod", None, None, tp),
        P(None, tp),
        P("mod", tp, None),
    )
    return jax.shard_map(shards, mesh=mesh, in_specs=placed, out_specs=P("seq", ("mod", *tp)), check_vma=False)
```

```python
import math

import jax
import jax.numpy as jnp
import numpy as np
from jax import lax
from jax.experimental import pallas as pl
from jax.experimental.pallas import tpu as pltpu
from jax.sharding import Mesh
from jax.sharding import PartitionSpec as P

HD = 128
EPS = 1e-05
MASKED = -1e30
NY = 4
NZ = 8
NX = 4
AXES = ("mod", "y", "zh", "zl", "seq")


def pairs(moves, wrap_x=True):
    out = []
    for c in range(2):
        if moves[c] is None:
            continue
        dc, dy, dz, dx = moves[c]
        for y in range(NY):
            for z in range(NZ):
                for x in range(NX):
                    if not wrap_x and not 0 <= x + dx < NX:
                        continue
                    from_z = z ^ 1 if dz == "pair" else (z + dz) % NZ
                    source = (((c + dc) % 2 * NY + (y + dy) % NY) * NZ + from_z) * NX + (x + dx) % NX
                    out.append((source, ((c * NY + y) * NZ + z) * NX + x))
    return out


def take(x, dc=0, dy=0, dz=0, dx=0, wrap_x=True):
    return lax.ppermute(x, AXES, pairs([(dc, dy, dz, dx)] * 2, wrap_x))


def take_by_core(x, on_y, on_z):
    return lax.ppermute(x, AXES, pairs([m and (0, *m, 0) for m in (on_y, on_z)]))


def gather(rows, beside):
    k1 = take_by_core(rows, (1, 0), (0, 2))
    k2 = take_by_core(rows, (-1, 0), (0, -2))
    k3 = take_by_core(rows, (2, 0), (0, 4))
    k1, k2, k3, beside = lax.optimization_barrier((k1, k2, k3, beside))
    g0 = jnp.stack([rows, k1, k2, k3])
    g1 = take_by_core(g0, (0, 1), (0, -1))
    x2 = take_by_core(g0, (0, -1), (-1, 0))
    x1 = take_by_core(g1, (0, 1), (1, 0))
    x4 = take_by_core(x2, (0, -1), (-1, 0))
    x3 = take_by_core(x1, (0, 1), (1, 0))
    x6 = take_by_core(x4, (0, -1), (-1, 0))
    x5 = take_by_core(x3, (0, 1), (1, 0))
    return [g0, g1, x1, x2, x3, x4, x5, x6], beside


OFFSETS = ((0, 0, 0), (1, 0, 7), (2, 1, 7), (7, 3, 0), (3, 2, 7), (6, 2, 0), (4, 3, 7), (5, 1, 0))


def piece_places(c, y, z):
    turn = np.tile(np.array([0, 1, 3, 2], np.int32), len(OFFSETS))
    dz0, dy1, dz1 = (np.repeat(np.array(o, np.int32), 4) for o in zip(*OFFSETS))
    dy = jnp.where(c == 0, turn, dy1)
    dz = jnp.where(c == 0, dz0, 2 * turn + dz1)
    return (y + dy) & (NY - 1), (z + dz) & (NZ - 1)


def columns(row):
    return jnp.broadcast_to(row, (HD, row.shape[1])).T


def qkv_kernel(at_ref, y_ref, z_ref, row_ref, got_ref, modality_ref, gain_ref, *rest):
    own_ws, other_ws, pieces = rest[:8], rest[8:16], rest[16:24]
    mine_ref, theirs_ref, acc, inv, own = rest[24:]
    step = pl.program_id(0)

    @pl.when(step == 0)
    def _():
        count = inv.shape[0]
        squares = row_ref[:, :count] + got_ref[:, :count]
        inv[...] = columns(lax.rsqrt(squares / (2 * NY * NZ * HD) + EPS))
        own[...] = columns((modality_ref[...] == at_ref[0]).astype(jnp.float32))

    inverse = inv[...]
    own_row = own[...] > 0
    normed, right = [], []
    for k, piece in enumerate(pieces):
        yi, zi = y_ref[4 * k + step], z_ref[4 * k + step]
        at_own = pl.ds(pl.multiple_of((yi * NZ + zi) * HD, HD), HD)
        at_got = pl.ds(pl.multiple_of(inv.shape[0] + (yi * NZ + zi) * HD, HD), HD)
        gain = jnp.where(own_row, gain_ref[:, at_own], got_ref[:, at_got])
        normed.append((piece[0].astype(jnp.float32) * inverse * gain).astype(jnp.bfloat16))
        right.append(jnp.concatenate([w[p, 0, 0, 0] for w in (own_ws[k], other_ws[k]) for p in range(3)], axis=1))
    part = jnp.dot(
        jnp.concatenate(normed, axis=1), jnp.concatenate(right, axis=0), preferred_element_type=jnp.float32
    )

    @pl.when(step == 0)
    def _():
        acc[...] = part

    @pl.when(step > 0)
    def _():
        acc[...] += part

    @pl.when(step == pl.num_programs(0) - 1)
    def _():
        half = acc.shape[0] // 2
        for ref, first in ((mine_ref, at_ref[0] * half), (theirs_ref, (1 - at_ref[0]) * half)):
            rows = pl.ds(pl.multiple_of(first, half), half)
            own_here = own[rows, :] > 0
            for p in range(3):
                low, high = acc[rows, p * HD : (p + 1) * HD], acc[rows, (3 + p) * HD : (4 + p) * HD]
                ref[:, p * HD : (p + 1) * HD] = jnp.where(own_here, low, high)


def project(at, ys, zs, row, got, modality, gain, w, w_other, arrays):
    rows = arrays[0].shape[1]
    block = (3, 1, 1, 1, HD, HD)
    whole = lambda shape: pl.BlockSpec(shape, lambda g, *_: (0,) * len(shape))
    piece = pl.BlockSpec((1, rows, HD), lambda g, *_: (g, 0, 0))
    weights = lambda k, other: pl.BlockSpec(
        block, lambda g, at, ys, zs: (0, 0 if other else at[0], ys[4 * k + g], zs[4 * k + g], 0, 0)
    )
    return pl.pallas_call(
        qkv_kernel,
        grid_spec=pltpu.PrefetchScalarGridSpec(
            num_scalar_prefetch=3,
            grid=(4,),
            in_specs=[whole(row.shape), whole(got.shape), whole((1, rows)), whole(gain.shape)]
            + [weights(k, False) for k in range(8)]
            + [weights(k, True) for k in range(8)]
            + [piece] * 8,
            out_specs=[whole((rows // 2, 3 * HD))] * 2,
            scratch_shapes=[pltpu.VMEM((rows, w), jnp.float32) for w in (6 * HD, HD, HD)],
        ),
        out_shape=[jax.ShapeDtypeStruct((rows // 2, 3 * HD), jnp.float32)] * 2,
        compiler_params=pltpu.CompilerParams(vmem_limit_bytes=61 * 2**20),
        cost_estimate=pl.CostEstimate(
            flops=2 * rows * 4096 * 6 * HD, bytes_accessed=11 * 2**20, transcendentals=0
        ),
    )(at, ys, zs, row, got, modality, gain, *[w] * 8, *[w_other] * 8, *arrays)


def finish_kernel(mine_ref, got_ref, gain_ref, cos_ref, sin_ref, q_ref, kv_ref):
    projected = mine_ref[...] + got_ref[...]
    half = HD // 2
    turned = []
    for p in range(2):
        x = projected[:, p * HD : (p + 1) * HD]
        centred = x - jnp.mean(x, axis=1, keepdims=True)
        variance = jnp.mean(centred * centred, axis=1, keepdims=True)
        x = centred * lax.rsqrt(variance + EPS) * gain_ref[p : p + 1, :]
        swapped = jnp.concatenate([x[:, half:], x[:, :half]], axis=1)
        turned.append((x * cos_ref[...] + swapped * sin_ref[...]).astype(jnp.bfloat16))
    q_ref[...] = turned[0]
    kv_ref[0] = turned[1]
    kv_ref[1] = projected[:, 2 * HD :].astype(jnp.bfloat16)


def finish(mine, got, qk_gain, cosines, sines):
    rows = mine.shape[0]
    vmem = pl.BlockSpec(memory_space=pltpu.VMEM)
    return pl.pallas_call(
        finish_kernel,
        in_specs=[vmem] * 5,
        out_specs=[vmem] * 2,
        out_shape=[
            jax.ShapeDtypeStruct((rows, HD), jnp.bfloat16),
            jax.ShapeDtypeStruct((2, rows, HD), jnp.bfloat16),
        ],
    )(mine, got, qk_gain, cosines, sines)


def attention_kernel(base_ref, q_ref, *rest):
    key_refs, out_ref = rest[:-1], rest[-1]
    rows = q_ref.shape[0]
    queries = q_ref[...]
    scale = 1.0 / math.sqrt(HD)
    row = base_ref[0] + lax.broadcasted_iota(jnp.int32, (rows, rows), 0)
    column = lax.broadcasted_iota(jnp.int32, (rows, rows), 1)
    blocks = [(ref, i) for ref in key_refs for i in range(ref.shape[0])]
    scores, seen = [], []
    for n, (ref, i) in enumerate(blocks):
        s = lax.dot_general(queries, ref[i, 0], (((1,), (1,)), ((), ())), preferred_element_type=jnp.float32)
        allowed = column + base_ref[n] <= row
        seen.append(allowed)
        scores.append(jnp.where(allowed, s * scale, MASKED))
    best = scores[0].max(axis=1, keepdims=True)
    for s in scores[1:]:
        best = jnp.maximum(best, s.max(axis=1, keepdims=True))
    total = jnp.zeros((rows, 1), jnp.float32)
    out = jnp.zeros((rows, HD), jnp.float32)
    for n, (ref, i) in enumerate(blocks):
        weights = jnp.where(seen[n], jnp.exp(scores[n] - best), 0.0)
        total += weights.sum(axis=1, keepdims=True)
        out += jnp.dot(weights.astype(jnp.bfloat16), ref[i, 1], preferred_element_type=jnp.float32)
    result = (out / total).astype(jnp.bfloat16)
    for i in range(out_ref.shape[0]):
        out_ref[i] = result


def attention(bases, queries, keys):
    vmem = pl.BlockSpec(memory_space=pltpu.VMEM)
    return pl.pallas_call(
        attention_kernel,
        in_specs=[pl.BlockSpec(memory_space=pltpu.SMEM)] + [vmem] * (1 + len(keys)),
        out_specs=vmem,
        out_shape=jax.ShapeDtypeStruct((2 * NY, *queries.shape), jnp.bfloat16),
        compiler_params=pltpu.CompilerParams(vmem_limit_bytes=40 * 2**20),
        cost_estimate=pl.CostEstimate(flops=2**28, bytes_accessed=2**20, transcendentals=2**19),
    )(bases, queries, *keys)


def out_kernel(at_ref, modality_ref, w_ref, other_ref, heads_ref, out_ref):
    heads = jnp.concatenate([heads_ref[i] for i in range(2 * NY)], axis=1)
    own_row = columns((modality_ref[...] == at_ref[0]).astype(jnp.float32)) > 0
    n = out_ref.shape[0]
    parts = []
    for ref in (w_ref, other_ref):
        for j in range(n):
            parts.append(jnp.concatenate([ref[x, i, j] for i in range(2 * NY) for x in range(NX)], axis=0))
    sums = jnp.dot(heads, jnp.concatenate(parts, axis=1), preferred_element_type=jnp.float32)
    for j in range(n):
        for i in range(2):
            own, other = ((2 * (n * m + j) + i) * HD for m in range(2))
            chosen = jnp.where(own_row, sums[:, own : own + HD], sums[:, other : other + HD])
            out_ref[j, :, i * HD : (i + 1) * HD] = chosen.astype(jnp.bfloat16)


def out_part(at, modality, w, w_other, heads):
    rows = heads.shape[1]
    steps = 2
    each = NZ // 2 // steps
    whole = lambda shape: pl.BlockSpec(shape, lambda g, at: (0,) * len(shape))
    weights = pl.BlockSpec((NX, 2 * NY, each, HD // NX, 2 * HD), lambda g, at: (0, 0, g, 0, 0))
    return pl.pallas_call(
        out_kernel,
        grid_spec=pltpu.PrefetchScalarGridSpec(
            num_scalar_prefetch=1,
            grid=(steps,),
            in_specs=[whole((1, rows)), weights, weights, whole(heads.shape)],
            out_specs=pl.BlockSpec((each, rows, 2 * HD), lambda g, at: (g, 0, 0)),
        ),
        out_shape=jax.ShapeDtypeStruct((NZ // 2, rows, 2 * HD), jnp.bfloat16),
        compiler_params=pltpu.CompilerParams(vmem_limit_bytes=61 * 2**20),
        cost_estimate=pl.CostEstimate(
            flops=8 * rows * NY * HD * NZ * HD, bytes_accessed=5 * 2**20, transcendentals=0
        ),
    )(at, modality, w, w_other, heads)


GROUPS = [[2 * p + (which ^ (p >> 1)) for p in range(NZ // 2)] for which in range(2)]


def cut_kernel(at_ref, w_ref, out_ref):
    upper = (at_ref[2] >> 2) & 1
    for y in range(NY):
        for odd in range(2):
            for p in range(NZ // 2):
                for c in range(2):
                    first = (c * NY + y) * NZ + 2 * p + ((odd ^ (p >> 1)) ^ upper)
                    piece = w_ref[:, pl.ds(pl.multiple_of(first * HD, HD), HD)]
                    out_ref[2 * y + odd, p, :, c * HD : (c + 1) * HD] = piece


def cut_w_out(at, w_out):
    rows = HD // NX
    shape = (2 * NY, NZ // 2, rows, 2 * HD)
    return pl.pallas_call(
        cut_kernel,
        grid_spec=pltpu.PrefetchScalarGridSpec(
            num_scalar_prefetch=1,
            grid=(1,),
            in_specs=[pl.BlockSpec((rows, w_out.shape[1]), lambda g, at: (at[3], 0))],
            out_specs=pl.BlockSpec(shape, lambda g, at: (0,) * 4),
        ),
        out_shape=jax.ShapeDtypeStruct(shape, jnp.bfloat16),
        cost_estimate=pl.CostEstimate(flops=0, bytes_accessed=2**20, transcendentals=0),
    )(at, w_out)


def spread_w_out(pieces, *ahead):
    lines = lax.all_to_all(pieces, ("y", "zl"), 0, 0)
    lines, *_ = lax.optimization_barrier((lines, *ahead))
    return lax.all_gather(lines, "seq", axis=0)


def shards(tokens, modality, norm_gain, w_qkv, qk_gain, w_out):
    row_count = tokens.shape[0]
    half = row_count // 2
    c, y, zh, zl, seq = (lax.axis_index(a) for a in AXES)
    z = 2 * zh + zl
    at = jnp.stack([c, y, z, seq]).astype(jnp.int32)
    modality = modality[None, :]
    ys, zs = piece_places(c.astype(jnp.int32), y.astype(jnp.int32), z.astype(jnp.int32))

    w = w_qkv[0].transpose(1, 0, 2).reshape(3, 2, NY, NZ, HD, HD)
    w_send = lax.dynamic_slice_in_dim(w, 1 - c, 1, axis=1)
    arrays, (pieces, w_send) = gather(tokens, (cut_w_out(at, w_out[0]), w_send))
    w_cols = spread_w_out(pieces, arrays[2], arrays[3])
    w_cols_other = take(w_cols, dc=1)

    first = seq * row_count + c * half
    places = first + jnp.arange(half, dtype=jnp.int32)
    rates = 1.0 / 10000.0 ** (jnp.arange(HD // 2, dtype=jnp.float32) * (2.0 / HD))
    angles = places.astype(jnp.float32)[:, None] * rates[None, :]
    cosines, sines = jnp.cos(angles), jnp.sin(angles)
    cosines, sines = jnp.concatenate([cosines, cosines], axis=1), jnp.concatenate([-sines, sines], axis=1)

    w_other = take(w_send, dc=1)
    width = NY * NZ * HD
    gain_send = lax.dynamic_slice_in_dim(norm_gain, (1 - c) * width, width, axis=1)
    gain = lax.dynamic_slice_in_dim(norm_gain, c * width, width, axis=1)

    squares = sum(jnp.sum(jnp.square(a.astype(jnp.float32)), axis=(0, 2)) for a in arrays)
    row = jnp.concatenate([squares[None, :], gain_send], axis=1)
    mine, theirs = project(at, ys, zs, row, take(row, dc=1), modality, gain, w, w_other, arrays)
    queries, own_keys = finish(mine, take(theirs, dc=1), qk_gain, cosines, sines)

    moved = {d: take(own_keys, dx=-d, wrap_x=False) for d in (2, 3, 1)}
    got = jnp.stack([own_keys] + [moved[d] for d in (1, 2, 3)])
    sibling = take(got, dc=1)
    never = 1 << 20
    begin = [jnp.where(seq >= d, (seq - d) * row_count, never) for d in range(NX)]
    bases = jnp.stack([b + c * half for b in begin] + [b + (1 - c) * half for b in begin]).astype(jnp.int32)
    heads_out = attention(bases, queries, [got, sibling])

    heads = lax.all_to_all(heads_out, ("y", "zl"), 0, 0)
    own_half = lax.dynamic_slice_in_dim(modality, c * half, half, axis=1)
    partial = out_part(at, own_half, w_cols, w_cols_other, heads)
    spread = lax.all_to_all(partial, ("zh", "zl"), 0, 0, axis_index_groups=GROUPS)
    summed = jnp.sum(spread.astype(jnp.float32), axis=0).astype(jnp.bfloat16).reshape(half, 2, HD)
    keep = lax.dynamic_index_in_dim(summed, c, axis=1, keepdims=False)
    other = take(lax.dynamic_index_in_dim(summed, 1 - c, axis=1, keepdims=False), dc=1)
    return jnp.where(c == 0, jnp.concatenate([keep, other]), jnp.concatenate([other, keep]))


def solution(mesh):
    mesh = Mesh(mesh.devices.reshape(2, NY, NZ // 2, 2, NX), AXES)
    tp = ("y", "zh", "zl")
    placed = (
        P("seq", ("mod", *tp)),
        P("seq"),
        P("mod", None),
        P("mod", None, None, tp),
        P(None, tp),
        P("mod", tp, None),
    )
    return jax.shard_map(shards, mesh=mesh, in_specs=placed, out_specs=P("seq", ("mod", *tp)), check_vma=False)
```

```python
import math

import jax
import jax.numpy as jnp
import numpy as np
from jax import lax
from jax.experimental import pallas as pl
from jax.experimental.pallas import tpu as pltpu
from jax.sharding import Mesh
from jax.sharding import PartitionSpec as P

HD = 128
EPS = 1e-05
MASKED = -1e30
NY = 4
NZ = 8
NX = 4
AXES = ("mod", "y", "zh", "zl", "seq")


def pairs(moves, wrap_x=True):
    out = []
    for c in range(2):
        if moves[c] is None:
            continue
        dc, dy, dz, dx = moves[c]
        for y in range(NY):
            for z in range(NZ):
                for x in range(NX):
                    if not wrap_x and not 0 <= x + dx < NX:
                        continue
                    from_z = z ^ 1 if dz == "pair" else (z + dz) % NZ
                    source = (((c + dc) % 2 * NY + (y + dy) % NY) * NZ + from_z) * NX + (x + dx) % NX
                    out.append((source, ((c * NY + y) * NZ + z) * NX + x))
    return out


def take(x, dc=0, dy=0, dz=0, dx=0, wrap_x=True):
    return lax.ppermute(x, AXES, pairs([(dc, dy, dz, dx)] * 2, wrap_x))


def take_by_core(x, on_y, on_z):
    return lax.ppermute(x, AXES, pairs([m and (0, *m, 0) for m in (on_y, on_z)]))


def gather(rows, beside):
    k1 = take_by_core(rows, (1, 0), (0, 2))
    k2 = take_by_core(rows, (-1, 0), (0, -2))
    k3 = take_by_core(rows, (2, 0), (0, 4))
    k1, k2, k3, beside = lax.optimization_barrier((k1, k2, k3, beside))
    g0 = jnp.stack([rows, k1, k2, k3])
    g1 = take_by_core(g0, (0, 1), (0, -1))
    x2 = take_by_core(g0, (0, -1), (-1, 0))
    x1 = take_by_core(g1, (0, 1), (1, 0))
    x4 = take_by_core(x2, (0, -1), (-1, 0))
    x3 = take_by_core(x1, (0, 1), (1, 0))
    x6 = take_by_core(x4, (0, -1), (-1, 0))
    x5 = take_by_core(x3, (0, 1), (1, 0))
    return [g0, g1, x1, x2, x3, x4, x5, x6], beside


OFFSETS = ((0, 0, 0), (1, 0, 7), (2, 1, 7), (7, 3, 0), (3, 2, 7), (6, 2, 0), (4, 3, 7), (5, 1, 0))


def piece_places(c, y, z):
    turn = np.tile(np.array([0, 1, 3, 2], np.int32), len(OFFSETS))
    dz0, dy1, dz1 = (np.repeat(np.array(o, np.int32), 4) for o in zip(*OFFSETS))
    dy = jnp.where(c == 0, turn, dy1)
    dz = jnp.where(c == 0, dz0, 2 * turn + dz1)
    return (y + dy) & (NY - 1), (z + dz) & (NZ - 1)


def columns(row):
    return jnp.broadcast_to(row, (HD, row.shape[1])).T


def qkv_kernel(at_ref, y_ref, z_ref, row_ref, got_ref, modality_ref, gain_ref, *rest):
    own_ws, other_ws, pieces = rest[:8], rest[8:16], rest[16:24]
    mine_ref, theirs_ref, acc, inv, own = rest[24:]
    step = pl.program_id(0)

    @pl.when(step == 0)
    def _():
        count = inv.shape[0]
        squares = row_ref[:, :count] + got_ref[:, :count]
        inv[...] = columns(lax.rsqrt(squares / (2 * NY * NZ * HD) + EPS))
        own[...] = columns((modality_ref[...] == at_ref[0]).astype(jnp.float32))

    inverse = inv[...]
    own_row = own[...] > 0
    normed, right = [], []
    for k, piece in enumerate(pieces):
        yi, zi = y_ref[4 * k + step], z_ref[4 * k + step]
        at_own = pl.ds(pl.multiple_of((yi * NZ + zi) * HD, HD), HD)
        at_got = pl.ds(pl.multiple_of(inv.shape[0] + (yi * NZ + zi) * HD, HD), HD)
        gain = jnp.where(own_row, gain_ref[:, at_own], got_ref[:, at_got])
        normed.append((piece[0].astype(jnp.float32) * inverse * gain).astype(jnp.bfloat16))
        right.append(jnp.concatenate([w[p, 0, 0, 0] for w in (own_ws[k], other_ws[k]) for p in range(3)], axis=1))
    part = jnp.dot(
        jnp.concatenate(normed, axis=1), jnp.concatenate(right, axis=0), preferred_element_type=jnp.float32
    )

    @pl.when(step == 0)
    def _():
        acc[...] = part

    @pl.when(step > 0)
    def _():
        acc[...] += part

    @pl.when(step == pl.num_programs(0) - 1)
    def _():
        half = acc.shape[0] // 2
        for ref, first in ((mine_ref, at_ref[0] * half), (theirs_ref, (1 - at_ref[0]) * half)):
            rows = pl.ds(pl.multiple_of(first, half), half)
            own_here = own[rows, :] > 0
            for p in range(3):
                low, high = acc[rows, p * HD : (p + 1) * HD], acc[rows, (3 + p) * HD : (4 + p) * HD]
                ref[:, p * HD : (p + 1) * HD] = jnp.where(own_here, low, high)


def project(at, ys, zs, row, got, modality, gain, w, w_other, arrays):
    rows = arrays[0].shape[1]
    block = (3, 1, 1, 1, HD, HD)
    whole = lambda shape: pl.BlockSpec(shape, lambda g, *_: (0,) * len(shape))
    piece = pl.BlockSpec((1, rows, HD), lambda g, *_: (g, 0, 0))
    weights = lambda k, other: pl.BlockSpec(
        block, lambda g, at, ys, zs: (0, 0 if other else at[0], ys[4 * k + g], zs[4 * k + g], 0, 0)
    )
    return pl.pallas_call(
        qkv_kernel,
        grid_spec=pltpu.PrefetchScalarGridSpec(
            num_scalar_prefetch=3,
            grid=(4,),
            in_specs=[whole(row.shape), whole(got.shape), whole((1, rows)), whole(gain.shape)]
            + [weights(k, False) for k in range(8)]
            + [weights(k, True) for k in range(8)]
            + [piece] * 8,
            out_specs=[whole((rows // 2, 3 * HD))] * 2,
            scratch_shapes=[pltpu.VMEM((rows, w), jnp.float32) for w in (6 * HD, HD, HD)],
        ),
        out_shape=[jax.ShapeDtypeStruct((rows // 2, 3 * HD), jnp.float32)] * 2,
        compiler_params=pltpu.CompilerParams(vmem_limit_bytes=61 * 2**20),
        cost_estimate=pl.CostEstimate(
            flops=2 * rows * 4096 * 6 * HD, bytes_accessed=11 * 2**20, transcendentals=0
        ),
    )(at, ys, zs, row, got, modality, gain, *[w] * 8, *[w_other] * 8, *arrays)


def finish_kernel(mine_ref, got_ref, gain_ref, cos_ref, sin_ref, q_ref, kv_ref):
    projected = mine_ref[...] + got_ref[...]
    half = HD // 2
    turned = []
    for p in range(2):
        x = projected[:, p * HD : (p + 1) * HD]
        centred = x - jnp.mean(x, axis=1, keepdims=True)
        variance = jnp.mean(centred * centred, axis=1, keepdims=True)
        x = centred * lax.rsqrt(variance + EPS) * gain_ref[p : p + 1, :]
        swapped = jnp.concatenate([x[:, half:], x[:, :half]], axis=1)
        turned.append((x * cos_ref[...] + swapped * sin_ref[...]).astype(jnp.bfloat16))
    q_ref[...] = turned[0]
    kv_ref[0] = turned[1]
    kv_ref[1] = projected[:, 2 * HD :].astype(jnp.bfloat16)


def finish(mine, got, qk_gain, cosines, sines):
    rows = mine.shape[0]
    vmem = pl.BlockSpec(memory_space=pltpu.VMEM)
    return pl.pallas_call(
        finish_kernel,
        in_specs=[vmem] * 5,
        out_specs=[vmem] * 2,
        out_shape=[
            jax.ShapeDtypeStruct((rows, HD), jnp.bfloat16),
            jax.ShapeDtypeStruct((2, rows, HD), jnp.bfloat16),
        ],
    )(mine, got, qk_gain, cosines, sines)


def attention_kernel(base_ref, q_ref, *rest):
    key_refs, out_ref = rest[:-1], rest[-1]
    rows = q_ref.shape[0]
    queries = q_ref[...]
    scale = 1.0 / math.sqrt(HD)
    row = base_ref[0] + lax.broadcasted_iota(jnp.int32, (rows, rows), 0)
    column = lax.broadcasted_iota(jnp.int32, (rows, rows), 1)
    blocks = [(ref, i) for ref in key_refs for i in range(ref.shape[0])]
    scores, seen = [], []
    for n, (ref, i) in enumerate(blocks):
        s = lax.dot_general(queries, ref[i, 0], (((1,), (1,)), ((), ())), preferred_element_type=jnp.float32)
        allowed = column + base_ref[n] <= row
        seen.append(allowed)
        scores.append(jnp.where(allowed, s * scale, MASKED))
    best = scores[0].max(axis=1, keepdims=True)
    for s in scores[1:]:
        best = jnp.maximum(best, s.max(axis=1, keepdims=True))
    total = jnp.zeros((rows, 1), jnp.float32)
    out = jnp.zeros((rows, HD), jnp.float32)
    for n, (ref, i) in enumerate(blocks):
        weights = jnp.where(seen[n], jnp.exp(scores[n] - best), 0.0)
        total += weights.sum(axis=1, keepdims=True)
        out += jnp.dot(weights.astype(jnp.bfloat16), ref[i, 1], preferred_element_type=jnp.float32)
    result = (out / total).astype(jnp.bfloat16)
    for i in range(out_ref.shape[0]):
        out_ref[i] = result


def attention(bases, queries, keys):
    vmem = pl.BlockSpec(memory_space=pltpu.VMEM)
    return pl.pallas_call(
        attention_kernel,
        in_specs=[pl.BlockSpec(memory_space=pltpu.SMEM)] + [vmem] * (1 + len(keys)),
        out_specs=vmem,
        out_shape=jax.ShapeDtypeStruct((2 * NY, *queries.shape), jnp.bfloat16),
        compiler_params=pltpu.CompilerParams(vmem_limit_bytes=24 * 2**20),
        cost_estimate=pl.CostEstimate(flops=2**28, bytes_accessed=2**20, transcendentals=2**19),
    )(bases, queries, *keys)


def out_kernel(at_ref, modality_ref, w_ref, other_ref, heads_ref, out_ref):
    heads = jnp.concatenate([heads_ref[i] for i in range(2 * NY)], axis=1)
    own_row = columns((modality_ref[...] == at_ref[0]).astype(jnp.float32)) > 0
    n = out_ref.shape[0]
    parts = []
    for ref in (w_ref, other_ref):
        for j in range(n):
            parts.append(jnp.concatenate([ref[x, i, j] for i in range(2 * NY) for x in range(NX)], axis=0))
    sums = jnp.dot(heads, jnp.concatenate(parts, axis=1), preferred_element_type=jnp.float32)
    for j in range(n):
        for i in range(2):
            own, other = ((2 * (n * m + j) + i) * HD for m in range(2))
            chosen = jnp.where(own_row, sums[:, own : own + HD], sums[:, other : other + HD])
            out_ref[j, :, i * HD : (i + 1) * HD] = chosen.astype(jnp.bfloat16)


def out_part(at, modality, w, w_other, heads):
    rows = heads.shape[1]
    steps = 2
    each = NZ // 2 // steps
    whole = lambda shape: pl.BlockSpec(shape, lambda g, at: (0,) * len(shape))
    weights = pl.BlockSpec((NX, 2 * NY, each, HD // NX, 2 * HD), lambda g, at: (0, 0, g, 0, 0))
    return pl.pallas_call(
        out_kernel,
        grid_spec=pltpu.PrefetchScalarGridSpec(
            num_scalar_prefetch=1,
            grid=(steps,),
            in_specs=[whole((1, rows)), weights, weights, whole(heads.shape)],
            out_specs=pl.BlockSpec((each, rows, 2 * HD), lambda g, at: (g, 0, 0)),
        ),
        out_shape=jax.ShapeDtypeStruct((NZ // 2, rows, 2 * HD), jnp.bfloat16),
        compiler_params=pltpu.CompilerParams(vmem_limit_bytes=20 * 2**20),
        cost_estimate=pl.CostEstimate(
            flops=8 * rows * NY * HD * NZ * HD, bytes_accessed=5 * 2**20, transcendentals=0
        ),
    )(at, modality, w, w_other, heads)


GROUPS = [[2 * p + (which ^ (p >> 1)) for p in range(NZ // 2)] for which in range(2)]


def cut_kernel(at_ref, w_ref, out_ref):
    upper = (at_ref[2] >> 2) & 1
    for y in range(NY):
        for odd in range(2):
            for p in range(NZ // 2):
                for c in range(2):
                    first = (c * NY + y) * NZ + 2 * p + ((odd ^ (p >> 1)) ^ upper)
                    piece = w_ref[:, pl.ds(pl.multiple_of(first * HD, HD), HD)]
                    out_ref[2 * y + odd, p, :, c * HD : (c + 1) * HD] = piece


def cut_w_out(at, w_out):
    rows = HD // NX
    shape = (2 * NY, NZ // 2, rows, 2 * HD)
    return pl.pallas_call(
        cut_kernel,
        grid_spec=pltpu.PrefetchScalarGridSpec(
            num_scalar_prefetch=1,
            grid=(1,),
            in_specs=[pl.BlockSpec((rows, w_out.shape[1]), lambda g, at: (at[3], 0))],
            out_specs=pl.BlockSpec(shape, lambda g, at: (0,) * 4),
        ),
        out_shape=jax.ShapeDtypeStruct(shape, jnp.bfloat16),
        cost_estimate=pl.CostEstimate(flops=0, bytes_accessed=2**20, transcendentals=0),
    )(at, w_out)


def spread_w_out(pieces, *ahead):
    lines = lax.all_to_all(pieces, ("y", "zl"), 0, 0)
    lines, *_ = lax.optimization_barrier((lines, *ahead))
    return lax.all_gather(lines, "seq", axis=0)


def shards(tokens, modality, norm_gain, w_qkv, qk_gain, w_out):
    row_count = tokens.shape[0]
    half = row_count // 2
    c, y, zh, zl, seq = (lax.axis_index(a) for a in AXES)
    z = 2 * zh + zl
    at = jnp.stack([c, y, z, seq]).astype(jnp.int32)
    modality = modality[None, :]
    ys, zs = piece_places(c.astype(jnp.int32), y.astype(jnp.int32), z.astype(jnp.int32))

    w = w_qkv[0].transpose(1, 0, 2).reshape(3, 2, NY, NZ, HD, HD)
    w_send = lax.dynamic_slice_in_dim(w, 1 - c, 1, axis=1)
    arrays, (pieces, w_send) = gather(tokens, (cut_w_out(at, w_out[0]), w_send))
    w_cols = spread_w_out(pieces, arrays[2], arrays[3])
    w_cols_other = take(w_cols, dc=1)

    first = seq * row_count + c * half
    places = first + jnp.arange(half, dtype=jnp.int32)
    rates = 1.0 / 10000.0 ** (jnp.arange(HD // 2, dtype=jnp.float32) * (2.0 / HD))
    angles = places.astype(jnp.float32)[:, None] * rates[None, :]
    cosines, sines = jnp.cos(angles), jnp.sin(angles)
    cosines, sines = jnp.concatenate([cosines, cosines], axis=1), jnp.concatenate([-sines, sines], axis=1)

    w_other = take(w_send, dc=1)
    width = NY * NZ * HD
    gain_send = lax.dynamic_slice_in_dim(norm_gain, (1 - c) * width, width, axis=1)
    gain = lax.dynamic_slice_in_dim(norm_gain, c * width, width, axis=1)

    squares = sum(jnp.sum(jnp.square(a.astype(jnp.float32)), axis=(0, 2)) for a in arrays)
    row = jnp.concatenate([squares[None, :], gain_send], axis=1)
    mine, theirs = project(at, ys, zs, row, take(row, dc=1), modality, gain, w, w_other, arrays)
    queries, own_keys = finish(mine, take(theirs, dc=1), qk_gain, cosines, sines)

    moved = {d: take(own_keys, dx=-d, wrap_x=False) for d in (2, 3, 1)}
    got = jnp.stack([own_keys] + [moved[d] for d in (1, 2, 3)])
    sibling = take(got, dc=1)
    never = 1 << 20
    begin = [jnp.where(seq >= d, (seq - d) * row_count, never) for d in range(NX)]
    bases = jnp.stack([b + c * half for b in begin] + [b + (1 - c) * half for b in begin]).astype(jnp.int32)
    heads_out = attention(bases, queries, [got, sibling])

    heads = lax.all_to_all(heads_out, ("y", "zl"), 0, 0)
    own_half = lax.dynamic_slice_in_dim(modality, c * half, half, axis=1)
    partial = out_part(at, own_half, w_cols, w_cols_other, heads)
    spread = lax.all_to_all(partial, ("zh", "zl"), 0, 0, axis_index_groups=GROUPS)
    summed = jnp.sum(spread.astype(jnp.float32), axis=0).astype(jnp.bfloat16).reshape(half, 2, HD)
    keep = lax.dynamic_index_in_dim(summed, c, axis=1, keepdims=False)
    other = take(lax.dynamic_index_in_dim(summed, 1 - c, axis=1, keepdims=False), dc=1)
    return jnp.where(c == 0, jnp.concatenate([keep, other]), jnp.concatenate([other, keep]))


def solution(mesh):
    mesh = Mesh(mesh.devices.reshape(2, NY, NZ // 2, 2, NX), AXES)
    tp = ("y", "zh", "zl")
    placed = (
        P("seq", ("mod", *tp)),
        P("seq"),
        P("mod", None),
        P("mod", None, None, tp),
        P(None, tp),
        P("mod", tp, None),
    )
    return jax.shard_map(shards, mesh=mesh, in_specs=placed, out_specs=P("seq", ("mod", *tp)), check_vma=False)
```

```python
import math

import jax
import jax.numpy as jnp
import numpy as np
from jax import lax
from jax.experimental import pallas as pl
from jax.experimental.pallas import tpu as pltpu
from jax.sharding import Mesh
from jax.sharding import PartitionSpec as P

HD = 128
EPS = 1e-05
MASKED = -1e30
NY = 4
NZ = 8
NX = 4
AXES = ("mod", "y", "zh", "zl", "seq")


def pairs(moves, wrap_x=True):
    out = []
    for c in range(2):
        if moves[c] is None:
            continue
        dc, dy, dz, dx = moves[c]
        for y in range(NY):
            for z in range(NZ):
                for x in range(NX):
                    if not wrap_x and not 0 <= x + dx < NX:
                        continue
                    from_z = z ^ 1 if dz == "pair" else (z + dz) % NZ
                    source = (((c + dc) % 2 * NY + (y + dy) % NY) * NZ + from_z) * NX + (x + dx) % NX
                    out.append((source, ((c * NY + y) * NZ + z) * NX + x))
    return out


def take(x, dc=0, dy=0, dz=0, dx=0, wrap_x=True):
    return lax.ppermute(x, AXES, pairs([(dc, dy, dz, dx)] * 2, wrap_x))


def take_by_core(x, on_y, on_z):
    return lax.ppermute(x, AXES, pairs([m and (0, *m, 0) for m in (on_y, on_z)]))


def gather(rows, beside):
    k1 = take_by_core(rows, (1, 0), (0, 2))
    k2 = take_by_core(rows, (-1, 0), (0, -2))
    k3 = take_by_core(rows, (2, 0), (0, 4))
    k1, k2, k3, beside = lax.optimization_barrier((k1, k2, k3, beside))
    g0 = jnp.stack([rows, k1, k2, k3])
    g1 = take_by_core(g0, (0, 1), (0, -1))
    x2 = take_by_core(g0, (0, -1), (-1, 0))
    x1 = take_by_core(g1, (0, 1), (1, 0))
    x4 = take_by_core(x2, (0, -1), (-1, 0))
    x3 = take_by_core(x1, (0, 1), (1, 0))
    x6 = take_by_core(x4, (0, -1), (-1, 0))
    x5 = take_by_core(x3, (0, 1), (1, 0))
    return [g0, g1, x1, x2, x3, x4, x5, x6], beside


OFFSETS = ((0, 0, 0), (1, 0, 7), (2, 1, 7), (7, 3, 0), (3, 2, 7), (6, 2, 0), (4, 3, 7), (5, 1, 0))


def piece_places(c, y, z):
    turn = np.tile(np.array([0, 1, 3, 2], np.int32), len(OFFSETS))
    dz0, dy1, dz1 = (np.repeat(np.array(o, np.int32), 4) for o in zip(*OFFSETS))
    dy = jnp.where(c == 0, turn, dy1)
    dz = jnp.where(c == 0, dz0, 2 * turn + dz1)
    return (y + dy) & (NY - 1), (z + dz) & (NZ - 1)


def columns(row):
    return jnp.broadcast_to(row, (HD, row.shape[1])).T


def qkv_kernel(at_ref, y_ref, z_ref, row_ref, got_ref, modality_ref, gain_ref, *rest):
    own_ws, other_ws, pieces = rest[:8], rest[8:16], rest[16:24]
    mine_ref, theirs_ref, acc, inv, own = rest[24:]
    step = pl.program_id(0)

    @pl.when(step == 0)
    def _():
        count = inv.shape[0]
        squares = row_ref[:, :count] + got_ref[:, :count]
        inv[...] = columns(lax.rsqrt(squares / (2 * NY * NZ * HD) + EPS))
        own[...] = columns((modality_ref[...] == at_ref[0]).astype(jnp.float32))

    inverse = inv[...]
    own_row = own[...] > 0
    normed, right = [], []
    for k, piece in enumerate(pieces):
        yi, zi = y_ref[4 * k + step], z_ref[4 * k + step]
        at_own = pl.ds(pl.multiple_of((yi * NZ + zi) * HD, HD), HD)
        at_got = pl.ds(pl.multiple_of(inv.shape[0] + (yi * NZ + zi) * HD, HD), HD)
        gain = jnp.where(own_row, gain_ref[:, at_own], got_ref[:, at_got])
        normed.append((piece[0].astype(jnp.float32) * inverse * gain).astype(jnp.bfloat16))
        right.append(jnp.concatenate([w[p, 0, 0, 0] for w in (own_ws[k], other_ws[k]) for p in range(3)], axis=1))
    part = jnp.dot(
        jnp.concatenate(normed, axis=1), jnp.concatenate(right, axis=0), preferred_element_type=jnp.float32
    )

    @pl.when(step == 0)
    def _():
        acc[...] = part

    @pl.when(step > 0)
    def _():
        acc[...] += part

    @pl.when(step == pl.num_programs(0) - 1)
    def _():
        half = acc.shape[0] // 2
        for ref, first in ((mine_ref, at_ref[0] * half), (theirs_ref, (1 - at_ref[0]) * half)):
            rows = pl.ds(pl.multiple_of(first, half), half)
            own_here = own[rows, :] > 0
            for p in range(3):
                low, high = acc[rows, p * HD : (p + 1) * HD], acc[rows, (3 + p) * HD : (4 + p) * HD]
                ref[:, p * HD : (p + 1) * HD] = jnp.where(own_here, low, high)


def project(at, ys, zs, row, got, modality, gain, w, w_other, arrays):
    rows = arrays[0].shape[1]
    block = (3, 1, 1, 1, HD, HD)
    whole = lambda shape: pl.BlockSpec(shape, lambda g, *_: (0,) * len(shape))
    piece = pl.BlockSpec((1, rows, HD), lambda g, *_: (g, 0, 0))
    weights = lambda k, other: pl.BlockSpec(
        block, lambda g, at, ys, zs: (0, 0 if other else at[0], ys[4 * k + g], zs[4 * k + g], 0, 0)
    )
    return pl.pallas_call(
        qkv_kernel,
        grid_spec=pltpu.PrefetchScalarGridSpec(
            num_scalar_prefetch=3,
            grid=(4,),
            in_specs=[whole(row.shape), whole(got.shape), whole((1, rows)), whole(gain.shape)]
            + [weights(k, False) for k in range(8)]
            + [weights(k, True) for k in range(8)]
            + [piece] * 8,
            out_specs=[whole((rows // 2, 3 * HD))] * 2,
            scratch_shapes=[pltpu.VMEM((rows, w), jnp.float32) for w in (6 * HD, HD, HD)],
        ),
        out_shape=[jax.ShapeDtypeStruct((rows // 2, 3 * HD), jnp.float32)] * 2,
        compiler_params=pltpu.CompilerParams(vmem_limit_bytes=52 * 2**20),
        cost_estimate=pl.CostEstimate(
            flops=2 * rows * 4096 * 6 * HD, bytes_accessed=11 * 2**20, transcendentals=0
        ),
    )(at, ys, zs, row, got, modality, gain, *[w] * 8, *[w_other] * 8, *arrays)


def finish_kernel(mine_ref, got_ref, gain_ref, cos_ref, sin_ref, q_ref, kv_ref):
    projected = mine_ref[...] + got_ref[...]
    half = HD // 2
    turned = []
    for p in range(2):
        x = projected[:, p * HD : (p + 1) * HD]
        centred = x - jnp.mean(x, axis=1, keepdims=True)
        variance = jnp.mean(centred * centred, axis=1, keepdims=True)
        x = centred * lax.rsqrt(variance + EPS) * gain_ref[p : p + 1, :]
        swapped = jnp.concatenate([x[:, half:], x[:, :half]], axis=1)
        turned.append((x * cos_ref[...] + swapped * sin_ref[...]).astype(jnp.bfloat16))
    q_ref[...] = turned[0]
    kv_ref[0] = turned[1]
    kv_ref[1] = projected[:, 2 * HD :].astype(jnp.bfloat16)


def finish(mine, got, qk_gain, cosines, sines):
    rows = mine.shape[0]
    vmem = pl.BlockSpec(memory_space=pltpu.VMEM)
    return pl.pallas_call(
        finish_kernel,
        in_specs=[vmem] * 5,
        out_specs=[vmem] * 2,
        out_shape=[
            jax.ShapeDtypeStruct((rows, HD), jnp.bfloat16),
            jax.ShapeDtypeStruct((2, rows, HD), jnp.bfloat16),
        ],
    )(mine, got, qk_gain, cosines, sines)


def attention_kernel(base_ref, q_ref, *rest):
    key_refs, out_ref = rest[:-1], rest[-1]
    rows = q_ref.shape[0]
    queries = q_ref[...]
    scale = 1.0 / math.sqrt(HD)
    row = base_ref[0] + lax.broadcasted_iota(jnp.int32, (rows, rows), 0)
    column = lax.broadcasted_iota(jnp.int32, (rows, rows), 1)
    blocks = [(ref, i) for ref in key_refs for i in range(ref.shape[0])]
    scores, seen = [], []
    for n, (ref, i) in enumerate(blocks):
        s = lax.dot_general(queries, ref[i, 0], (((1,), (1,)), ((), ())), preferred_element_type=jnp.float32)
        allowed = column + base_ref[n] <= row
        seen.append(allowed)
        scores.append(jnp.where(allowed, s * scale, MASKED))
    best = scores[0].max(axis=1, keepdims=True)
    for s in scores[1:]:
        best = jnp.maximum(best, s.max(axis=1, keepdims=True))
    total = jnp.zeros((rows, 1), jnp.float32)
    out = jnp.zeros((rows, HD), jnp.float32)
    for n, (ref, i) in enumerate(blocks):
        weights = jnp.where(seen[n], jnp.exp(scores[n] - best), 0.0)
        total += weights.sum(axis=1, keepdims=True)
        out += jnp.dot(weights.astype(jnp.bfloat16), ref[i, 1], preferred_element_type=jnp.float32)
    result = (out / total).astype(jnp.bfloat16)
    for i in range(out_ref.shape[0]):
        out_ref[i] = result


def attention(bases, queries, keys):
    vmem = pl.BlockSpec(memory_space=pltpu.VMEM)
    return pl.pallas_call(
        attention_kernel,
        in_specs=[pl.BlockSpec(memory_space=pltpu.SMEM)] + [vmem] * (1 + len(keys)),
        out_specs=vmem,
        out_shape=jax.ShapeDtypeStruct((2 * NY, *queries.shape), jnp.bfloat16),
        compiler_params=pltpu.CompilerParams(vmem_limit_bytes=24 * 2**20),
        cost_estimate=pl.CostEstimate(flops=2**28, bytes_accessed=2**20, transcendentals=2**19),
    )(bases, queries, *keys)


def out_kernel(at_ref, modality_ref, w_ref, other_ref, heads_ref, out_ref):
    heads = jnp.concatenate([heads_ref[i] for i in range(2 * NY)], axis=1)
    own_row = columns((modality_ref[...] == at_ref[0]).astype(jnp.float32)) > 0
    n = out_ref.shape[0]
    parts = []
    for ref in (w_ref, other_ref):
        for j in range(n):
            parts.append(jnp.concatenate([ref[x, i, j] for i in range(2 * NY) for x in range(NX)], axis=0))
    sums = jnp.dot(heads, jnp.concatenate(parts, axis=1), preferred_element_type=jnp.float32)
    for j in range(n):
        for i in range(2):
            own, other = ((2 * (n * m + j) + i) * HD for m in range(2))
            chosen = jnp.where(own_row, sums[:, own : own + HD], sums[:, other : other + HD])
            out_ref[j, :, i * HD : (i + 1) * HD] = chosen.astype(jnp.bfloat16)


def out_part(at, modality, w, w_other, heads):
    rows = heads.shape[1]
    steps = 2
    each = NZ // 2 // steps
    whole = lambda shape: pl.BlockSpec(shape, lambda g, at: (0,) * len(shape))
    weights = pl.BlockSpec((NX, 2 * NY, each, HD // NX, 2 * HD), lambda g, at: (0, 0, g, 0, 0))
    return pl.pallas_call(
        out_kernel,
        grid_spec=pltpu.PrefetchScalarGridSpec(
            num_scalar_prefetch=1,
            grid=(steps,),
            in_specs=[whole((1, rows)), weights, weights, whole(heads.shape)],
            out_specs=pl.BlockSpec((each, rows, 2 * HD), lambda g, at: (g, 0, 0)),
        ),
        out_shape=jax.ShapeDtypeStruct((NZ // 2, rows, 2 * HD), jnp.bfloat16),
        compiler_params=pltpu.CompilerParams(vmem_limit_bytes=20 * 2**20),
        cost_estimate=pl.CostEstimate(
            flops=8 * rows * NY * HD * NZ * HD, bytes_accessed=5 * 2**20, transcendentals=0
        ),
    )(at, modality, w, w_other, heads)


GROUPS = [[2 * p + (which ^ (p >> 1)) for p in range(NZ // 2)] for which in range(2)]


def cut_kernel(at_ref, w_ref, out_ref):
    upper = (at_ref[2] >> 2) & 1
    for y in range(NY):
        for odd in range(2):
            for p in range(NZ // 2):
                for c in range(2):
                    first = (c * NY + y) * NZ + 2 * p + ((odd ^ (p >> 1)) ^ upper)
                    piece = w_ref[:, pl.ds(pl.multiple_of(first * HD, HD), HD)]
                    out_ref[2 * y + odd, p, :, c * HD : (c + 1) * HD] = piece


def cut_w_out(at, w_out):
    rows = HD // NX
    shape = (2 * NY, NZ // 2, rows, 2 * HD)
    return pl.pallas_call(
        cut_kernel,
        grid_spec=pltpu.PrefetchScalarGridSpec(
            num_scalar_prefetch=1,
            grid=(1,),
            in_specs=[pl.BlockSpec((rows, w_out.shape[1]), lambda g, at: (at[3], 0))],
            out_specs=pl.BlockSpec(shape, lambda g, at: (0,) * 4),
        ),
        out_shape=jax.ShapeDtypeStruct(shape, jnp.bfloat16),
        cost_estimate=pl.CostEstimate(flops=0, bytes_accessed=2**20, transcendentals=0),
    )(at, w_out)


def spread_w_out(pieces, *ahead):
    lines = lax.all_to_all(pieces, ("y", "zl"), 0, 0)
    lines, *_ = lax.optimization_barrier((lines, *ahead))
    return lax.all_gather(lines, "seq", axis=0)


def shards(tokens, modality, norm_gain, w_qkv, qk_gain, w_out):
    row_count = tokens.shape[0]
    half = row_count // 2
    c, y, zh, zl, seq = (lax.axis_index(a) for a in AXES)
    z = 2 * zh + zl
    at = jnp.stack([c, y, z, seq]).astype(jnp.int32)
    modality = modality[None, :]
    ys, zs = piece_places(c.astype(jnp.int32), y.astype(jnp.int32), z.astype(jnp.int32))

    w = w_qkv[0].transpose(1, 0, 2).reshape(3, 2, NY, NZ, HD, HD)
    w_send = lax.dynamic_slice_in_dim(w, 1 - c, 1, axis=1)
    arrays, (pieces, w_send) = gather(tokens, (cut_w_out(at, w_out[0]), w_send))
    w_cols = spread_w_out(pieces, arrays[2], arrays[3])
    w_cols_other = take(w_cols, dc=1)

    first = seq * row_count + c * half
    places = first + jnp.arange(half, dtype=jnp.int32)
    rates = 1.0 / 10000.0 ** (jnp.arange(HD // 2, dtype=jnp.float32) * (2.0 / HD))
    angles = places.astype(jnp.float32)[:, None] * rates[None, :]
    cosines, sines = jnp.cos(angles), jnp.sin(angles)
    cosines, sines = jnp.concatenate([cosines, cosines], axis=1), jnp.concatenate([-sines, sines], axis=1)

    w_other = take(w_send, dc=1)
    width = NY * NZ * HD
    gain_send = lax.dynamic_slice_in_dim(norm_gain, (1 - c) * width, width, axis=1)
    gain = lax.dynamic_slice_in_dim(norm_gain, c * width, width, axis=1)

    squares = sum(jnp.sum(jnp.square(a.astype(jnp.float32)), axis=(0, 2)) for a in arrays)
    row = jnp.concatenate([squares[None, :], gain_send], axis=1)
    mine, theirs = project(at, ys, zs, row, take(row, dc=1), modality, gain, w, w_other, arrays)
    queries, own_keys = finish(mine, take(theirs, dc=1), qk_gain, cosines, sines)

    moved = {d: take(own_keys, dx=-d, wrap_x=False) for d in (2, 3, 1)}
    got = jnp.stack([own_keys] + [moved[d] for d in (1, 2, 3)])
    sibling = take(got, dc=1)
    never = 1 << 20
    begin = [jnp.where(seq >= d, (seq - d) * row_count, never) for d in range(NX)]
    bases = jnp.stack([b + c * half for b in begin] + [b + (1 - c) * half for b in begin]).astype(jnp.int32)
    heads_out = attention(bases, queries, [got, sibling])

    heads = lax.all_to_all(heads_out, ("y", "zl"), 0, 0)
    own_half = lax.dynamic_slice_in_dim(modality, c * half, half, axis=1)
    partial = out_part(at, own_half, w_cols, w_cols_other, heads)
    spread = lax.all_to_all(partial, ("zh", "zl"), 0, 0, axis_index_groups=GROUPS)
    summed = jnp.sum(spread.astype(jnp.float32), axis=0).astype(jnp.bfloat16).reshape(half, 2, HD)
    keep = lax.dynamic_index_in_dim(summed, c, axis=1, keepdims=False)
    other = take(lax.dynamic_index_in_dim(summed, 1 - c, axis=1, keepdims=False), dc=1)
    return jnp.where(c == 0, jnp.concatenate([keep, other]), jnp.concatenate([other, keep]))


def solution(mesh):
    mesh = Mesh(mesh.devices.reshape(2, NY, NZ // 2, 2, NX), AXES)
    tp = ("y", "zh", "zl")
    placed = (
        P("seq", ("mod", *tp)),
        P("seq"),
        P("mod", None),
        P("mod", None, None, tp),
        P(None, tp),
        P("mod", tp, None),
    )
    return jax.shard_map(shards, mesh=mesh, in_specs=placed, out_specs=P("seq", ("mod", *tp)), check_vma=False)
```
